32 devices in a mesh: row: 8 (over y, x, core), rep: 4 (over z).
Axes of the slice: x: 2, y: 2, z: 4, core: 2. Of those that a mesh axis runs over, the one named last changes fastest.
Arguments:
- node_feats: bfloat16 [8192, 1024], P('row'), may hold values from -6 to 6
- block_cols: int32 [64, 4], P('row'), may hold values from -1 to 63, as said below
- block_vals: bfloat16 [64, 4, 128, 128], P('row'), may hold values from -0.26367188 to 0.26367188
- w_in: bfloat16 [1024, 4096], P(None, 'rep'), may hold values from -0.1875 to 0.1875
- w_out: bfloat16 [1024, 4096], P(None, 'rep'), may hold values from -0.09375 to 0.09375
- cotangent: bfloat16 [8192, 1024], P('row', 'rep'), may hold values from -6 to 6
Outputs:
- updated: bfloat16 [8192, 1024], P('row', 'rep')
- grad_nodes: bfloat16 [8192, 1024], P('row', 'rep')
The draws below stay inside these ranges and needn't reach their ends.
Inputs may be any that keep to these rules, and one draw needn't show every extreme that they name: `block_cols`: slot 0 of block-row b holds b itself. Every other present block-column lies within 16 block-rows of its block-row; absent slots hold -1, and the number of present blocks differs from block-row to block-row. A pair of block-row and block-column may repeat.
All inputs are finite; a program needn't handle non-finite values.
Results may differ from the reference program's by a relative error of at most 0.013.
Values may be sent and summed in bfloat16 or wider, within the bound.
A program may use at most 128 MiB of HBM per device.

```python
import jax
import jax.numpy as jnp
from jax import lax

D = 1024
HID = 4096
SLOTS = 4
ROWS_DEV = 1024
NODES = 8192
BLOCK_ROWS = 64
N_REP = 4


def draw_block_cols(key, part):
    reach = 2 * (ROWS_DEV // 128)
    grid_shape = (BLOCK_ROWS, SLOTS)
    block_rows = jnp.arange(BLOCK_ROWS, dtype=jnp.int32)[:, None]
    slot_ids = jnp.arange(SLOTS, dtype=jnp.int32)[None, :]
    key_mag = jax.random.fold_in(key, 11)
    key_sign = jax.random.fold_in(key, 12)
    key_live = jax.random.fold_in(key, 13)
    magnitude = jax.random.randint(key_mag, grid_shape, 1, reach + 1)
    signs = jax.random.randint(key_sign, grid_shape, 0, 2) * 2 - 1
    alive = jax.random.randint(key_live, grid_shape, 0, 10) < 7
    target = block_rows + magnitude * signs
    usable = alive & (target >= 0) & (target < BLOCK_ROWS)
    chosen = jnp.where(usable, target, -1)
    chosen = jnp.where(slot_ids == 0, block_rows, chosen)
    chosen = jnp.where((block_rows == 0) & (slot_ids == SLOTS - 1), -1, chosen)
    return chosen.astype(jnp.int32)


def block_scale(stream_key, shape, cuts, low, top_value):
    factor_of = 1.0
    for axis_at, blocks in cuts:
        steps = jax.random.uniform(jax.random.fold_in(jax.random.fold_in(stream_key, 6), axis_at), (blocks,), jnp.float32, low / len(cuts), top_value / len(cuts))
        factor_of = factor_of * jnp.repeat(jnp.exp(steps), shape[axis_at] // blocks).reshape((-1,) + (1,) * (len(shape) - 1 - axis_at))
    return factor_of


def scatter_about(stream_key, dims, spread, limit, split=(), held_as=jnp.bfloat16):
    drawn = spread * jax.random.normal(stream_key, dims, jnp.float32)
    if split:
        drawn = drawn * block_scale(stream_key, dims, split, -0.22, 0.18)
    return jnp.clip(drawn, -limit, limit).astype(held_as)


def setup_inputs(seed: int = 0) -> dict:
    key_of = jax.random.split(jax.random.key(seed), 7)
    node_feats = scatter_about(key_of[0], (NODES, D), 1.0, 6.0, ((0, 8),))
    block_cols = draw_block_cols(jax.random.fold_in(key_of[6], 71), 0)
    block_vals = scatter_about(key_of[2], (BLOCK_ROWS, SLOTS, 128, 128), ((SLOTS * 128) ** -0.5), 0.26367188, ((0, 8),))
    w_in = scatter_about(key_of[3], (D, HID), D ** -0.5, 0.1875, ((1, 4),))
    w_out = scatter_about(key_of[4], (D, HID), HID ** -0.5, 0.09375, ((1, 4),))
    cotangent = scatter_about(key_of[5], (NODES, D), 1.0, 6.0, ((0, 8), (1, 4)))
    return dict(node_feats=node_feats, block_cols=block_cols, block_vals=block_vals, w_in=w_in, w_out=w_out, cotangent=cotangent)


def gelu_value(values):
    cubic_arg = 0.7978845608 * (values + 0.044715 * values * values * values)
    return 0.5 * values * (1.0 + jnp.tanh(cubic_arg))


def gelu_slope(values):
    cubic_arg = 0.7978845608 * (values + 0.044715 * values * values * values)
    tangent = jnp.tanh(cubic_arg)
    return 0.5 * (1.0 + tangent) + 0.5 * values * (1.0 - tangent * tangent) * 0.7978845608 * (1.0 + 3.0 * 0.044715 * values * values)


def grouped_product(left, weight, groups):
    width = left.shape[1] // groups
    total = jnp.zeros((left.shape[0], weight.shape[0]), jnp.float32)
    for group in range(groups):
        part = jnp.dot(left[:, group * width:(group + 1) * width], weight[:, group * width:(group + 1) * width].T, preferred_element_type=jnp.float32)
        rounded = lax.optimization_barrier(part.astype(jnp.bfloat16))
        total = total + rounded.astype(jnp.float32)
    return total


def reference(node_feats, block_cols, block_vals, w_in, w_out, cotangent):
    block_count = block_cols.shape[0]
    feat_width = node_feats.shape[1]
    present = block_cols >= 0
    padded_index = jnp.where(present, block_cols + 2, 0).astype(jnp.int32)
    mask_f = present.astype(jnp.float32)[:, :, None, None]
    vals_f = block_vals.astype(jnp.float32)
    panels = node_feats.reshape(block_count, 128, feat_width).astype(jnp.float32)
    padded = jnp.pad(panels, ((2, 2), (0, 0), (0, 0)))
    picked = padded[padded_index] * mask_f
    agg = jnp.einsum("rsij,rsjf->rif", vals_f, picked).reshape(-1, feat_width).astype(jnp.bfloat16)
    pre_act = jnp.dot(agg, w_in, preferred_element_type=jnp.float32)
    hidden = gelu_value(pre_act).astype(jnp.bfloat16)
    branch_out = grouped_product(hidden, w_out, N_REP)
    updated = (node_feats.astype(jnp.float32) + branch_out).astype(jnp.bfloat16)
    grad_hidden = jnp.dot(cotangent, w_out, preferred_element_type=jnp.float32)
    grad_pre = (grad_hidden * gelu_slope(pre_act)).astype(jnp.bfloat16)
    adjoint = grouped_product(grad_pre, w_in, N_REP).astype(jnp.bfloat16)
    adjoint_blocks = adjoint.reshape(block_count, 128, feat_width).astype(jnp.float32)
    contrib = jnp.einsum("rsji,rjf->rsif", vals_f, adjoint_blocks) * mask_f
    landing = jnp.zeros((block_count + 4, 128, feat_width), jnp.float32)
    landing = landing.at[padded_index].add(contrib)
    transposed = landing[2:-2].reshape(-1, feat_width)
    grad_nodes = (cotangent.astype(jnp.float32) + transposed).astype(jnp.bfloat16)
    return updated, grad_nodes
```

```python
import functools

import jax
import jax.numpy as jnp
from jax import lax
from jax.experimental import pallas as pl
from jax.experimental.pallas import tpu as pltpu
from jax.sharding import PartitionSpec as P

F32 = jnp.float32
BF16 = jnp.bfloat16
MESH = pl.DeviceIdType.MESH
PARTS = 2


def dot(a, b, dims=((1,), (0,))):
    return lax.dot_general(a, b, (dims, ((), ())), preferred_element_type=F32)


def gelu_pair(v):
    c = 0.7978845608
    vv = v * v
    t = jnp.tanh(c * (v + 0.044715 * v * vv))
    half = 0.5 * (1.0 + t)
    value = v * half
    slope = half + 0.5 * v * (1.0 - t * t) * c * (1.0 + 3.0 * 0.044715 * vv)
    return value, slope


def kernel(
    n_row, n_rep, cols_ref, spread_ref, feats_ref, vals_ref, w_in_ref, w_out_ref, cot_ref,
    upd_ref, grad_ref,
    ext, marks, vals, vals_t, dense_t, w1_in, w1_out, w2_in, w2_out, cot, cot_full, agg, agg_full, hid, gp,
    adj_p, out_p, adj_in, out_in, adj, c_send, c_sib, c_nbr,
    loc_sem, f_send, f_recv, w_send, w_recv, a_send, a_recv, c_sends, c_recvs,
):
    r, z = lax.axis_index("row"), lax.axis_index("rep")
    k = lax.rem(r, 2)
    sib = r + 1 - 2 * k
    z1, z2 = lax.rem(z, 2), lax.div(z, 2)
    mate = z + 1 - 2 * z1
    peers = [z + 2 - 4 * z2, n_rep - 1 - z, mate]
    bit2, bit4 = lax.rem(lax.div(r, 2), 2), lax.rem(lax.div(r, 4), 2)
    near, far = r + 2 - 4 * bit2, r + 4 - 8 * bit4
    rows, quarter = cot.shape
    half = rows // 2
    part = half // PARTS
    row_blocks, slots = cols_ref.shape
    feat, hidw = w1_in.shape
    has_up, has_dn = r + 2 < n_row, r >= 2
    first = (r - 2) * row_blocks

    def remote(src, dst, send, recv, dev):
        return pltpu.make_async_remote_copy(
            src_ref=src, dst_ref=dst, send_sem=send, recv_sem=recv, device_id=dev, device_id_type=MESH
        )

    def panel(ref, slot):
        return ref.at[pl.ds(slot * row_blocks, row_blocks)]

    def half_part(ref, s, c, count=1):
        start = pl.multiple_of(s * half + c * part, part)
        return ref.at[pl.ds(start, count * part)]

    barrier = pltpu.get_barrier_semaphore()
    for zp in peers:
        pl.semaphore_signal(barrier, inc=1, device_id=(r, zp), device_id_type=MESH)
    pl.semaphore_signal(barrier, inc=1, device_id=(sib, z), device_id_type=MESH)
    pl.semaphore_signal(barrier, inc=1, device_id=(far, z), device_id_type=MESH)

    @pl.when(has_up)
    def _():
        pl.semaphore_signal(barrier, inc=1, device_id=(r + 2, z), device_id_type=MESH)

    @pl.when(has_dn)
    def _():
        pl.semaphore_signal(barrier, inc=1, device_id=(r - 2, z), device_id_type=MESH)

    columns = pl.ds(pl.multiple_of(z * quarter, quarter), quarter)
    own_copy = pltpu.make_async_copy(feats_ref.at[:, :, columns], panel(ext, 2), loc_sem.at[0])
    loads = [
        pltpu.make_async_copy(src, dst, loc_sem.at[1 + i])
        for i, (src, dst) in enumerate(
            (
                (vals_ref, vals),
                (half_part(cot_ref, z1, 0, PARTS), cot_full.at[z]),
                (w_in_ref, w1_in),
                (w_out_ref, w1_out),
                (cot_ref, cot),
            )
        )
    ]
    own_copy.start()
    for copy in loads:
        copy.start()
    own_copy.wait()
    pl.semaphore_wait(barrier, n_rep + 1 + has_up.astype(jnp.int32) + has_dn.astype(jnp.int32))

    own = panel(ext, 2)
    f_up = remote(own, panel(ext, 0), f_send.at[0], f_recv.at[0], (r + 2, z))
    f_dn = remote(own, panel(ext, 4), f_send.at[1], f_recv.at[1], (r - 2, z))
    f_sib = remote(own, panel(ext, 1 + 2 * k), f_send.at[2], f_recv.at[2], (sib, z))
    f_fwd = remote(
        panel(ext, 4 - 4 * k), panel(ext, 3 - 2 * k), f_send.at[3], f_recv.at[3], (sib, z)
    )
    from_dn = remote(own, panel(ext, 0), f_send.at[0], f_recv.at[0], (r - 2, z))
    from_up = remote(own, panel(ext, 4), f_send.at[1], f_recv.at[1], (r + 2, z))
    from_sib = remote(own, panel(ext, 3 - 2 * k), f_send.at[2], f_recv.at[2], (sib, z))
    from_fwd = remote(own, panel(ext, 1 + 2 * k), f_send.at[3], f_recv.at[3], (sib, z))
    fwd_out = jnp.where(k == 0, r + 2 < n_row, r >= 2)
    fwd_in = jnp.where(k == 0, r >= 2, r + 2 < n_row)

    @pl.when(has_up)
    def _():
        f_up.start()

    @pl.when(has_dn)
    def _():
        f_dn.start()

    f_sib.start()

    eighth = feat // 8

    def span(ref, start, count):
        return ref.at[pl.ds(pl.multiple_of(start * eighth, eighth), count * eighth)]

    def rounds(raw, full, base, bit_a, dev_a, bit_b, dev_b):
        mine = 4 * k + 2 * bit_b + bit_a
        plan = (
            (raw, mine, mine, 1, (r, mate)),
            (full, mine, mine + 1 - 2 * bit_a, 1, (dev_a, z)),
            (full, 4 * k + 2 * bit_b, 4 * k + 2 - 2 * bit_b, 2, (dev_b, z)),
            (full, 4 * k, 4 - 4 * k, 4, (sib, z)),
        )
        sent, got = [], []
        for i, (src, lo, there, count, dev) in enumerate(plan):
            sems = (w_send.at[base + i], w_recv.at[base + i])
            sent.append(remote(span(src, lo, count), span(full, lo, count), *sems, dev))
            got.append(remote(span(full, there, count), span(full, there, count), *sems, dev))
        return sent, got

    in_sent, in_got = rounds(w_in_ref, w2_in, 0, bit2, near, bit4, far)
    out_sent, out_got = rounds(w_out_ref, w2_out, 4, bit4, far, bit2, near)

    def exchange(src, dst, kind, c, count=1):
        return [
            remote(
                half_part(src, lax.rem(zp, 2), c, count),
                dst.at[z, pl.ds(c * part, count * part)],
                a_send.at[kind, i], a_recv.at[kind, i], (r, zp),
            )
            for i, zp in enumerate(peers)
        ]

    def arrivals(buf, kind, c, count=1):
        views = [buf.at[zf, pl.ds(c * part, count * part)] for zf in peers]
        return [
            remote(v, v, a_send.at[kind, i], a_recv.at[kind, i], (r, zf))
            for i, (v, zf) in enumerate(zip(views, peers))
        ]

    in_sent[0].start()
    out_sent[0].start()
    cot_out = exchange(cot_ref, cot_full, 0, 0, PARTS)
    for copy in cot_out:
        copy.start()

    @pl.when(jnp.logical_not(has_dn))
    def _():
        ext[0:row_blocks] = jnp.zeros((row_blocks, 128, quarter), BF16)

    @pl.when(jnp.logical_not(has_up))
    def _():
        ext[4 * row_blocks : 5 * row_blocks] = jnp.zeros((row_blocks, 128, quarter), BF16)

    @pl.when(r < 1)
    def _():
        ext[row_blocks : 2 * row_blocks] = jnp.zeros((row_blocks, 128, quarter), BF16)

    @pl.when(r + 1 >= n_row)
    def _():
        ext[3 * row_blocks : 4 * row_blocks] = jnp.zeros((row_blocks, 128, quarter), BF16)

    for copy in loads:
        copy.wait()

    def transpose_block(b, carry):
        for s in range(slots):
            vals_t[b, s] = vals[b, s].astype(F32).T.astype(BF16)
        return carry

    lax.fori_loop(0, row_blocks, transpose_block, 0)

    for b in range(row_blocks):
        for s in range(slots):
            col = jnp.broadcast_to(spread_ref[b : b + 1, s : s + 1], (16, 128))
            marks[b * slots + s] = jnp.where(col >= 0, col - first, -1)

    def fill_dense(t, carry):
        at = pl.ds(pl.multiple_of(t * 128, 128), 128)
        for b in range(row_blocks):
            turned = jnp.zeros((8, 16, 128), BF16)
            for s in range(slots):
                keep = jnp.where(marks[b * slots + s] == t, 1.0, 0.0).astype(BF16)[None]
                turned = turned + vals_t[b, s].reshape(8, 16, 128) * keep
            dense_t[at, b * 128 : (b + 1) * 128] = turned.reshape(128, 128)
        return carry

    out_got[0].wait_recv()
    out_sent[1].start()
    in_got[0].wait_recv()

    @pl.when(has_dn)
    def _():
        from_dn.wait_recv()

    @pl.when(has_up)
    def _():
        from_up.wait_recv()

    @pl.when(fwd_out)
    def _():
        f_fwd.start()

    in_sent[1].start()
    from_sib.wait_recv()

    @pl.when(fwd_in)
    def _():
        from_fwd.wait_recv()

    def gather(b):
        left, right = [], []
        for s in range(slots):
            col = cols_ref[b, s]
            absent = lax.shift_right_logical(col, 31)
            place = col - first + absent * (1 + first + 2 * row_blocks + b)
            keep = jnp.where(marks[b * slots + s] >= 0, 1.0, 0.0).astype(BF16)[None]
            left.append((vals[b, s].reshape(8, 16, 128) * keep).reshape(128, 128))
            right.append(ext[jnp.minimum(jnp.maximum(place, 0), 5 * row_blocks - 1)])
        res = dot(jnp.concatenate(left, axis=1), jnp.concatenate(right, axis=0))
        agg[b * 128 : (b + 1) * 128, :] = res.astype(BF16)

    agg_out = []
    per_part = part // 128
    for c in range(PARTS):
        for s in range(2):
            for i in range(per_part):
                gather((s * PARTS + c) * per_part + i)
        sent = exchange(agg, agg_full, 1 + c, c)
        for copy in sent:
            copy.start()
        agg_out += sent
    for c in range(PARTS):
        agg_full[z, pl.ds(c * part, part)] = agg[
            pl.ds(pl.multiple_of(z1 * half + c * part, part), part), :
        ]

    cut = 3 * row_blocks
    lax.fori_loop(0, cut, fill_dense, 0)
    in_got[1].wait_recv()
    in_sent[2].start()
    out_got[1].wait_recv()
    out_sent[2].start()
    lax.fori_loop(cut, 5 * row_blocks, fill_dense, 0)
    tile = 256

    def hidden_part(w_a, w_b, base, c):
        rs = pl.ds(c * part, part)

        def step(i, carry):
            hc = pl.ds(pl.multiple_of(i * tile, tile), tile)
            to = pl.ds(pl.multiple_of(base + i * tile, tile), tile)
            x = jnp.concatenate([agg_full[q, rs] for q in range(n_rep)], axis=1)
            g = jnp.concatenate([cot_full[q, rs] for q in range(n_rep)], axis=1)
            value, slope = gelu_pair(dot(x, w_a[:, hc]))
            hid[rs, to] = value.astype(BF16)
            gp[rs, to] = (dot(g, w_b[:, hc]) * slope).astype(BF16)
            return carry

        lax.fori_loop(0, hidw // tile, step, 0)

    def product(src, w_a, w_b, dst, zq, c):
        at = pl.ds(pl.multiple_of(zq * quarter, quarter), quarter)
        rs = pl.ds(c * part, part)
        res = dot(src[rs, :hidw], w_a[at, :], ((1,), (1,)))
        res = res + dot(src[rs, hidw:], w_b[at, :], ((1,), (1,)))
        dst[zq, rs] = res.astype(BF16)

    def spread(src, w_a, w_b, made, landing, kind, c):
        sent = []
        for i, zp in enumerate(peers):
            product(src, w_a, w_b, made, zp, c)
            rs = pl.ds(c * part, part)
            copy = remote(
                made.at[zp, rs], landing.at[z, rs], a_send.at[kind, i], a_recv.at[kind, i], (r, zp)
            )
            copy.start()
            sent.append(copy)
        product(src, w_a, w_b, landing, z, c)
        return sent

    for copy in arrivals(cot_full, 0, 0, PARTS):
        copy.wait_recv()
    adj_out, out_out = [], []
    for c in range(PARTS):
        for copy in arrivals(agg_full, 1 + c, c):
            copy.wait_recv()
        hidden_part(w1_in, w1_out, 0, c)
        if c == 0:
            in_got[2].wait_recv()
            in_sent[3].start()
            out_got[2].wait_recv()
            out_sent[3].start()
            in_got[3].wait_recv()
            out_got[3].wait_recv()
        hidden_part(w2_in, w2_out, hidw, c)
        adj_out += spread(gp, w1_in, w2_in, adj_p, adj_in, 1 + PARTS + c, c)
    for c in range(PARTS):
        out_out += spread(hid, w1_out, w2_out, out_p, out_in, 1 + 2 * PARTS + c, c)

    for c in range(PARTS):
        for copy in arrivals(adj_in, 1 + PARTS + c, c):
            copy.wait_recv()
    for s in range(2):
        total = adj_in[s].astype(F32)
        for q in range(s + 2, n_rep, 2):
            total = total + adj_in[q].astype(F32)
        adj[s * half : (s + 1) * half] = total.astype(BF16)

    def piece(p, m):
        at = pl.ds(pl.multiple_of(p * rows + m * tile, tile), tile)
        return dot(dense_t[at, :], adj[...])

    def put(p, slot):
        def step(m, carry):
            at = pl.ds(pl.multiple_of(m * tile, tile), tile)
            c_send[slot, at, :] = piece(p, m).astype(BF16)
            return carry

        lax.fori_loop(0, rows // tile, step, 0)

    plain_to, helped_to = r - 2 + 4 * k, r + 2 - 4 * k
    c_help = remote(c_send.at[0], c_sib.at[0], c_sends.at[0], c_recvs.at[0], (sib, z))
    c_own = remote(c_send.at[1], c_sib.at[1], c_sends.at[1], c_recvs.at[1], (sib, z))
    c_plain = remote(
        c_send.at[2], c_nbr.at[1 - k], c_sends.at[2], c_recvs.at[3 - k], (plain_to, z)
    )
    c_helped = remote(
        c_send.at[3], c_nbr.at[k], c_sends.at[3], c_recvs.at[2 + k], (helped_to, z)
    )
    put(1 + 2 * k, 0)
    c_help.start()
    put(4 * k, 2)
    plain_ok, helped_ok = fwd_in, fwd_out

    @pl.when(plain_ok)
    def _():
        c_plain.start()

    c_help.wait_recv()

    def add_help(m, carry):
        at = pl.ds(pl.multiple_of(m * tile, tile), tile)
        total = piece(4 - 4 * k, m) + c_sib[0, at, :].astype(F32)
        c_send[3, at, :] = total.astype(BF16)
        return carry

    lax.fori_loop(0, rows // tile, add_help, 0)

    @pl.when(helped_ok)
    def _():
        c_helped.start()

    put(3 - 2 * k, 1)
    c_own.start()

    for c in range(PARTS):
        for copy in arrivals(out_in, 1 + 2 * PARTS + c, c):
            copy.wait_recv()
    for s in range(2):
        total = out_in[s].astype(F32)
        for q in range(s + 2, n_rep, 2):
            total = total + out_in[q].astype(F32)
        start, count = 2 * row_blocks + s * row_blocks // 2, row_blocks // 2
        mine = ext[start : start + count].reshape(half, quarter)
        upd_ref[s * half : (s + 1) * half] = (mine.astype(F32) + total).astype(BF16)

    c_own.wait_recv()
    from_low = remote(c_nbr.at[0], c_nbr.at[0], c_sends.at[2], c_recvs.at[2], (r - 2, z))
    from_high = remote(c_nbr.at[1], c_nbr.at[1], c_sends.at[3], c_recvs.at[3], (r + 2, z))

    @pl.when(has_dn)
    def _():
        from_low.wait_recv()

    @pl.when(jnp.logical_not(has_dn))
    def _():
        c_nbr[0] = jnp.zeros((rows, quarter), BF16)

    @pl.when(has_up)
    def _():
        from_high.wait_recv()

    @pl.when(jnp.logical_not(has_up))
    def _():
        c_nbr[1] = jnp.zeros((rows, quarter), BF16)

    def finish(m, carry):
        at = pl.ds(pl.multiple_of(m * tile, tile), tile)
        total = piece(2, m) + c_sib[1, at, :].astype(F32)
        total = total + c_nbr[0, at, :].astype(F32) + c_nbr[1, at, :].astype(F32)
        grad_ref[at, :] = (cot[at, :].astype(F32) + total).astype(BF16)
        return carry

    lax.fori_loop(0, rows // tile, finish, 0)

    for copy in cot_out + in_sent + out_sent + agg_out + adj_out + out_out + [f_sib, c_help, c_own]:
        copy.wait_send()
    for ok, copy in (
        (has_up, f_up), (has_dn, f_dn), (fwd_out, f_fwd), (plain_ok, c_plain), (helped_ok, c_helped)
    ):
        pl.when(ok)(copy.wait_send)


def body(n_row, n_rep, node_feats, block_cols, block_vals, w_in, w_out, cotangent):
    rows, quarter = cotangent.shape
    row_blocks, slots = block_cols.shape
    feat, hidw = w_in.shape
    half = rows // 2
    kinds = 1 + 3 * PARTS
    vmem = pl.BlockSpec(memory_space=pltpu.VMEM)
    anywhere = pl.BlockSpec(memory_space=pl.ANY)
    dma = pltpu.SemaphoreType.DMA
    return pl.pallas_call(
        functools.partial(kernel, n_row, n_rep),
        out_shape=(jax.ShapeDtypeStruct((rows, quarter), BF16),) * 2,
        in_specs=[pl.BlockSpec(memory_space=pltpu.SMEM), vmem] + [anywhere] * 5,
        out_specs=(vmem, vmem),
        scratch_shapes=[
            pltpu.VMEM((5 * row_blocks, 128, quarter), BF16),
            pltpu.VMEM((row_blocks * slots, 16, 128), jnp.int32),
            pltpu.VMEM((row_blocks, slots, 128, 128), BF16),
            pltpu.VMEM((row_blocks, slots, 128, 128), BF16),
            pltpu.VMEM((5 * rows, rows), BF16),
            pltpu.VMEM((feat, hidw), BF16),
            pltpu.VMEM((feat, hidw), BF16),
            pltpu.VMEM((feat, hidw), BF16),
            pltpu.VMEM((feat, hidw), BF16),
            pltpu.VMEM((rows, quarter), BF16),
            pltpu.VMEM((n_rep, half, quarter), BF16),
            pltpu.VMEM((rows, quarter), BF16),
            pltpu.VMEM((n_rep, half, quarter), BF16),
            pltpu.VMEM((half, 2 * hidw), BF16),
            pltpu.VMEM((half, 2 * hidw), BF16),
            pltpu.VMEM((n_rep, half, quarter), BF16),
            pltpu.VMEM((n_rep, half, quarter), BF16),
            pltpu.VMEM((n_rep, half, quarter), BF16),
            pltpu.VMEM((n_rep, half, quarter), BF16),
            pltpu.VMEM((rows, quarter), BF16),
            pltpu.VMEM((4, rows, quarter), BF16),
            pltpu.VMEM((2, rows, quarter), BF16),
            pltpu.VMEM((2, rows, quarter), BF16),
            dma((6,)),
            dma((4,)),
            dma((4,)),
            dma((8,)),
            dma((8,)),
            dma((kinds, n_rep - 1)),
            dma((kinds, n_rep - 1)),
            dma((4,)),
            dma((4,)),
        ],
        compiler_params=pltpu.CompilerParams(
            collective_id=0, has_side_effects=True, vmem_limit_bytes=60 * 1024 * 1024
        ),
    )(block_cols, block_cols, node_feats.reshape(row_blocks, 128, feat), block_vals, w_in, w_out, cotangent)


def solution(mesh):
    in_specs = (
        P("row", None),
        P("row", None),
        P("row", None, None, None),
        P(None, "rep"),
        P(None, "rep"),
        P("row", "rep"),
    )
    out_specs = (P("row", "rep"), P("row", "rep"))
    run = functools.partial(body, mesh.shape["row"], mesh.shape["rep"])
    return jax.shard_map(run, mesh=mesh, in_specs=in_specs, out_specs=out_specs, check_vma=False)
```

```python
import functools

import jax
import jax.numpy as jnp
from jax import lax
from jax.experimental import pallas as pl
from jax.experimental.pallas import tpu as pltpu
from jax.sharding import PartitionSpec as P

F32 = jnp.float32
BF16 = jnp.bfloat16
MESH = pl.DeviceIdType.MESH
PARTS = 2
WIDE = 2


def dot(a, b, dims=((1,), (0,))):
    return lax.dot_general(a, b, (dims, ((), ())), preferred_element_type=F32)


def gelu_pair(v):
    c = 0.7978845608
    vv = v * v
    t = jnp.tanh(c * (v + 0.044715 * v * vv))
    half = 0.5 * (1.0 + t)
    value = v * half
    slope = half + 0.5 * v * (1.0 - t * t) * c * (1.0 + 3.0 * 0.044715 * vv)
    return value, slope


def kernel(
    n_row, n_rep, cols_ref, spread_ref, feats_ref, vals_ref, w_in_ref, w_out_ref, cot_ref,
    upd_ref, grad_ref,
    ext, marks, vals, vals_t, dense_t, w1_in, w1_out, w2_in, w2_out, cot, cot_full, agg, agg_full, hid, gp,
    adj_p, out_p, adj_in, out_in, adj, c_send, c_sib, c_nbr,
    loc_sem, f_send, f_recv, w_send, w_recv, a_send, a_recv, c_sends, c_recvs,
):
    r, z = lax.axis_index("row"), lax.axis_index("rep")
    k = lax.rem(r, 2)
    sib = r + 1 - 2 * k
    z1, z2 = lax.rem(z, 2), lax.div(z, 2)
    mate = z + 1 - 2 * z1
    peers = [z + 2 - 4 * z2, n_rep - 1 - z, mate]
    bit2, bit4 = lax.rem(lax.div(r, 2), 2), lax.rem(lax.div(r, 4), 2)
    near, far = r + 2 - 4 * bit2, r + 4 - 8 * bit4
    rows, quarter = cot.shape
    half = rows // 2
    part = half // PARTS
    width = quarter // WIDE
    row_blocks, slots = cols_ref.shape
    feat, hidw = w1_in.shape
    has_up, has_dn = r + 2 < n_row, r >= 2
    first = (r - 2) * row_blocks

    def remote(src, dst, send, recv, dev):
        return pltpu.make_async_remote_copy(
            src_ref=src, dst_ref=dst, send_sem=send, recv_sem=recv, device_id=dev, device_id_type=MESH
        )

    def panel(ref, slot):
        return ref.at[pl.ds(slot * row_blocks, row_blocks)]

    def half_part(ref, s, c, count=1):
        start = pl.multiple_of(s * half + c * part, part)
        return ref.at[pl.ds(start, count * part)]

    barrier = pltpu.get_barrier_semaphore()
    for zp in peers:
        pl.semaphore_signal(barrier, inc=1, device_id=(r, zp), device_id_type=MESH)
    pl.semaphore_signal(barrier, inc=1, device_id=(sib, z), device_id_type=MESH)
    pl.semaphore_signal(barrier, inc=1, device_id=(far, z), device_id_type=MESH)

    @pl.when(has_up)
    def _():
        pl.semaphore_signal(barrier, inc=1, device_id=(r + 2, z), device_id_type=MESH)

    @pl.when(has_dn)
    def _():
        pl.semaphore_signal(barrier, inc=1, device_id=(r - 2, z), device_id_type=MESH)

    columns = pl.ds(pl.multiple_of(z * quarter, quarter), quarter)
    own_copy = pltpu.make_async_copy(feats_ref.at[:, :, columns], panel(ext, 2), loc_sem.at[0])
    loads = [
        pltpu.make_async_copy(src, dst, loc_sem.at[1 + i])
        for i, (src, dst) in enumerate(
            (
                (vals_ref, vals),
                (half_part(cot_ref, z1, 0, PARTS), cot_full.at[z]),
                (w_in_ref, w1_in),
                (w_out_ref, w1_out),
                (cot_ref, cot),
            )
        )
    ]
    own_copy.start()
    for copy in loads:
        copy.start()
    own_copy.wait()
    pl.semaphore_wait(barrier, n_rep + 1 + has_up.astype(jnp.int32) + has_dn.astype(jnp.int32))

    own = panel(ext, 2)
    f_up = remote(own, panel(ext, 0), f_send.at[0], f_recv.at[0], (r + 2, z))
    f_dn = remote(own, panel(ext, 4), f_send.at[1], f_recv.at[1], (r - 2, z))
    f_sib = remote(own, panel(ext, 1 + 2 * k), f_send.at[2], f_recv.at[2], (sib, z))
    f_fwd = remote(
        panel(ext, 4 - 4 * k), panel(ext, 3 - 2 * k), f_send.at[3], f_recv.at[3], (sib, z)
    )
    from_dn = remote(own, panel(ext, 0), f_send.at[0], f_recv.at[0], (r - 2, z))
    from_up = remote(own, panel(ext, 4), f_send.at[1], f_recv.at[1], (r + 2, z))
    from_sib = remote(own, panel(ext, 3 - 2 * k), f_send.at[2], f_recv.at[2], (sib, z))
    from_fwd = remote(own, panel(ext, 1 + 2 * k), f_send.at[3], f_recv.at[3], (sib, z))
    fwd_out = jnp.where(k == 0, r + 2 < n_row, r >= 2)
    fwd_in = jnp.where(k == 0, r >= 2, r + 2 < n_row)

    @pl.when(has_up)
    def _():
        f_up.start()

    @pl.when(has_dn)
    def _():
        f_dn.start()

    f_sib.start()

    eighth = feat // 8

    def span(ref, start, count):
        return ref.at[pl.ds(pl.multiple_of(start * eighth, eighth), count * eighth)]

    def rounds(raw, full, base, bit_a, dev_a, bit_b, dev_b):
        mine = 4 * k + 2 * bit_b + bit_a
        plan = (
            (raw, mine, mine, 1, (r, mate)),
            (full, mine, mine + 1 - 2 * bit_a, 1, (dev_a, z)),
            (full, 4 * k + 2 * bit_b, 4 * k + 2 - 2 * bit_b, 2, (dev_b, z)),
            (full, 4 * k, 4 - 4 * k, 4, (sib, z)),
        )
        sent, got = [], []
        for i, (src, lo, there, count, dev) in enumerate(plan):
            sems = (w_send.at[base + i], w_recv.at[base + i])
            sent.append(remote(span(src, lo, count), span(full, lo, count), *sems, dev))
            got.append(remote(span(full, there, count), span(full, there, count), *sems, dev))
        return sent, got

    in_sent, in_got = rounds(w_in_ref, w2_in, 0, bit2, near, bit4, far)
    out_sent, out_got = rounds(w_out_ref, w2_out, 4, bit4, far, bit2, near)

    def exchange(src, dst, kind, c, count=1):
        return [
            remote(
                half_part(src, lax.rem(zp, 2), c, count),
                dst.at[z, pl.ds(c * part, count * part)],
                a_send.at[kind, i], a_recv.at[kind, i], (r, zp),
            )
            for i, zp in enumerate(peers)
        ]

    def arrivals(buf, kind, c, count=1):
        views = [buf.at[zf, pl.ds(c * part, count * part)] for zf in peers]
        return [
            remote(v, v, a_send.at[kind, i], a_recv.at[kind, i], (r, zf))
            for i, (v, zf) in enumerate(zip(views, peers))
        ]

    in_sent[0].start()
    out_sent[0].start()
    cot_out = exchange(cot_ref, cot_full, 0, 0, PARTS)
    for copy in cot_out:
        copy.start()

    @pl.when(jnp.logical_not(has_dn))
    def _():
        ext[0:row_blocks] = jnp.zeros((row_blocks, 128, quarter), BF16)

    @pl.when(jnp.logical_not(has_up))
    def _():
        ext[4 * row_blocks : 5 * row_blocks] = jnp.zeros((row_blocks, 128, quarter), BF16)

    @pl.when(r < 1)
    def _():
        ext[row_blocks : 2 * row_blocks] = jnp.zeros((row_blocks, 128, quarter), BF16)

    @pl.when(r + 1 >= n_row)
    def _():
        ext[3 * row_blocks : 4 * row_blocks] = jnp.zeros((row_blocks, 128, quarter), BF16)

    for copy in loads:
        copy.wait()

    def transpose_block(b, carry):
        for s in range(slots):
            vals_t[b, s] = vals[b, s].astype(F32).T.astype(BF16)
        return carry

    lax.fori_loop(0, row_blocks, transpose_block, 0)

    for b in range(row_blocks):
        for s in range(slots):
            col = jnp.broadcast_to(spread_ref[b : b + 1, s : s + 1], (16, 128))
            marks[b * slots + s] = jnp.where(col >= 0, col - first, -1)

    def fill_dense(t, carry):
        at = pl.ds(pl.multiple_of(t * 128, 128), 128)
        for b in range(row_blocks):
            turned = jnp.zeros((8, 16, 128), BF16)
            for s in range(slots):
                keep = jnp.where(marks[b * slots + s] == t, 1.0, 0.0).astype(BF16)[None]
                turned = turned + vals_t[b, s].reshape(8, 16, 128) * keep
            dense_t[at, b * 128 : (b + 1) * 128] = turned.reshape(128, 128)
        return carry

    out_got[0].wait_recv()
    out_sent[1].start()
    in_got[0].wait_recv()

    @pl.when(has_dn)
    def _():
        from_dn.wait_recv()

    @pl.when(has_up)
    def _():
        from_up.wait_recv()

    @pl.when(fwd_out)
    def _():
        f_fwd.start()

    in_sent[1].start()
    from_sib.wait_recv()

    @pl.when(fwd_in)
    def _():
        from_fwd.wait_recv()

    def gather(b):
        left, right = [], []
        for s in range(slots):
            col = cols_ref[b, s]
            absent = lax.shift_right_logical(col, 31)
            place = col - first + absent * (1 + first + 2 * row_blocks + b)
            keep = jnp.where(marks[b * slots + s] >= 0, 1.0, 0.0).astype(BF16)[None]
            left.append((vals[b, s].reshape(8, 16, 128) * keep).reshape(128, 128))
            right.append(ext[jnp.minimum(jnp.maximum(place, 0), 5 * row_blocks - 1)])
        res = dot(jnp.concatenate(left, axis=1), jnp.concatenate(right, axis=0))
        agg[b * 128 : (b + 1) * 128, :] = res.astype(BF16)

    agg_out = []
    per_part = part // 128
    for c in range(PARTS):
        for s in range(2):
            for i in range(per_part):
                gather((s * PARTS + c) * per_part + i)
        agg_out.append(exchange(agg, agg_full, 1 + c, c))
        if c == 0:
            for copy in agg_out[0]:
                copy.start()
    for c in range(PARTS):
        agg_full[z, pl.ds(c * part, part)] = agg[
            pl.ds(pl.multiple_of(z1 * half + c * part, part), part), :
        ]

    cut = 3 * row_blocks
    lax.fori_loop(0, cut, fill_dense, 0)
    in_got[1].wait_recv()
    in_sent[2].start()
    out_got[1].wait_recv()
    out_sent[2].start()
    for c in range(1, PARTS):
        for copy in agg_out[c - 1]:
            copy.wait_send()
        for copy in agg_out[c]:
            copy.start()
    lax.fori_loop(cut, 5 * row_blocks, fill_dense, 0)
    tile = 256

    def hidden_part(w_a, w_b, base, c):
        rs = pl.ds(c * part, part)

        def step(i, carry):
            hc = pl.ds(pl.multiple_of(i * tile, tile), tile)
            to = pl.ds(pl.multiple_of(base + i * tile, tile), tile)
            x = jnp.concatenate([agg_full[q, rs] for q in range(n_rep)], axis=1)
            g = jnp.concatenate([cot_full[q, rs] for q in range(n_rep)], axis=1)
            value, slope = gelu_pair(dot(x, w_a[:, hc]))
            hid[rs, to] = value.astype(BF16)
            gp[rs, to] = (dot(g, w_b[:, hc]) * slope).astype(BF16)
            return carry

        lax.fori_loop(0, hidw // tile, step, 0)

    def product(src, w_a, w_b, zq, c):
        at = pl.ds(pl.multiple_of(zq * quarter, quarter), quarter)
        rs = pl.ds(c * part, part)
        res = dot(src[rs, :hidw], w_a[at, :], ((1,), (1,)))
        res = res + dot(src[rs, hidw:], w_b[at, :], ((1,), (1,)))
        return res.astype(BF16)

    def adj_copies(f, c):
        kind = 1 + PARTS + f * PARTS + c
        rs = pl.ds(c * part, part)
        return [
            remote(
                adj_p.at[zp, f, rs], adj_in.at[z, f, rs],
                a_send.at[kind, i], a_recv.at[kind, i], (r, zp),
            )
            for i, zp in enumerate(peers)
        ]

    def adj_arrivals(f, c):
        kind = 1 + PARTS + f * PARTS + c
        views = [adj_in.at[zf, f, pl.ds(c * part, part)] for zf in peers]
        return [
            remote(v, v, a_send.at[kind, i], a_recv.at[kind, i], (r, zf))
            for i, (v, zf) in enumerate(zip(views, peers))
        ]

    for copy in arrivals(cot_full, 0, 0, PARTS):
        copy.wait_recv()
    adj_sent = [[adj_copies(f, c) for c in range(PARTS)] for f in range(WIDE)]
    for c in range(PARTS):
        for copy in arrivals(agg_full, 1 + c, c):
            copy.wait_recv()
        hidden_part(w1_in, w1_out, 0, c)
        if c == 0:
            in_got[2].wait_recv()
            in_sent[3].start()
            out_got[2].wait_recv()
            out_sent[3].start()
            in_got[3].wait_recv()
            out_got[3].wait_recv()
        hidden_part(w2_in, w2_out, hidw, c)
        rs = pl.ds(c * part, part)
        for i, zp in enumerate(peers + [z]):
            res = product(gp, w1_in, w2_in, zp, c)
            made = adj_p if i < n_rep - 1 else adj_in
            for f in range(WIDE):
                made[zp, f, rs] = res[:, f * width : (f + 1) * width]
            if i < n_rep - 1:
                adj_sent[0][c][i].start()

    out_sends = []
    for c in range(PARTS):
        rs = pl.ds(c * part, part)
        kind = 1 + (1 + WIDE) * PARTS + c
        for i, zp in enumerate(peers):
            out_p[zp, rs] = product(hid, w1_out, w2_out, zp, c)
            out_sends.append(
                remote(
                    out_p.at[zp, rs], out_in.at[z, rs],
                    a_send.at[kind, i], a_recv.at[kind, i], (r, zp),
                )
            )
        out_in[z, rs] = product(hid, w1_out, w2_out, z, c)

    tile = 256
    plain_to, helped_to = r - 2 + 4 * k, r + 2 - 4 * k
    plain_ok, helped_ok = fwd_in, fwd_out
    p5_sent = []

    def turn(f):
        for c in range(PARTS):
            for copy in adj_arrivals(f, c):
                copy.wait_recv()
        for s in range(2):
            total = adj_in[s, f].astype(F32)
            for q in range(s + 2, n_rep, 2):
                total = total + adj_in[q, f].astype(F32)
            adj[f, s * half : (s + 1) * half] = total.astype(BF16)

        def put(p, slot):
            def step(m, carry):
                at = pl.ds(pl.multiple_of(m * tile, tile), tile)
                c_send[4 * f + slot, at, :] = piece(f, p, m).astype(BF16)
                return carry

            lax.fori_loop(0, rows // tile, step, 0)

        def cross(slot, dst, got, dev):
            return remote(
                c_send.at[4 * f + slot], dst, c_sends.at[4 * f + slot], c_recvs.at[4 * f + got], dev
            )

        c_help = cross(0, c_sib.at[2 * f], 0, (sib, z))
        c_own = cross(1, c_sib.at[2 * f + 1], 1, (sib, z))
        c_plain = cross(2, c_nbr.at[2 * f + 1 - k], 3 - k, (plain_to, z))
        c_helped = cross(3, c_nbr.at[2 * f + k], 2 + k, (helped_to, z))
        put(1 + 2 * k, 0)
        c_help.start()
        put(4 * k, 2)

        @pl.when(plain_ok)
        def _():
            c_plain.start()

        c_help.wait_recv()

        def add_help(m, carry):
            at = pl.ds(pl.multiple_of(m * tile, tile), tile)
            total = piece(f, 4 - 4 * k, m) + c_sib[2 * f, at, :].astype(F32)
            c_send[4 * f + 3, at, :] = total.astype(BF16)
            return carry

        lax.fori_loop(0, rows // tile, add_help, 0)

        @pl.when(helped_ok)
        def _():
            c_helped.start()

        put(3 - 2 * k, 1)
        c_own.start()
        p5_sent.append((c_help, c_own, c_plain, c_helped))

    def piece(f, p, m):
        at = pl.ds(pl.multiple_of(p * rows + m * tile, tile), tile)
        return dot(dense_t[at, :], adj[f])

    def finish(f):
        p5_sent[f][1].wait_recv()
        from_low = remote(
            c_nbr.at[2 * f], c_nbr.at[2 * f], c_sends.at[4 * f + 2], c_recvs.at[4 * f + 2], (r - 2, z)
        )
        from_high = remote(
            c_nbr.at[2 * f + 1], c_nbr.at[2 * f + 1], c_sends.at[4 * f + 3], c_recvs.at[4 * f + 3],
            (r + 2, z),
        )

        @pl.when(has_dn)
        def _():
            from_low.wait_recv()

        @pl.when(jnp.logical_not(has_dn))
        def _():
            c_nbr[2 * f] = jnp.zeros((rows, width), BF16)

        @pl.when(has_up)
        def _():
            from_high.wait_recv()

        @pl.when(jnp.logical_not(has_up))
        def _():
            c_nbr[2 * f + 1] = jnp.zeros((rows, width), BF16)

        cs = slice(f * width, (f + 1) * width)

        def step(m, carry):
            at = pl.ds(pl.multiple_of(m * tile, tile), tile)
            total = piece(f, 2, m) + c_sib[2 * f + 1, at, :].astype(F32)
            total = total + c_nbr[2 * f, at, :].astype(F32) + c_nbr[2 * f + 1, at, :].astype(F32)
            grad_ref[at, cs] = (cot[at, cs].astype(F32) + total).astype(BF16)
            return carry

        lax.fori_loop(0, rows // tile, step, 0)

    for f in range(WIDE):
        for copies in adj_sent[f]:
            for copy in copies:
                copy.wait_send()
        following = sum(adj_sent[f + 1], []) if f + 1 < WIDE else out_sends
        for copy in following:
            copy.start()
        turn(f)
    for f in range(WIDE - 1):
        finish(f)
    for c in range(PARTS):
        for copy in arrivals(out_in, 1 + (1 + WIDE) * PARTS + c, c):
            copy.wait_recv()
    for s in range(2):
        total = out_in[s].astype(F32)
        for q in range(s + 2, n_rep, 2):
            total = total + out_in[q].astype(F32)
        start, count = 2 * row_blocks + s * row_blocks // 2, row_blocks // 2
        mine = ext[start : start + count].reshape(half, quarter)
        upd_ref[s * half : (s + 1) * half] = (mine.astype(F32) + total).astype(BF16)
    finish(WIDE - 1)

    for copy in cot_out + in_sent + out_sent + agg_out[-1] + out_sends + [f_sib]:
        copy.wait_send()
    late = [(has_up, f_up), (has_dn, f_dn), (fwd_out, f_fwd)]
    for c_help, c_own, c_plain, c_helped in p5_sent:
        c_help.wait_send()
        c_own.wait_send()
        late += [(plain_ok, c_plain), (helped_ok, c_helped)]
    for ok, copy in late:
        pl.when(ok)(copy.wait_send)


def body(n_row, n_rep, node_feats, block_cols, block_vals, w_in, w_out, cotangent):
    rows, quarter = cotangent.shape
    row_blocks, slots = block_cols.shape
    feat, hidw = w_in.shape
    half = rows // 2
    kinds = 1 + (2 + WIDE) * PARTS
    width = quarter // WIDE
    vmem = pl.BlockSpec(memory_space=pltpu.VMEM)
    anywhere = pl.BlockSpec(memory_space=pl.ANY)
    dma = pltpu.SemaphoreType.DMA
    return pl.pallas_call(
        functools.partial(kernel, n_row, n_rep),
        out_shape=(jax.ShapeDtypeStruct((rows, quarter), BF16),) * 2,
        in_specs=[pl.BlockSpec(memory_space=pltpu.SMEM), vmem] + [anywhere] * 5,
        out_specs=(vmem, vmem),
        scratch_shapes=[
            pltpu.VMEM((5 * row_blocks, 128, quarter), BF16),
            pltpu.VMEM((row_blocks * slots, 16, 128), jnp.int32),
            pltpu.VMEM((row_blocks, slots, 128, 128), BF16),
            pltpu.VMEM((row_blocks, slots, 128, 128), BF16),
            pltpu.VMEM((5 * rows, rows), BF16),
            pltpu.VMEM((feat, hidw), BF16),
            pltpu.VMEM((feat, hidw), BF16),
            pltpu.VMEM((feat, hidw), BF16),
            pltpu.VMEM((feat, hidw), BF16),
            pltpu.VMEM((rows, quarter), BF16),
            pltpu.VMEM((n_rep, half, quarter), BF16),
            pltpu.VMEM((rows, quarter), BF16),
            pltpu.VMEM((n_rep, half, quarter), BF16),
            pltpu.VMEM((half, 2 * hidw), BF16),
            pltpu.VMEM((half, 2 * hidw), BF16),
            pltpu.VMEM((n_rep, WIDE, half, width), BF16),
            pltpu.VMEM((n_rep, half, quarter), BF16),
            pltpu.VMEM((n_rep, WIDE, half, width), BF16),
            pltpu.VMEM((n_rep, half, quarter), BF16),
            pltpu.VMEM((WIDE, rows, width), BF16),
            pltpu.VMEM((4 * WIDE, rows, width), BF16),
            pltpu.VMEM((2 * WIDE, rows, width), BF16),
            pltpu.VMEM((2 * WIDE, rows, width), BF16),
            dma((6,)),
            dma((4,)),
            dma((4,)),
            dma((8,)),
            dma((8,)),
            dma((kinds, n_rep - 1)),
            dma((kinds, n_rep - 1)),
            dma((4 * WIDE,)),
            dma((4 * WIDE,)),
        ],
        compiler_params=pltpu.CompilerParams(
            collective_id=0, has_side_effects=True, vmem_limit_bytes=60 * 1024 * 1024
        ),
    )(block_cols, block_cols, node_feats.reshape(row_blocks, 128, feat), block_vals, w_in, w_out, cotangent)


def solution(mesh):
    in_specs = (
        P("row", None),
        P("row", None),
        P("row", None, None, None),
        P(None, "rep"),
        P(None, "rep"),
        P("row", "rep"),
    )
    out_specs = (P("row", "rep"), P("row", "rep"))
    run = functools.partial(body, mesh.shape["row"], mesh.shape["rep"])
    return jax.shard_map(run, mesh=mesh, in_specs=in_specs, out_specs=out_specs, check_vma=False)
```

```python
import functools

import jax
import jax.numpy as jnp
from jax import lax
from jax.experimental import pallas as pl
from jax.experimental.pallas import tpu as pltpu
from jax.sharding import PartitionSpec as P

F32 = jnp.float32
BF16 = jnp.bfloat16
MESH = pl.DeviceIdType.MESH
PARTS = 2
WIDE = 2
CUTS = 4


def dot(a, b, dims=((1,), (0,))):
    return lax.dot_general(a, b, (dims, ((), ())), preferred_element_type=F32)


def gelu_pair(v):
    c = 0.7978845608
    vv = v * v
    t = jnp.tanh(c * (v + 0.044715 * v * vv))
    half = 0.5 * (1.0 + t)
    value = v * half
    slope = half + 0.5 * v * (1.0 - t * t) * c * (1.0 + 3.0 * 0.044715 * vv)
    return value, slope


def kernel(
    n_row, n_rep, cols_ref, spread_ref, feats_ref, vals_ref, w_in_ref, w_out_ref, cot_ref,
    upd_hbm, grad_hbm,
    upd_ref, grad_ref, ext, marks, vals, vals_t, dense_t, w1_in, w1_out, w2_in, w2_out, cot, cot_full, agg, agg_full, hid, gp,
    adj_p, out_p, adj_in, out_in, adj, c_send, c_sib, c_nbr,
    loc_sem, f_send, f_recv, w_send, w_recv, a_send, a_recv, c_sends, c_recvs,
):
    r, z = lax.axis_index("row"), lax.axis_index("rep")
    k = lax.rem(r, 2)
    sib = r + 1 - 2 * k
    z1, z2 = lax.rem(z, 2), lax.div(z, 2)
    mate = z + 1 - 2 * z1
    peers = [z + 2 - 4 * z2, n_rep - 1 - z, mate]
    bit2, bit4 = lax.rem(lax.div(r, 2), 2), lax.rem(lax.div(r, 4), 2)
    near, far = r + 2 - 4 * bit2, r + 4 - 8 * bit4
    rows, quarter = cot.shape
    half = rows // 2
    part = half // PARTS
    width = quarter // WIDE
    slots, row_blocks = cols_ref.shape
    feat, hidw = w1_in.shape
    has_up, has_dn = r + 2 < n_row, r >= 2
    first = (r - 2) * row_blocks

    def remote(src, dst, send, recv, dev):
        return pltpu.make_async_remote_copy(
            src_ref=src, dst_ref=dst, send_sem=send, recv_sem=recv, device_id=dev, device_id_type=MESH
        )

    def panel(ref, slot):
        return ref.at[pl.ds(slot * row_blocks, row_blocks)]

    def half_part(ref, s, c, count=1):
        start = pl.multiple_of(s * half + c * part, part)
        return ref.at[pl.ds(start, count * part)]

    barrier = pltpu.get_barrier_semaphore()
    for zp in peers:
        pl.semaphore_signal(barrier, inc=1, device_id=(r, zp), device_id_type=MESH)
    pl.semaphore_signal(barrier, inc=1, device_id=(sib, z), device_id_type=MESH)
    pl.semaphore_signal(barrier, inc=1, device_id=(far, z), device_id_type=MESH)

    @pl.when(has_up)
    def _():
        pl.semaphore_signal(barrier, inc=1, device_id=(r + 2, z), device_id_type=MESH)

    @pl.when(has_dn)
    def _():
        pl.semaphore_signal(barrier, inc=1, device_id=(r - 2, z), device_id_type=MESH)

    columns = pl.ds(pl.multiple_of(z * quarter, quarter), quarter)
    own_copy = pltpu.make_async_copy(feats_ref.at[:, :, columns], panel(ext, 2), loc_sem.at[0])
    loads = [
        pltpu.make_async_copy(src, dst, loc_sem.at[1 + i])
        for i, (src, dst) in enumerate(
            (
                (vals_ref, vals),
                (half_part(cot_ref, z1, 0, PARTS), cot_full.at[z]),
                (w_in_ref, w1_in),
                (w_out_ref, w1_out),
                (cot_ref, cot),
            )
        )
    ]
    own_copy.start()
    for copy in loads:
        copy.start()
    own_copy.wait()
    pl.semaphore_wait(barrier, n_rep + 1 + has_up.astype(jnp.int32) + has_dn.astype(jnp.int32))

    own = panel(ext, 2)
    f_up = remote(own, panel(ext, 0), f_send.at[0], f_recv.at[0], (r + 2, z))
    f_dn = remote(own, panel(ext, 4), f_send.at[1], f_recv.at[1], (r - 2, z))
    f_sib = remote(own, panel(ext, 1 + 2 * k), f_send.at[2], f_recv.at[2], (sib, z))
    f_fwd = remote(
        panel(ext, 4 - 4 * k), panel(ext, 3 - 2 * k), f_send.at[3], f_recv.at[3], (sib, z)
    )
    from_dn = remote(own, panel(ext, 0), f_send.at[0], f_recv.at[0], (r - 2, z))
    from_up = remote(own, panel(ext, 4), f_send.at[1], f_recv.at[1], (r + 2, z))
    from_sib = remote(own, panel(ext, 3 - 2 * k), f_send.at[2], f_recv.at[2], (sib, z))
    from_fwd = remote(own, panel(ext, 1 + 2 * k), f_send.at[3], f_recv.at[3], (sib, z))
    fwd_out = jnp.where(k == 0, r + 2 < n_row, r >= 2)
    fwd_in = jnp.where(k == 0, r >= 2, r + 2 < n_row)

    @pl.when(has_up)
    def _():
        f_up.start()

    @pl.when(has_dn)
    def _():
        f_dn.start()

    f_sib.start()

    eighth = feat // 8

    def span(ref, start, count):
        return ref.at[pl.ds(pl.multiple_of(start * eighth, eighth), count * eighth)]

    def rounds(raw, full, base, bit_a, dev_a, bit_b, dev_b):
        mine = 4 * k + 2 * bit_b + bit_a
        plan = (
            (raw, mine, mine, 1, (r, mate)),
            (full, mine, mine + 1 - 2 * bit_a, 1, (dev_a, z)),
            (full, 4 * k + 2 * bit_b, 4 * k + 2 - 2 * bit_b, 2, (dev_b, z)),
            (full, 4 * k, 4 - 4 * k, 4, (sib, z)),
        )
        sent, got = [], []
        for i, (src, lo, there, count, dev) in enumerate(plan):
            sems = (w_send.at[base + i], w_recv.at[base + i])
            sent.append(remote(span(src, lo, count), span(full, lo, count), *sems, dev))
            got.append(remote(span(full, there, count), span(full, there, count), *sems, dev))
        return sent, got

    in_sent, in_got = rounds(w_in_ref, w2_in, 0, bit2, near, bit4, far)
    out_sent, out_got = rounds(w_out_ref, w2_out, 4, bit4, far, bit2, near)

    def exchange(src, dst, kind, c, count=1):
        return [
            remote(
                half_part(src, lax.rem(zp, 2), c, count),
                dst.at[z, pl.ds(c * part, count * part)],
                a_send.at[kind, i], a_recv.at[kind, i], (r, zp),
            )
            for i, zp in enumerate(peers)
        ]

    def arrivals(buf, kind, c, count=1):
        views = [buf.at[zf, pl.ds(c * part, count * part)] for zf in peers]
        return [
            remote(v, v, a_send.at[kind, i], a_recv.at[kind, i], (r, zf))
            for i, (v, zf) in enumerate(zip(views, peers))
        ]

    in_sent[0].start()
    out_sent[0].start()
    cot_out = exchange(cot_ref, cot_full, 0, 0, PARTS)
    for copy in cot_out:
        copy.start()

    @pl.when(jnp.logical_not(has_dn))
    def _():
        ext[0:row_blocks] = jnp.zeros((row_blocks, 128, quarter), BF16)

    @pl.when(jnp.logical_not(has_up))
    def _():
        ext[4 * row_blocks : 5 * row_blocks] = jnp.zeros((row_blocks, 128, quarter), BF16)

    @pl.when(r < 1)
    def _():
        ext[row_blocks : 2 * row_blocks] = jnp.zeros((row_blocks, 128, quarter), BF16)

    @pl.when(r + 1 >= n_row)
    def _():
        ext[3 * row_blocks : 4 * row_blocks] = jnp.zeros((row_blocks, 128, quarter), BF16)

    for copy in loads:
        copy.wait()

    def transpose_block(b, carry):
        for s in range(slots):
            vals_t[b, s] = vals[b, s].astype(F32).T.astype(BF16)
        return carry

    lax.fori_loop(0, row_blocks, transpose_block, 0)

    for b in range(row_blocks):
        for s in range(slots):
            col = jnp.broadcast_to(spread_ref[s : s + 1, b : b + 1], (16, 128))
            marks[b * slots + s] = jnp.where(col >= 0, col - first, -1)

    def fill_dense(t, carry):
        at = pl.ds(pl.multiple_of(t * 128, 128), 128)
        for b in range(row_blocks):
            turned = jnp.zeros((8, 16, 128), BF16)
            for s in range(slots):
                keep = jnp.where(marks[b * slots + s] == t, 1.0, 0.0).astype(BF16)[None]
                turned = turned + vals_t[b, s].reshape(8, 16, 128) * keep
            dense_t[at, b * 128 : (b + 1) * 128] = turned.reshape(128, 128)
        return carry

    out_got[0].wait_recv()
    out_sent[1].start()
    in_got[0].wait_recv()

    @pl.when(has_dn)
    def _():
        from_dn.wait_recv()

    @pl.when(has_up)
    def _():
        from_up.wait_recv()

    @pl.when(fwd_out)
    def _():
        f_fwd.start()

    in_sent[1].start()
    from_sib.wait_recv()

    @pl.when(fwd_in)
    def _():
        from_fwd.wait_recv()

    def gather(b):
        left, right = [], []
        for s in range(slots):
            col = cols_ref[s, b]
            absent = lax.shift_right_logical(col, 31)
            place = col - first + absent * (1 + first + 2 * row_blocks + b)
            keep = jnp.where(marks[b * slots + s] >= 0, 1.0, 0.0).astype(BF16)[None]
            left.append((vals[b, s].reshape(8, 16, 128) * keep).reshape(128, 128))
            right.append(ext[jnp.minimum(jnp.maximum(place, 0), 5 * row_blocks - 1)])
        res = dot(jnp.concatenate(left, axis=1), jnp.concatenate(right, axis=0))
        agg[b * 128 : (b + 1) * 128, :] = res.astype(BF16)

    agg_out = []
    per_part = part // 128
    for c in range(PARTS):
        for s in range(2):
            for i in range(per_part):
                gather((s * PARTS + c) * per_part + i)
        agg_out.append(exchange(agg, agg_full, 1 + c, c))
        if c == 0:
            for copy in agg_out[0]:
                copy.start()
    for c in range(PARTS):
        agg_full[z, pl.ds(c * part, part)] = agg[
            pl.ds(pl.multiple_of(z1 * half + c * part, part), part), :
        ]

    cut = 3 * row_blocks
    lax.fori_loop(0, cut, fill_dense, 0)
    in_got[1].wait_recv()
    in_sent[2].start()
    out_got[1].wait_recv()
    out_sent[2].start()
    for c in range(1, PARTS):
        for copy in agg_out[c - 1]:
            copy.wait_send()
        for copy in agg_out[c]:
            copy.start()
    lax.fori_loop(cut, 5 * row_blocks, fill_dense, 0)
    tile = 256

    def hidden_part(w_a, w_b, base, c):
        rs = pl.ds(c * part, part)

        def step(i, carry):
            hc = pl.ds(pl.multiple_of(i * tile, tile), tile)
            to = pl.ds(pl.multiple_of(base + i * tile, tile), tile)
            x = jnp.concatenate([agg_full[q, rs] for q in range(n_rep)], axis=1)
            g = jnp.concatenate([cot_full[q, rs] for q in range(n_rep)], axis=1)
            value, slope = gelu_pair(dot(x, w_a[:, hc]))
            hid[rs, to] = value.astype(BF16)
            gp[rs, to] = (dot(g, w_b[:, hc]) * slope).astype(BF16)
            return carry

        lax.fori_loop(0, hidw // tile, step, 0)

    def product(src, w_a, w_b, zq, c):
        at = pl.ds(pl.multiple_of(zq * quarter, quarter), quarter)
        rs = pl.ds(c * part, part)
        res = dot(src[rs, :hidw], w_a[at, :], ((1,), (1,)))
        res = res + dot(src[rs, hidw:], w_b[at, :], ((1,), (1,)))
        return res.astype(BF16)

    def adj_copies(f, c):
        kind = 1 + PARTS + f * PARTS + c
        rs = pl.ds(c * part, part)
        return [
            remote(
                adj_p.at[zp, f, rs], adj_in.at[z, f, rs],
                a_send.at[kind, i], a_recv.at[kind, i], (r, zp),
            )
            for i, zp in enumerate(peers)
        ]

    def adj_arrivals(f, c):
        kind = 1 + PARTS + f * PARTS + c
        views = [adj_in.at[zf, f, pl.ds(c * part, part)] for zf in peers]
        return [
            remote(v, v, a_send.at[kind, i], a_recv.at[kind, i], (r, zf))
            for i, (v, zf) in enumerate(zip(views, peers))
        ]

    for copy in arrivals(cot_full, 0, 0, PARTS):
        copy.wait_recv()
    adj_sent = [[adj_copies(f, c) for c in range(PARTS)] for f in range(WIDE)]
    for c in range(PARTS):
        for copy in arrivals(agg_full, 1 + c, c):
            copy.wait_recv()
        hidden_part(w1_in, w1_out, 0, c)
        if c == 0:
            in_got[2].wait_recv()
            in_sent[3].start()
            out_got[2].wait_recv()
            out_sent[3].start()
            in_got[3].wait_recv()
            out_got[3].wait_recv()
        hidden_part(w2_in, w2_out, hidw, c)
        rs = pl.ds(c * part, part)
        for i, zp in enumerate(peers + [z]):
            res = product(gp, w1_in, w2_in, zp, c)
            made = adj_p if i < n_rep - 1 else adj_in
            for f in range(WIDE):
                made[zp, f, rs] = res[:, f * width : (f + 1) * width]
            if i < n_rep - 1:
                adj_sent[0][c][i].start()

    out_sends = []
    for c in range(PARTS):
        rs = pl.ds(c * part, part)
        kind = 1 + (1 + WIDE) * PARTS + c
        for i, zp in enumerate(peers):
            out_p[zp, rs] = product(hid, w1_out, w2_out, zp, c)
            out_sends.append(
                remote(
                    out_p.at[zp, rs], out_in.at[z, rs],
                    a_send.at[kind, i], a_recv.at[kind, i], (r, zp),
                )
            )
        out_in[z, rs] = product(hid, w1_out, w2_out, z, c)

    tile = 256
    plain_to, helped_to = r - 2 + 4 * k, r + 2 - 4 * k
    plain_ok, helped_ok = fwd_in, fwd_out
    p5_sent = []

    def turn(f):
        for c in range(PARTS):
            for copy in adj_arrivals(f, c):
                copy.wait_recv()
        for s in range(2):
            total = adj_in[s, f].astype(F32)
            for q in range(s + 2, n_rep, 2):
                total = total + adj_in[q, f].astype(F32)
            adj[f, s * half : (s + 1) * half] = total.astype(BF16)

        def put(p, slot):
            def step(m, carry):
                at = pl.ds(pl.multiple_of(m * tile, tile), tile)
                c_send[4 * f + slot, at, :] = piece(f, p, m).astype(BF16)
                return carry

            lax.fori_loop(0, rows // tile, step, 0)

        def cross(slot, dst, got, dev):
            return remote(
                c_send.at[4 * f + slot], dst, c_sends.at[4 * f + slot], c_recvs.at[4 * f + got], dev
            )

        c_help = cross(0, c_sib.at[2 * f], 0, (sib, z))
        c_own = cross(1, c_sib.at[2 * f + 1], 1, (sib, z))
        c_plain = cross(2, c_nbr.at[2 * f + 1 - k], 3 - k, (plain_to, z))
        c_helped = cross(3, c_nbr.at[2 * f + k], 2 + k, (helped_to, z))
        put(1 + 2 * k, 0)
        c_help.start()
        put(4 * k, 2)

        @pl.when(plain_ok)
        def _():
            c_plain.start()

        c_help.wait_recv()

        def add_help(m, carry):
            at = pl.ds(pl.multiple_of(m * tile, tile), tile)
            total = piece(f, 4 - 4 * k, m) + c_sib[2 * f, at, :].astype(F32)
            c_send[4 * f + 3, at, :] = total.astype(BF16)
            return carry

        lax.fori_loop(0, rows // tile, add_help, 0)

        @pl.when(helped_ok)
        def _():
            c_helped.start()

        put(3 - 2 * k, 1)
        c_own.start()
        p5_sent.append((c_help, c_own, c_plain, c_helped))

    def piece(f, p, m):
        at = pl.ds(pl.multiple_of(p * rows + m * tile, tile), tile)
        return dot(dense_t[at, :], adj[f])

    def finish(f):
        p5_sent[f][1].wait_recv()
        from_low = remote(
            c_nbr.at[2 * f], c_nbr.at[2 * f], c_sends.at[4 * f + 2], c_recvs.at[4 * f + 2], (r - 2, z)
        )
        from_high = remote(
            c_nbr.at[2 * f + 1], c_nbr.at[2 * f + 1], c_sends.at[4 * f + 3], c_recvs.at[4 * f + 3],
            (r + 2, z),
        )

        @pl.when(has_dn)
        def _():
            from_low.wait_recv()

        @pl.when(jnp.logical_not(has_dn))
        def _():
            c_nbr[2 * f] = jnp.zeros((rows, width), BF16)

        @pl.when(has_up)
        def _():
            from_high.wait_recv()

        @pl.when(jnp.logical_not(has_up))
        def _():
            c_nbr[2 * f + 1] = jnp.zeros((rows, width), BF16)

        cs = slice(f * width, (f + 1) * width)

        def step(m, carry):
            at = pl.ds(pl.multiple_of(m * tile, tile), tile)
            total = piece(f, 2, m) + c_sib[2 * f + 1, at, :].astype(F32)
            total = total + c_nbr[2 * f, at, :].astype(F32) + c_nbr[2 * f + 1, at, :].astype(F32)
            grad_ref[at, cs] = (cot[at, cs].astype(F32) + total).astype(BF16)
            return carry

        lax.fori_loop(0, rows // tile, step, 0)

    for f in range(WIDE):
        for copies in adj_sent[f]:
            for copy in copies:
                copy.wait_send()
        following = sum(adj_sent[f + 1], []) if f + 1 < WIDE else out_sends
        for copy in following:
            copy.start()
        turn(f)
    for f in range(WIDE):
        finish(f)
    grad_out = pltpu.make_async_copy(grad_ref, grad_hbm, loc_sem.at[6])
    grad_out.start()
    for c in range(PARTS):
        for copy in arrivals(out_in, 1 + (1 + WIDE) * PARTS + c, c):
            copy.wait_recv()
        rs = pl.ds(c * part, part)
        for s in range(2):
            total = out_in[s, rs].astype(F32)
            for q in range(s + 2, n_rep, 2):
                total = total + out_in[q, rs].astype(F32)
            start, count = 2 * row_blocks + s * row_blocks // 2 + c * per_part, per_part
            mine = ext[start : start + count].reshape(part, quarter)
            at = pl.ds(s * half + c * part, part)
            upd_ref[at] = (mine.astype(F32) + total).astype(BF16)

    upd_out = pltpu.make_async_copy(upd_ref, upd_hbm, loc_sem.at[7])
    upd_out.start()
    for copy in cot_out + in_sent + out_sent + agg_out[-1] + out_sends + [f_sib]:
        copy.wait_send()
    late = [(has_up, f_up), (has_dn, f_dn), (fwd_out, f_fwd)]
    for c_help, c_own, c_plain, c_helped in p5_sent:
        c_help.wait_send()
        c_own.wait_send()
        late += [(plain_ok, c_plain), (helped_ok, c_helped)]
    for ok, copy in late:
        pl.when(ok)(copy.wait_send)
    grad_out.wait()
    upd_out.wait()


def settle(upd_ref, grad_ref, upd_out, grad_out, held, sems):
    size = upd_ref.shape[0] // CUTS
    steps = []
    for i in range(CUTS):
        rs = pl.ds(i * size, size)
        for j, (src, dst) in enumerate(((upd_ref, upd_out), (grad_ref, grad_out))):
            steps.append((
                pltpu.make_async_copy(src.at[rs], held.at[j, rs], sems.at[0, j, i]),
                pltpu.make_async_copy(held.at[j, rs], dst.at[rs], sems.at[1, j, i]),
            ))
    for load, _ in steps:
        load.start()
    for load, store in steps:
        load.wait()
        store.start()
    for _, store in steps:
        store.wait()


def body(n_row, n_rep, node_feats, block_cols, block_vals, w_in, w_out, cotangent):
    rows, quarter = cotangent.shape
    row_blocks, slots = block_cols.shape
    feat, hidw = w_in.shape
    half = rows // 2
    kinds = 1 + (2 + WIDE) * PARTS
    width = quarter // WIDE
    vmem = pl.BlockSpec(memory_space=pltpu.VMEM)
    anywhere = pl.BlockSpec(memory_space=pl.ANY)
    dma = pltpu.SemaphoreType.DMA
    made = pl.pallas_call(
        functools.partial(kernel, n_row, n_rep),
        out_shape=(jax.ShapeDtypeStruct((rows, quarter), BF16),) * 2,
        in_specs=[pl.BlockSpec(memory_space=pltpu.SMEM), vmem] + [anywhere] * 5,
        out_specs=(anywhere, anywhere),
        scratch_shapes=[
            pltpu.VMEM((rows, quarter), BF16),
            pltpu.VMEM((rows, quarter), BF16),
            pltpu.VMEM((5 * row_blocks, 128, quarter), BF16),
            pltpu.VMEM((row_blocks * slots, 16, 128), jnp.int32),
            pltpu.VMEM((row_blocks, slots, 128, 128), BF16),
            pltpu.VMEM((row_blocks, slots, 128, 128), BF16),
            pltpu.VMEM((5 * rows, rows), BF16),
            pltpu.VMEM((feat, hidw), BF16),
            pltpu.VMEM((feat, hidw), BF16),
            pltpu.VMEM((feat, hidw), BF16),
            pltpu.VMEM((feat, hidw), BF16),
            pltpu.VMEM((rows, quarter), BF16),
            pltpu.VMEM((n_rep, half, quarter), BF16),
            pltpu.VMEM((rows, quarter), BF16),
            pltpu.VMEM((n_rep, half, quarter), BF16),
            pltpu.VMEM((half, 2 * hidw), BF16),
            pltpu.VMEM((half, 2 * hidw), BF16),
            pltpu.VMEM((n_rep, WIDE, half, width), BF16),
            pltpu.VMEM((n_rep, half, quarter), BF16),
            pltpu.VMEM((n_rep, WIDE, half, width), BF16),
            pltpu.VMEM((n_rep, half, quarter), BF16),
            pltpu.VMEM((WIDE, rows, width), BF16),
            pltpu.VMEM((4 * WIDE, rows, width), BF16),
            pltpu.VMEM((2 * WIDE, rows, width), BF16),
            pltpu.VMEM((2 * WIDE, rows, width), BF16),
            dma((8,)),
            dma((4,)),
            dma((4,)),
            dma((8,)),
            dma((8,)),
            dma((kinds, n_rep - 1)),
            dma((kinds, n_rep - 1)),
            dma((4 * WIDE,)),
            dma((4 * WIDE,)),
        ],
        compiler_params=pltpu.CompilerParams(
            collective_id=0, has_side_effects=True, vmem_limit_bytes=60 * 1024 * 1024
        ),
    )(block_cols.T, block_cols.T, node_feats.reshape(row_blocks, 128, feat), block_vals, w_in, w_out, cotangent)
    return pl.pallas_call(
        settle,
        out_shape=(jax.ShapeDtypeStruct((rows, quarter), BF16),) * 2,
        in_specs=[anywhere] * 2,
        out_specs=(anywhere,) * 2,
        scratch_shapes=[pltpu.VMEM((2, rows, quarter), BF16), dma((2, 2, CUTS))],
    )(*made)


def solution(mesh):
    in_specs = (
        P("row", None),
        P("row", None),
        P("row", None, None, None),
        P(None, "rep"),
        P(None, "rep"),
        P("row", "rep"),
    )
    out_specs = (P("row", "rep"), P("row", "rep"))
    run = functools.partial(body, mesh.shape["row"], mesh.shape["rep"])
    return jax.shard_map(run, mesh=mesh, in_specs=in_specs, out_specs=out_specs, check_vma=False)
```

```python
import functools

import jax
import jax.numpy as jnp
from jax import lax
from jax.experimental import pallas as pl
from jax.experimental.pallas import tpu as pltpu
from jax.sharding import PartitionSpec as P

F32 = jnp.float32
BF16 = jnp.bfloat16
MESH = pl.DeviceIdType.MESH
PARTS = 2
WIDE = 2
CUTS = 4


def dot(a, b, dims=((1,), (0,))):
    return lax.dot_general(a, b, (dims, ((), ())), preferred_element_type=F32)


def gelu_pair(v):
    c = 0.7978845608
    vv = v * v
    t = jnp.tanh(c * (v + 0.044715 * v * vv))
    half = 0.5 * (1.0 + t)
    value = v * half
    slope = half + 0.5 * v * (1.0 - t * t) * c * (1.0 + 3.0 * 0.044715 * vv)
    return value, slope


def kernel(
    n_row, n_rep, cols_ref, spread_ref, feats_ref, vals_ref, w_in_ref, w_out_ref, cot_ref,
    upd_hbm, grad_hbm,
    upd_ref, grad_ref, ext, marks, vals, vals_t, dense_t, w1_in, w1_out, w2_in, w2_out, cot, cot_full, agg, agg_full, hid, gp,
    adj_p, out_p, adj_in, out_in, adj, c_send, c_sib, c_nbr, f_relay, c_relay,
    loc_sem, f_send, f_recv, w_send, w_recv, a_send, a_recv, c_sends, c_recvs, b_sends, b_recvs,
):
    r, z = lax.axis_index("row"), lax.axis_index("rep")
    k = lax.rem(r, 2)
    sib = r + 1 - 2 * k
    z1, z2 = lax.rem(z, 2), lax.div(z, 2)
    mate = z + 1 - 2 * z1
    peers = [z + 2 - 4 * z2, n_rep - 1 - z, mate]
    bit2, bit4 = lax.rem(lax.div(r, 2), 2), lax.rem(lax.div(r, 4), 2)
    near, far = r + 2 - 4 * bit2, r + 4 - 8 * bit4
    rows, quarter = cot.shape
    half = rows // 2
    part = half // PARTS
    width = quarter // WIDE
    slots, row_blocks = cols_ref.shape
    feat, hidw = w1_in.shape
    has_up, has_dn = r + 2 < n_row, r >= 2
    turning, passing = bit2 != bit4, bit2 == bit4
    turn_up, turn_dn = jnp.logical_and(turning, bit2 == 1), jnp.logical_and(turning, bit2 == 0)
    straight_up = jnp.logical_and(has_up, jnp.logical_not(turn_up))
    straight_dn = jnp.logical_and(has_dn, jnp.logical_not(turn_dn))
    hb = row_blocks // 2
    first = (r - 2) * row_blocks

    def remote(src, dst, send, recv, dev):
        return pltpu.make_async_remote_copy(
            src_ref=src, dst_ref=dst, send_sem=send, recv_sem=recv, device_id=dev, device_id_type=MESH
        )

    def panel(ref, slot):
        return ref.at[pl.ds(slot * row_blocks, row_blocks)]

    def half_part(ref, s, c, count=1):
        start = pl.multiple_of(s * half + c * part, part)
        return ref.at[pl.ds(start, count * part)]

    barrier = pltpu.get_barrier_semaphore()
    for zp in peers:
        pl.semaphore_signal(barrier, inc=1, device_id=(r, zp), device_id_type=MESH)
    pl.semaphore_signal(barrier, inc=1, device_id=(sib, z), device_id_type=MESH)
    pl.semaphore_signal(barrier, inc=1, device_id=(far, z), device_id_type=MESH)

    @pl.when(has_up)
    def _():
        pl.semaphore_signal(barrier, inc=1, device_id=(r + 2, z), device_id_type=MESH)

    @pl.when(has_dn)
    def _():
        pl.semaphore_signal(barrier, inc=1, device_id=(r - 2, z), device_id_type=MESH)

    columns = pl.ds(pl.multiple_of(z * quarter, quarter), quarter)
    own_copy = pltpu.make_async_copy(feats_ref.at[:, :, columns], panel(ext, 2), loc_sem.at[0])
    loads = [
        pltpu.make_async_copy(src, dst, loc_sem.at[1 + i])
        for i, (src, dst) in enumerate(
            (
                (vals_ref, vals),
                (half_part(cot_ref, z1, 0, PARTS), cot_full.at[z]),
                (w_in_ref, w1_in),
                (w_out_ref, w1_out),
                (cot_ref, cot),
            )
        )
    ]
    own_copy.start()
    for copy in loads:
        copy.start()
    own_copy.wait()
    pl.semaphore_wait(barrier, n_rep + 1 + has_up.astype(jnp.int32) + has_dn.astype(jnp.int32))

    own = panel(ext, 2)

    def some(slot, h):
        return ext.at[pl.ds(slot * row_blocks + h * hb, hb)]

    f_up = remote(some(2, 0), some(0, 0), f_send.at[0], f_recv.at[0], (r + 2, z))
    f_dn = remote(some(2, 0), some(4, 0), f_send.at[1], f_recv.at[1], (r - 2, z))
    f_up2 = remote(some(2, 1), some(0, 1), f_send.at[4], f_recv.at[4], (r + 2, z))
    f_dn2 = remote(some(2, 1), some(4, 1), f_send.at[5], f_recv.at[5], (r - 2, z))
    f_out = remote(some(2, 1), f_relay, f_send.at[6], f_recv.at[6], (far, z))
    f_on = remote(f_relay, some(4 - 4 * bit2, 1), f_send.at[7], f_recv.at[5 - bit2], (near, z))
    f_sib = remote(own, panel(ext, 1 + 2 * k), f_send.at[2], f_recv.at[2], (sib, z))
    f_fwd = remote(
        panel(ext, 4 - 4 * k), panel(ext, 3 - 2 * k), f_send.at[3], f_recv.at[3], (sib, z)
    )
    from_dn = [
        remote(some(0, h), some(0, h), f_send.at[4 * h], f_recv.at[4 * h], (r - 2, z))
        for h in range(2)
    ]
    from_up = [
        remote(some(4, h), some(4, h), f_send.at[4 * h + 1], f_recv.at[4 * h + 1], (r + 2, z))
        for h in range(2)
    ]
    from_sib = remote(own, panel(ext, 3 - 2 * k), f_send.at[2], f_recv.at[2], (sib, z))
    from_fwd = remote(own, panel(ext, 1 + 2 * k), f_send.at[3], f_recv.at[3], (sib, z))
    fwd_out = jnp.where(k == 0, r + 2 < n_row, r >= 2)
    fwd_in = jnp.where(k == 0, r >= 2, r + 2 < n_row)

    starts = (
        (turning, f_out), (has_up, f_up), (has_dn, f_dn), (straight_up, f_up2), (straight_dn, f_dn2)
    )
    for ok, copy in starts:
        pl.when(ok)(copy.start)
    f_sib.start()

    eighth = feat // 8

    def span(ref, start, count):
        return ref.at[pl.ds(pl.multiple_of(start * eighth, eighth), count * eighth)]

    def rounds(raw, full, base, bit_a, dev_a, bit_b, dev_b):
        mine = 4 * k + 2 * bit_b + bit_a
        plan = (
            (raw, mine, mine, 1, (r, mate)),
            (full, mine, mine + 1 - 2 * bit_a, 1, (dev_a, z)),
            (full, 4 * k + 2 * bit_b, 4 * k + 2 - 2 * bit_b, 2, (dev_b, z)),
            (full, 4 * k, 4 - 4 * k, 4, (sib, z)),
        )
        sent, got = [], []
        for i, (src, lo, there, count, dev) in enumerate(plan):
            sems = (w_send.at[base + i], w_recv.at[base + i])
            sent.append(remote(span(src, lo, count), span(full, lo, count), *sems, dev))
            got.append(remote(span(full, there, count), span(full, there, count), *sems, dev))
        return sent, got

    in_sent, in_got = rounds(w_in_ref, w2_in, 0, bit2, near, bit4, far)
    out_sent, out_got = rounds(w_out_ref, w2_out, 4, bit4, far, bit2, near)

    def exchange(src, dst, kind, c, count=1):
        return [
            remote(
                half_part(src, lax.rem(zp, 2), c, count),
                dst.at[z, pl.ds(c * part, count * part)],
                a_send.at[kind, i], a_recv.at[kind, i], (r, zp),
            )
            for i, zp in enumerate(peers)
        ]

    def arrivals(buf, kind, c, count=1):
        views = [buf.at[zf, pl.ds(c * part, count * part)] for zf in peers]
        return [
            remote(v, v, a_send.at[kind, i], a_recv.at[kind, i], (r, zf))
            for i, (v, zf) in enumerate(zip(views, peers))
        ]

    in_sent[0].start()
    out_sent[0].start()
    cot_out = exchange(cot_ref, cot_full, 0, 0, PARTS)
    for copy in cot_out:
        copy.start()

    @pl.when(jnp.logical_not(has_dn))
    def _():
        ext[0:row_blocks] = jnp.zeros((row_blocks, 128, quarter), BF16)

    @pl.when(jnp.logical_not(has_up))
    def _():
        ext[4 * row_blocks : 5 * row_blocks] = jnp.zeros((row_blocks, 128, quarter), BF16)

    @pl.when(r < 1)
    def _():
        ext[row_blocks : 2 * row_blocks] = jnp.zeros((row_blocks, 128, quarter), BF16)

    @pl.when(r + 1 >= n_row)
    def _():
        ext[3 * row_blocks : 4 * row_blocks] = jnp.zeros((row_blocks, 128, quarter), BF16)

    for copy in loads:
        copy.wait()

    def transpose_block(b, carry):
        for s in range(slots):
            vals_t[b, s] = vals[b, s].astype(F32).T.astype(BF16)
        return carry

    lax.fori_loop(0, row_blocks, transpose_block, 0)

    for b in range(row_blocks):
        for s in range(slots):
            col = jnp.broadcast_to(spread_ref[s : s + 1, b : b + 1], (16, 128))
            marks[b * slots + s] = jnp.where(col >= 0, col - first, -1)

    def fill_dense(t, carry):
        at = pl.ds(pl.multiple_of(t * 128, 128), 128)
        for b in range(row_blocks):
            turned = jnp.zeros((8, 16, 128), BF16)
            for s in range(slots):
                keep = jnp.where(marks[b * slots + s] == t, 1.0, 0.0).astype(BF16)[None]
                turned = turned + vals_t[b, s].reshape(8, 16, 128) * keep
            dense_t[at, b * 128 : (b + 1) * 128] = turned.reshape(128, 128)
        return carry

    @pl.when(passing)
    def _():
        f_out.wait_recv()
        f_on.start()

    @pl.when(has_dn)
    def _():
        for copy in from_dn:
            copy.wait_recv()

    @pl.when(has_up)
    def _():
        for copy in from_up:
            copy.wait_recv()

    @pl.when(fwd_out)
    def _():
        f_fwd.start()

    from_sib.wait_recv()

    @pl.when(fwd_in)
    def _():
        from_fwd.wait_recv()

    def gather(b):
        left, right = [], []
        for s in range(slots):
            col = cols_ref[s, b]
            absent = lax.shift_right_logical(col, 31)
            place = col - first + absent * (1 + first + 2 * row_blocks + b)
            keep = jnp.where(marks[b * slots + s] >= 0, 1.0, 0.0).astype(BF16)[None]
            left.append((vals[b, s].reshape(8, 16, 128) * keep).reshape(128, 128))
            right.append(ext[jnp.minimum(jnp.maximum(place, 0), 5 * row_blocks - 1)])
        res = dot(jnp.concatenate(left, axis=1), jnp.concatenate(right, axis=0))
        agg[b * 128 : (b + 1) * 128, :] = res.astype(BF16)

    agg_out = []
    per_part = part // 128
    for c in range(PARTS):
        for s in range(2):
            for i in range(per_part):
                gather((s * PARTS + c) * per_part + i)
        agg_out.append(exchange(agg, agg_full, 1 + c, c))
        if c == 0:
            for copy in agg_out[0]:
                copy.start()
    for c in range(PARTS):
        agg_full[z, pl.ds(c * part, part)] = agg[
            pl.ds(pl.multiple_of(z1 * half + c * part, part), part), :
        ]

    out_got[0].wait_recv()
    out_sent[1].start()
    in_got[0].wait_recv()
    in_sent[1].start()
    cut = 3 * row_blocks
    lax.fori_loop(0, cut, fill_dense, 0)
    in_got[1].wait_recv()
    in_sent[2].start()
    out_got[1].wait_recv()
    out_sent[2].start()
    for c in range(1, PARTS):
        for copy in agg_out[c - 1]:
            copy.wait_send()
        for copy in agg_out[c]:
            copy.start()
    lax.fori_loop(cut, 5 * row_blocks, fill_dense, 0)
    tile = 256

    def hidden_part(w_a, w_b, base, c):
        rs = pl.ds(c * part, part)

        def step(i, carry):
            hc = pl.ds(pl.multiple_of(i * tile, tile), tile)
            to = pl.ds(pl.multiple_of(base + i * tile, tile), tile)
            x = jnp.concatenate([agg_full[q, rs] for q in range(n_rep)], axis=1)
            g = jnp.concatenate([cot_full[q, rs] for q in range(n_rep)], axis=1)
            value, slope = gelu_pair(dot(x, w_a[:, hc]))
            hid[rs, to] = value.astype(BF16)
            gp[rs, to] = (dot(g, w_b[:, hc]) * slope).astype(BF16)
            return carry

        lax.fori_loop(0, hidw // tile, step, 0)

    def product(src, w_a, w_b, zq, c):
        at = pl.ds(pl.multiple_of(zq * quarter, quarter), quarter)
        rs = pl.ds(c * part, part)
        res = dot(src[rs, :hidw], w_a[at, :], ((1,), (1,)))
        res = res + dot(src[rs, hidw:], w_b[at, :], ((1,), (1,)))
        return res.astype(BF16)

    def adj_copies(f, c):
        kind = 1 + PARTS + f * PARTS + c
        rs = pl.ds(c * part, part)
        return [
            remote(
                adj_p.at[zp, f, rs], adj_in.at[z, f, rs],
                a_send.at[kind, i], a_recv.at[kind, i], (r, zp),
            )
            for i, zp in enumerate(peers)
        ]

    def adj_arrivals(f, c):
        kind = 1 + PARTS + f * PARTS + c
        views = [adj_in.at[zf, f, pl.ds(c * part, part)] for zf in peers]
        return [
            remote(v, v, a_send.at[kind, i], a_recv.at[kind, i], (r, zf))
            for i, (v, zf) in enumerate(zip(views, peers))
        ]

    for copy in arrivals(cot_full, 0, 0, PARTS):
        copy.wait_recv()
    adj_sent = [[adj_copies(f, c) for c in range(PARTS)] for f in range(WIDE)]
    for c in range(PARTS):
        for copy in arrivals(agg_full, 1 + c, c):
            copy.wait_recv()
        hidden_part(w1_in, w1_out, 0, c)
        if c == 0:
            in_got[2].wait_recv()
            in_sent[3].start()
            out_got[2].wait_recv()
            out_sent[3].start()
            in_got[3].wait_recv()
            out_got[3].wait_recv()
        hidden_part(w2_in, w2_out, hidw, c)
        rs = pl.ds(c * part, part)
        for i, zp in enumerate(peers + [z]):
            res = product(gp, w1_in, w2_in, zp, c)
            made = adj_p if i < n_rep - 1 else adj_in
            for f in range(WIDE):
                made[zp, f, rs] = res[:, f * width : (f + 1) * width]
            if i < n_rep - 1:
                adj_sent[0][c][i].start()

    out_sends = []
    for c in range(PARTS):
        rs = pl.ds(c * part, part)
        kind = 1 + (1 + WIDE) * PARTS + c
        for i, zp in enumerate(peers):
            out_p[zp, rs] = product(hid, w1_out, w2_out, zp, c)
            out_sends.append(
                remote(
                    out_p.at[zp, rs], out_in.at[z, rs],
                    a_send.at[kind, i], a_recv.at[kind, i], (r, zp),
                )
            )
        out_in[z, rs] = product(hid, w1_out, w2_out, z, c)

    tile = 256
    plain_to, helped_to = r - 2 + 4 * k, r + 2 - 4 * k
    plain_ok, helped_ok = fwd_in, fwd_out
    turn_plain = jnp.logical_and(turning, k == bit2)
    turn_helped = jnp.logical_and(turning, k != bit2)
    p5_sent = []

    def turn(f):
        for c in range(PARTS):
            for copy in adj_arrivals(f, c):
                copy.wait_recv()
        for s in range(2):
            total = adj_in[s, f].astype(F32)
            for q in range(s + 2, n_rep, 2):
                total = total + adj_in[q, f].astype(F32)
            adj[f, s * half : (s + 1) * half] = total.astype(BF16)

        def put(p, slot):
            def step(m, carry):
                at = pl.ds(pl.multiple_of(m * tile, tile), tile)
                c_send[4 * f + slot, at, :] = piece(f, p, m).astype(BF16)
                return carry

            lax.fori_loop(0, rows // tile, step, 0)

        def cross(slot, dst, got, dev):
            return remote(
                c_send.at[4 * f + slot], dst, c_sends.at[4 * f + slot], c_recvs.at[4 * f + got], dev
            )

        c_help = cross(0, c_sib.at[2 * f], 0, (sib, z))
        c_own = cross(1, c_sib.at[2 * f + 1], 1, (sib, z))
        top, low = pl.ds(0, rows // 2), pl.ds(rows // 2, rows // 2)

        def sides(slot, nbr, dev):
            return (
                remote(
                    c_send.at[4 * f + slot, top], c_nbr.at[2 * f + nbr, top],
                    c_sends.at[4 * f + slot], c_recvs.at[4 * f + 2 + nbr], dev,
                ),
                remote(
                    c_send.at[4 * f + slot, low], c_nbr.at[2 * f + nbr, low],
                    b_sends.at[4 * f + slot], b_recvs.at[4 * f + 2 + nbr], dev,
                ),
            )

        c_plain = sides(2, 1 - k, (plain_to, z))
        c_helped = sides(3, k, (helped_to, z))
        c_out = remote(
            c_send.at[4 * f + jnp.where(k == bit2, 2, 3), low], c_relay.at[f],
            b_sends.at[4 * f], b_recvs.at[4 * f], (far, z),
        )
        c_on = remote(
            c_relay.at[f], c_nbr.at[2 * f + 1 - bit2, low],
            b_sends.at[4 * f + 1], b_recvs.at[4 * f + 3 - bit2], (near, z),
        )
        moves = (
            (plain_ok, c_plain[0]), (jnp.logical_and(plain_ok, jnp.logical_not(turn_plain)), c_plain[1]),
            (helped_ok, c_helped[0]),
            (jnp.logical_and(helped_ok, jnp.logical_not(turn_helped)), c_helped[1]),
            (turning, c_out), (passing, c_on),
        )
        put(1 + 2 * k, 0)
        c_help.start()
        put(4 * k, 2)

        pl.when(turn_plain)(c_out.start)
        for ok, copy in moves[:2]:
            pl.when(ok)(copy.start)
        c_help.wait_recv()

        def add_help(m, carry):
            at = pl.ds(pl.multiple_of(m * tile, tile), tile)
            total = piece(f, 4 - 4 * k, m) + c_sib[2 * f, at, :].astype(F32)
            c_send[4 * f + 3, at, :] = total.astype(BF16)
            return carry

        lax.fori_loop(0, rows // tile, add_help, 0)

        pl.when(turn_helped)(c_out.start)
        for ok, copy in moves[2:4]:
            pl.when(ok)(copy.start)
        put(3 - 2 * k, 1)
        c_own.start()

        @pl.when(passing)
        def _():
            c_out.wait_recv()
            c_on.start()

        p5_sent.append((c_help, c_own, moves))

    def piece(f, p, m):
        at = pl.ds(pl.multiple_of(p * rows + m * tile, tile), tile)
        return dot(dense_t[at, :], adj[f])

    def finish(f):
        p5_sent[f][1].wait_recv()

        def landed(nbr, dev):
            for h, sems in enumerate((c_recvs, b_recvs)):
                ref = c_nbr.at[2 * f + nbr, pl.ds(h * (rows // 2), rows // 2)]
                remote(ref, ref, c_sends.at[4 * f + 2], sems.at[4 * f + 2 + nbr], (dev, z)).wait_recv()

        @pl.when(has_dn)
        def _():
            landed(0, r - 2)

        @pl.when(jnp.logical_not(has_dn))
        def _():
            c_nbr[2 * f] = jnp.zeros((rows, width), BF16)

        @pl.when(has_up)
        def _():
            landed(1, r + 2)

        @pl.when(jnp.logical_not(has_up))
        def _():
            c_nbr[2 * f + 1] = jnp.zeros((rows, width), BF16)

        cs = slice(f * width, (f + 1) * width)

        def step(m, carry):
            at = pl.ds(pl.multiple_of(m * tile, tile), tile)
            total = piece(f, 2, m) + c_sib[2 * f + 1, at, :].astype(F32)
            total = total + c_nbr[2 * f, at, :].astype(F32) + c_nbr[2 * f + 1, at, :].astype(F32)
            grad_ref[at, cs] = (cot[at, cs].astype(F32) + total).astype(BF16)
            return carry

        lax.fori_loop(0, rows // tile, step, 0)

    for f in range(WIDE):
        for copies in adj_sent[f]:
            for copy in copies:
                copy.wait_send()
        following = sum(adj_sent[f + 1], []) if f + 1 < WIDE else out_sends
        for copy in following:
            copy.start()
        turn(f)
    for f in range(WIDE):
        finish(f)
    grad_out = pltpu.make_async_copy(grad_ref, grad_hbm, loc_sem.at[6])
    grad_out.start()
    for c in range(PARTS):
        for copy in arrivals(out_in, 1 + (1 + WIDE) * PARTS + c, c):
            copy.wait_recv()
        rs = pl.ds(c * part, part)
        for s in range(2):
            total = out_in[s, rs].astype(F32)
            for q in range(s + 2, n_rep, 2):
                total = total + out_in[q, rs].astype(F32)
            start, count = 2 * row_blocks + s * row_blocks // 2 + c * per_part, per_part
            mine = ext[start : start + count].reshape(part, quarter)
            at = pl.ds(s * half + c * part, part)
            upd_ref[at] = (mine.astype(F32) + total).astype(BF16)

    upd_out = pltpu.make_async_copy(upd_ref, upd_hbm, loc_sem.at[7])
    upd_out.start()
    for copy in cot_out + in_sent + out_sent + agg_out[-1] + out_sends + [f_sib]:
        copy.wait_send()
    late = list(starts) + [(fwd_out, f_fwd), (passing, f_on)]
    for c_help, c_own, moves in p5_sent:
        c_help.wait_send()
        c_own.wait_send()
        late += list(moves)
    for ok, copy in late:
        pl.when(ok)(copy.wait_send)
    grad_out.wait()
    upd_out.wait()


def settle(upd_ref, grad_ref, upd_out, grad_out, held, sems):
    size = upd_ref.shape[0] // CUTS
    steps = []
    for i in range(CUTS):
        rs = pl.ds(i * size, size)
        for j, (src, dst) in enumerate(((upd_ref, upd_out), (grad_ref, grad_out))):
            steps.append((
                pltpu.make_async_copy(src.at[rs], held.at[j, rs], sems.at[0, j, i]),
                pltpu.make_async_copy(held.at[j, rs], dst.at[rs], sems.at[1, j, i]),
            ))
    for load, _ in steps:
        load.start()
    for load, store in steps:
        load.wait()
        store.start()
    for _, store in steps:
        store.wait()


def body(n_row, n_rep, node_feats, block_cols, block_vals, w_in, w_out, cotangent):
    rows, quarter = cotangent.shape
    row_blocks, slots = block_cols.shape
    feat, hidw = w_in.shape
    half = rows // 2
    kinds = 1 + (2 + WIDE) * PARTS
    width = quarter // WIDE
    vmem = pl.BlockSpec(memory_space=pltpu.VMEM)
    anywhere = pl.BlockSpec(memory_space=pl.ANY)
    dma = pltpu.SemaphoreType.DMA
    made = pl.pallas_call(
        functools.partial(kernel, n_row, n_rep),
        out_shape=(jax.ShapeDtypeStruct((rows, quarter), BF16),) * 2,
        in_specs=[pl.BlockSpec(memory_space=pltpu.SMEM), vmem] + [anywhere] * 5,
        out_specs=(anywhere, anywhere),
        scratch_shapes=[
            pltpu.VMEM((rows, quarter), BF16),
            pltpu.VMEM((rows, quarter), BF16),
            pltpu.VMEM((5 * row_blocks, 128, quarter), BF16),
            pltpu.VMEM((row_blocks * slots, 16, 128), jnp.int32),
            pltpu.VMEM((row_blocks, slots, 128, 128), BF16),
            pltpu.VMEM((row_blocks, slots, 128, 128), BF16),
            pltpu.VMEM((5 * rows, rows), BF16),
            pltpu.VMEM((feat, hidw), BF16),
            pltpu.VMEM((feat, hidw), BF16),
            pltpu.VMEM((feat, hidw), BF16),
            pltpu.VMEM((feat, hidw), BF16),
            pltpu.VMEM((rows, quarter), BF16),
            pltpu.VMEM((n_rep, half, quarter), BF16),
            pltpu.VMEM((rows, quarter), BF16),
            pltpu.VMEM((n_rep, half, quarter), BF16),
            pltpu.VMEM((half, 2 * hidw), BF16),
            pltpu.VMEM((half, 2 * hidw), BF16),
            pltpu.VMEM((n_rep, WIDE, half, width), BF16),
            pltpu.VMEM((n_rep, half, quarter), BF16),
            pltpu.VMEM((n_rep, WIDE, half, width), BF16),
            pltpu.VMEM((n_rep, half, quarter), BF16),
            pltpu.VMEM((WIDE, rows, width), BF16),
            pltpu.VMEM((4 * WIDE, rows, width), BF16),
            pltpu.VMEM((2 * WIDE, rows, width), BF16),
            pltpu.VMEM((2 * WIDE, rows, width), BF16),
            pltpu.VMEM((row_blocks // 2, 128, quarter), BF16),
            pltpu.VMEM((WIDE, rows // 2, width), BF16),
            dma((8,)),
            dma((8,)),
            dma((8,)),
            dma((8,)),
            dma((8,)),
            dma((kinds, n_rep - 1)),
            dma((kinds, n_rep - 1)),
            dma((4 * WIDE,)),
            dma((4 * WIDE,)),
            dma((4 * WIDE,)),
            dma((4 * WIDE,)),
        ],
        compiler_params=pltpu.CompilerParams(
            collective_id=0, has_side_effects=True, vmem_limit_bytes=60 * 1024 * 1024
        ),
    )(block_cols.T, block_cols.T, node_feats.reshape(row_blocks, 128, feat), block_vals, w_in, w_out, cotangent)
    return pl.pallas_call(
        settle,
        out_shape=(jax.ShapeDtypeStruct((rows, quarter), BF16),) * 2,
        in_specs=[anywhere] * 2,
        out_specs=(anywhere,) * 2,
        scratch_shapes=[pltpu.VMEM((2, rows, quarter), BF16), dma((2, 2, CUTS))],
    )(*made)


def solution(mesh):
    in_specs = (
        P("row", None),
        P("row", None),
        P("row", None, None, None),
        P(None, "rep"),
        P(None, "rep"),
        P("row", "rep"),
    )
    out_specs = (P("row", "rep"), P("row", "rep"))
    run = functools.partial(body, mesh.shape["row"], mesh.shape["rep"])
    return jax.shard_map(run, mesh=mesh, in_specs=in_specs, out_specs=out_specs, check_vma=False)
```

```python
import functools

import jax
import jax.numpy as jnp
from jax import lax
from jax.experimental import pallas as pl
from jax.experimental.pallas import tpu as pltpu
from jax.sharding import PartitionSpec as P

F32 = jnp.float32
BF16 = jnp.bfloat16
MESH = pl.DeviceIdType.MESH
PARTS = 2
WIDE = 2
CUTS = 4


def dot(a, b, dims=((1,), (0,))):
    return lax.dot_general(a, b, (dims, ((), ())), preferred_element_type=F32)


def gelu_pair(v):
    c = 0.7978845608
    vv = v * v
    t = jnp.tanh(c * (v + 0.044715 * v * vv))
    half = 0.5 * (1.0 + t)
    value = v * half
    slope = half + 0.5 * v * (1.0 - t * t) * c * (1.0 + 3.0 * 0.044715 * vv)
    return value, slope


def kernel(
    n_row, n_rep, cols_ref, spread_ref, feats_ref, vals_ref, w_in_ref, w_out_ref, cot_ref,
    upd_hbm, grad_hbm,
    upd_ref, grad_ref, ext, marks, vals, vals_t, dense_t, w1_in, w1_out, w2_in, w2_out, cot, cot_full, agg, agg_full, hid, gp,
    adj_p, out_p, adj_in, out_in, adj, c_send, c_sib, c_nbr, f_relay, c_relay,
    loc_sem, f_send, f_recv, w_send, w_recv, a_send, a_recv, c_sends, c_recvs, b_sends, b_recvs,
):
    r, z = lax.axis_index("row"), lax.axis_index("rep")
    k = lax.rem(r, 2)
    sib = r + 1 - 2 * k
    z1, z2 = lax.rem(z, 2), lax.div(z, 2)
    mate = z + 1 - 2 * z1
    peers = [z + 2 - 4 * z2, n_rep - 1 - z, mate]
    bit2, bit4 = lax.rem(lax.div(r, 2), 2), lax.rem(lax.div(r, 4), 2)
    near, far = r + 2 - 4 * bit2, r + 4 - 8 * bit4
    rows, quarter = cot.shape
    half = rows // 2
    part = half // PARTS
    width = quarter // WIDE
    slots, row_blocks = cols_ref.shape
    feat, hidw = w1_in.shape
    has_up, has_dn = r + 2 < n_row, r >= 2
    turning, passing = bit2 != bit4, bit2 == bit4
    turn_up, turn_dn = jnp.logical_and(turning, bit2 == 1), jnp.logical_and(turning, bit2 == 0)
    straight_up = jnp.logical_and(has_up, jnp.logical_not(turn_up))
    straight_dn = jnp.logical_and(has_dn, jnp.logical_not(turn_dn))
    hb = row_blocks // 2
    first = (r - 2) * row_blocks

    def remote(src, dst, send, recv, dev):
        return pltpu.make_async_remote_copy(
            src_ref=src, dst_ref=dst, send_sem=send, recv_sem=recv, device_id=dev, device_id_type=MESH
        )

    def panel(ref, slot):
        return ref.at[pl.ds(slot * row_blocks, row_blocks)]

    def half_part(ref, s, c, count=1):
        start = pl.multiple_of(s * half + c * part, part)
        return ref.at[pl.ds(start, count * part)]

    barrier = pltpu.get_barrier_semaphore()
    for zp in peers:
        pl.semaphore_signal(barrier, inc=1, device_id=(r, zp), device_id_type=MESH)
    pl.semaphore_signal(barrier, inc=1, device_id=(sib, z), device_id_type=MESH)
    pl.semaphore_signal(barrier, inc=1, device_id=(far, z), device_id_type=MESH)

    @pl.when(has_up)
    def _():
        pl.semaphore_signal(barrier, inc=1, device_id=(r + 2, z), device_id_type=MESH)

    @pl.when(has_dn)
    def _():
        pl.semaphore_signal(barrier, inc=1, device_id=(r - 2, z), device_id_type=MESH)

    columns = pl.ds(pl.multiple_of(z * quarter, quarter), quarter)
    own_copy = pltpu.make_async_copy(feats_ref.at[:, :, columns], panel(ext, 2), loc_sem.at[0])
    loads = [
        pltpu.make_async_copy(src, dst, loc_sem.at[1 + i])
        for i, (src, dst) in enumerate(
            (
                (vals_ref, vals),
                (half_part(cot_ref, z1, 0, PARTS), cot_full.at[z]),
                (w_in_ref, w1_in),
                (w_out_ref, w1_out),
                (cot_ref, cot),
            )
        )
    ]
    own_copy.start()
    for copy in loads:
        copy.start()
    own_copy.wait()
    pl.semaphore_wait(barrier, n_rep + 1 + has_up.astype(jnp.int32) + has_dn.astype(jnp.int32))

    own = panel(ext, 2)

    def some(slot, h):
        return ext.at[pl.ds(slot * row_blocks + h * hb, hb)]

    f_up = remote(some(2, 0), some(0, 0), f_send.at[0], f_recv.at[0], (r + 2, z))
    f_dn = remote(some(2, 0), some(4, 0), f_send.at[1], f_recv.at[1], (r - 2, z))
    f_up2 = remote(some(2, 1), some(0, 1), f_send.at[4], f_recv.at[4], (r + 2, z))
    f_dn2 = remote(some(2, 1), some(4, 1), f_send.at[5], f_recv.at[5], (r - 2, z))
    f_out = remote(some(2, 1), f_relay, f_send.at[6], f_recv.at[6], (far, z))
    f_on = remote(f_relay, some(4 - 4 * bit2, 1), f_send.at[7], f_recv.at[5 - bit2], (near, z))
    f_sib = remote(own, panel(ext, 1 + 2 * k), f_send.at[2], f_recv.at[2], (sib, z))
    f_fwd = remote(
        panel(ext, 4 - 4 * k), panel(ext, 3 - 2 * k), f_send.at[3], f_recv.at[3], (sib, z)
    )
    from_dn = [
        remote(some(0, h), some(0, h), f_send.at[4 * h], f_recv.at[4 * h], (r - 2, z))
        for h in range(2)
    ]
    from_up = [
        remote(some(4, h), some(4, h), f_send.at[4 * h + 1], f_recv.at[4 * h + 1], (r + 2, z))
        for h in range(2)
    ]
    from_sib = remote(own, panel(ext, 3 - 2 * k), f_send.at[2], f_recv.at[2], (sib, z))
    from_fwd = remote(own, panel(ext, 1 + 2 * k), f_send.at[3], f_recv.at[3], (sib, z))
    fwd_out = jnp.where(k == 0, r + 2 < n_row, r >= 2)
    fwd_in = jnp.where(k == 0, r >= 2, r + 2 < n_row)

    starts = (
        (turning, f_out), (has_up, f_up), (has_dn, f_dn), (straight_up, f_up2), (straight_dn, f_dn2)
    )
    for ok, copy in starts:
        pl.when(ok)(copy.start)
    f_sib.start()

    eighth = feat // 8

    def span(ref, start, count):
        return ref.at[pl.ds(pl.multiple_of(start * eighth, eighth), count * eighth)]

    def rounds(raw, full, base, bit_a, dev_a, bit_b, dev_b):
        mine = 4 * k + 2 * bit_b + bit_a
        plan = (
            (raw, mine, mine, 1, (r, mate)),
            (full, mine, mine + 1 - 2 * bit_a, 1, (dev_a, z)),
            (full, 4 * k + 2 * bit_b, 4 * k + 2 - 2 * bit_b, 2, (dev_b, z)),
            (full, 4 * k, 4 - 4 * k, 4, (sib, z)),
        )
        sent, got = [], []
        for i, (src, lo, there, count, dev) in enumerate(plan):
            sems = (w_send.at[base + i], w_recv.at[base + i])
            sent.append(remote(span(src, lo, count), span(full, lo, count), *sems, dev))
            got.append(remote(span(full, there, count), span(full, there, count), *sems, dev))
        return sent, got

    in_sent, in_got = rounds(w_in_ref, w2_in, 0, bit2, near, bit4, far)
    out_sent, out_got = rounds(w_out_ref, w2_out, 4, bit4, far, bit2, near)

    def exchange(src, dst, kind, c, count=1):
        return [
            remote(
                half_part(src, lax.rem(zp, 2), c, count),
                dst.at[z, pl.ds(c * part, count * part)],
                a_send.at[kind, i], a_recv.at[kind, i], (r, zp),
            )
            for i, zp in enumerate(peers)
        ]

    def arrivals(buf, kind, c, count=1):
        views = [buf.at[zf, pl.ds(c * part, count * part)] for zf in peers]
        return [
            remote(v, v, a_send.at[kind, i], a_recv.at[kind, i], (r, zf))
            for i, (v, zf) in enumerate(zip(views, peers))
        ]

    in_sent[0].start()
    out_sent[0].start()
    cot_out = exchange(cot_ref, cot_full, 0, 0, PARTS)
    for copy in cot_out:
        copy.start()

    @pl.when(jnp.logical_not(has_dn))
    def _():
        ext[0:row_blocks] = jnp.zeros((row_blocks, 128, quarter), BF16)

    @pl.when(jnp.logical_not(has_up))
    def _():
        ext[4 * row_blocks : 5 * row_blocks] = jnp.zeros((row_blocks, 128, quarter), BF16)

    @pl.when(r < 1)
    def _():
        ext[row_blocks : 2 * row_blocks] = jnp.zeros((row_blocks, 128, quarter), BF16)

    @pl.when(r + 1 >= n_row)
    def _():
        ext[3 * row_blocks : 4 * row_blocks] = jnp.zeros((row_blocks, 128, quarter), BF16)

    for copy in loads:
        copy.wait()

    def transpose_block(b, carry):
        for s in range(slots):
            vals_t[b, s] = vals[b, s].astype(F32).T.astype(BF16)
        return carry

    lax.fori_loop(0, row_blocks, transpose_block, 0)

    for b in range(row_blocks):
        for s in range(slots):
            col = jnp.broadcast_to(spread_ref[s : s + 1, b : b + 1], (16, 128))
            marks[b * slots + s] = jnp.where(col >= 0, col - first, -1)

    def fill_dense(t, carry):
        at = pl.ds(pl.multiple_of(t * 128, 128), 128)
        for b in range(row_blocks):
            turned = jnp.zeros((8, 16, 128), BF16)
            for s in range(slots):
                keep = jnp.where(marks[b * slots + s] == t, 1.0, 0.0).astype(BF16)[None]
                turned = turned + vals_t[b, s].reshape(8, 16, 128) * keep
            dense_t[at, b * 128 : (b + 1) * 128] = turned.reshape(128, 128)
        return carry

    @pl.when(passing)
    def _():
        f_out.wait_recv()
        f_on.start()

    @pl.when(has_dn)
    def _():
        for copy in from_dn:
            copy.wait_recv()

    @pl.when(has_up)
    def _():
        for copy in from_up:
            copy.wait_recv()

    @pl.when(fwd_out)
    def _():
        f_fwd.start()

    from_sib.wait_recv()

    @pl.when(fwd_in)
    def _():
        from_fwd.wait_recv()

    def gather(b):
        left, right = [], []
        for s in range(slots):
            col = cols_ref[s, b]
            absent = lax.shift_right_logical(col, 31)
            place = col - first + absent * (1 + first + 2 * row_blocks + b)
            keep = jnp.where(marks[b * slots + s] >= 0, 1.0, 0.0).astype(BF16)[None]
            left.append((vals[b, s].reshape(8, 16, 128) * keep).reshape(128, 128))
            right.append(ext[jnp.minimum(jnp.maximum(place, 0), 5 * row_blocks - 1)])
        res = dot(jnp.concatenate(left, axis=1), jnp.concatenate(right, axis=0))
        agg[b * 128 : (b + 1) * 128, :] = res.astype(BF16)

    agg_out = []
    per_part = part // 128
    for c in range(PARTS):
        for s in range(2):
            for i in range(per_part):
                gather((s * PARTS + c) * per_part + i)
        agg_out.append(exchange(agg, agg_full, 1 + c, c))
        for copy in agg_out[c]:
            copy.start()
    for c in range(PARTS):
        agg_full[z, pl.ds(c * part, part)] = agg[
            pl.ds(pl.multiple_of(z1 * half + c * part, part), part), :
        ]

    out_got[0].wait_recv()
    out_sent[1].start()
    in_got[0].wait_recv()
    in_sent[1].start()
    cut = 3 * row_blocks
    lax.fori_loop(0, cut, fill_dense, 0)
    in_got[1].wait_recv()
    in_sent[2].start()
    out_got[1].wait_recv()
    out_sent[2].start()
    lax.fori_loop(cut, 5 * row_blocks, fill_dense, 0)
    tile = 256

    def hidden_part(w_a, w_b, base, c):
        rs = pl.ds(c * part, part)

        def step(i, carry):
            hc = pl.ds(pl.multiple_of(i * tile, tile), tile)
            to = pl.ds(pl.multiple_of(base + i * tile, tile), tile)
            x = jnp.concatenate([agg_full[q, rs] for q in range(n_rep)], axis=1)
            g = jnp.concatenate([cot_full[q, rs] for q in range(n_rep)], axis=1)
            value, slope = gelu_pair(dot(x, w_a[:, hc]))
            hid[rs, to] = value.astype(BF16)
            gp[rs, to] = (dot(g, w_b[:, hc]) * slope).astype(BF16)
            return carry

        lax.fori_loop(0, hidw // tile, step, 0)

    def product(src, w_a, w_b, zq, c):
        at = pl.ds(pl.multiple_of(zq * quarter, quarter), quarter)
        rs = pl.ds(c * part, part)
        res = dot(src[rs, :hidw], w_a[at, :], ((1,), (1,)))
        res = res + dot(src[rs, hidw:], w_b[at, :], ((1,), (1,)))
        return res.astype(BF16)

    def adj_copies(f, c):
        kind = 1 + PARTS + f * PARTS + c
        rs = pl.ds(c * part, part)
        return [
            remote(
                adj_p.at[zp, f, rs], adj_in.at[z, f, rs],
                a_send.at[kind, i], a_recv.at[kind, i], (r, zp),
            )
            for i, zp in enumerate(peers)
        ]

    def adj_arrivals(f, c):
        kind = 1 + PARTS + f * PARTS + c
        views = [adj_in.at[zf, f, pl.ds(c * part, part)] for zf in peers]
        return [
            remote(v, v, a_send.at[kind, i], a_recv.at[kind, i], (r, zf))
            for i, (v, zf) in enumerate(zip(views, peers))
        ]

    for copy in arrivals(cot_full, 0, 0, PARTS):
        copy.wait_recv()
    adj_sent = [[adj_copies(f, c) for c in range(PARTS)] for f in range(WIDE)]
    for c in range(PARTS):
        for copy in arrivals(agg_full, 1 + c, c):
            copy.wait_recv()
        hidden_part(w1_in, w1_out, 0, c)
        if c == 0:
            in_got[2].wait_recv()
            in_sent[3].start()
            out_got[2].wait_recv()
            out_sent[3].start()
            in_got[3].wait_recv()
            out_got[3].wait_recv()
        hidden_part(w2_in, w2_out, hidw, c)
        rs = pl.ds(c * part, part)
        for i, zp in enumerate(peers + [z]):
            res = product(gp, w1_in, w2_in, zp, c)
            made = adj_p if i < n_rep - 1 else adj_in
            for f in range(WIDE):
                made[zp, f, rs] = res[:, f * width : (f + 1) * width]
            if i < n_rep - 1:
                adj_sent[0][c][i].start()

    out_sends = []
    for c in range(PARTS):
        rs = pl.ds(c * part, part)
        kind = 1 + (1 + WIDE) * PARTS + c
        for i, zp in enumerate(peers):
            out_p[zp, rs] = product(hid, w1_out, w2_out, zp, c)
            out_sends.append(
                remote(
                    out_p.at[zp, rs], out_in.at[z, rs],
                    a_send.at[kind, i], a_recv.at[kind, i], (r, zp),
                )
            )
        out_in[z, rs] = product(hid, w1_out, w2_out, z, c)

    tile = 256
    plain_to, helped_to = r - 2 + 4 * k, r + 2 - 4 * k
    plain_ok, helped_ok = fwd_in, fwd_out
    turn_plain = jnp.logical_and(turning, k == bit2)
    turn_helped = jnp.logical_and(turning, k != bit2)
    p5_sent = []

    def turn(f):
        for c in range(PARTS):
            for copy in adj_arrivals(f, c):
                copy.wait_recv()
        for s in range(2):
            total = adj_in[s, f].astype(F32)
            for q in range(s + 2, n_rep, 2):
                total = total + adj_in[q, f].astype(F32)
            adj[f, s * half : (s + 1) * half] = total.astype(BF16)

        def put(p, slot):
            def step(m, carry):
                at = pl.ds(pl.multiple_of(m * tile, tile), tile)
                c_send[4 * f + slot, at, :] = piece(f, p, m).astype(BF16)
                return carry

            lax.fori_loop(0, rows // tile, step, 0)

        def cross(slot, dst, got, dev):
            return remote(
                c_send.at[4 * f + slot], dst, c_sends.at[4 * f + slot], c_recvs.at[4 * f + got], dev
            )

        c_help = cross(0, c_sib.at[2 * f], 0, (sib, z))
        c_own = cross(1, c_sib.at[2 * f + 1], 1, (sib, z))
        top, low = pl.ds(0, rows // 2), pl.ds(rows // 2, rows // 2)

        def sides(slot, nbr, dev):
            return (
                remote(
                    c_send.at[4 * f + slot, top], c_nbr.at[2 * f + nbr, top],
                    c_sends.at[4 * f + slot], c_recvs.at[4 * f + 2 + nbr], dev,
                ),
                remote(
                    c_send.at[4 * f + slot, low], c_nbr.at[2 * f + nbr, low],
                    b_sends.at[4 * f + slot], b_recvs.at[4 * f + 2 + nbr], dev,
                ),
            )

        c_plain = sides(2, 1 - k, (plain_to, z))
        c_helped = sides(3, k, (helped_to, z))
        c_out = remote(
            c_send.at[4 * f + jnp.where(k == bit2, 2, 3), low], c_relay.at[f],
            b_sends.at[4 * f], b_recvs.at[4 * f], (far, z),
        )
        c_on = remote(
            c_relay.at[f], c_nbr.at[2 * f + 1 - bit2, low],
            b_sends.at[4 * f + 1], b_recvs.at[4 * f + 3 - bit2], (near, z),
        )
        moves = (
            (plain_ok, c_plain[0]), (jnp.logical_and(plain_ok, jnp.logical_not(turn_plain)), c_plain[1]),
            (helped_ok, c_helped[0]),
            (jnp.logical_and(helped_ok, jnp.logical_not(turn_helped)), c_helped[1]),
            (turning, c_out), (passing, c_on),
        )
        put(1 + 2 * k, 0)
        c_help.start()
        put(4 * k, 2)

        pl.when(turn_plain)(c_out.start)
        for ok, copy in moves[:2]:
            pl.when(ok)(copy.start)
        c_help.wait_recv()

        def add_help(m, carry):
            at = pl.ds(pl.multiple_of(m * tile, tile), tile)
            total = piece(f, 4 - 4 * k, m) + c_sib[2 * f, at, :].astype(F32)
            c_send[4 * f + 3, at, :] = total.astype(BF16)
            return carry

        lax.fori_loop(0, rows // tile, add_help, 0)

        pl.when(turn_helped)(c_out.start)
        for ok, copy in moves[2:4]:
            pl.when(ok)(copy.start)
        put(3 - 2 * k, 1)
        c_own.start()

        @pl.when(passing)
        def _():
            c_out.wait_recv()
            c_on.start()

        p5_sent.append((c_help, c_own, moves))

    def piece(f, p, m):
        at = pl.ds(pl.multiple_of(p * rows + m * tile, tile), tile)
        return dot(dense_t[at, :], adj[f])

    def finish(f):
        p5_sent[f][1].wait_recv()

        def landed(nbr, dev):
            for h, sems in enumerate((c_recvs, b_recvs)):
                ref = c_nbr.at[2 * f + nbr, pl.ds(h * (rows // 2), rows // 2)]
                remote(ref, ref, c_sends.at[4 * f + 2], sems.at[4 * f + 2 + nbr], (dev, z)).wait_recv()

        @pl.when(has_dn)
        def _():
            landed(0, r - 2)

        @pl.when(jnp.logical_not(has_dn))
        def _():
            c_nbr[2 * f] = jnp.zeros((rows, width), BF16)

        @pl.when(has_up)
        def _():
            landed(1, r + 2)

        @pl.when(jnp.logical_not(has_up))
        def _():
            c_nbr[2 * f + 1] = jnp.zeros((rows, width), BF16)

        cs = slice(f * width, (f + 1) * width)

        def step(m, carry):
            at = pl.ds(pl.multiple_of(m * tile, tile), tile)
            total = piece(f, 2, m) + c_sib[2 * f + 1, at, :].astype(F32)
            total = total + c_nbr[2 * f, at, :].astype(F32) + c_nbr[2 * f + 1, at, :].astype(F32)
            grad_ref[at, cs] = (cot[at, cs].astype(F32) + total).astype(BF16)
            return carry

        lax.fori_loop(0, rows // tile, step, 0)

    for f in range(WIDE):
        for copies in adj_sent[f]:
            for copy in copies:
                copy.wait_send()
        following = sum(adj_sent[f + 1], []) if f + 1 < WIDE else out_sends
        for copy in following:
            copy.start()
        turn(f)
    for f in range(WIDE):
        finish(f)
    grad_out = pltpu.make_async_copy(grad_ref, grad_hbm, loc_sem.at[6])
    grad_out.start()
    for c in range(PARTS):
        for copy in arrivals(out_in, 1 + (1 + WIDE) * PARTS + c, c):
            copy.wait_recv()
        rs = pl.ds(c * part, part)
        for s in range(2):
            total = out_in[s, rs].astype(F32)
            for q in range(s + 2, n_rep, 2):
                total = total + out_in[q, rs].astype(F32)
            start, count = 2 * row_blocks + s * row_blocks // 2 + c * per_part, per_part
            mine = ext[start : start + count].reshape(part, quarter)
            at = pl.ds(s * half + c * part, part)
            upd_ref[at] = (mine.astype(F32) + total).astype(BF16)

    upd_out = pltpu.make_async_copy(upd_ref, upd_hbm, loc_sem.at[7])
    upd_out.start()
    for copy in cot_out + in_sent + out_sent + agg_out[0] + agg_out[1] + out_sends + [f_sib]:
        copy.wait_send()
    late = list(starts) + [(fwd_out, f_fwd), (passing, f_on)]
    for c_help, c_own, moves in p5_sent:
        c_help.wait_send()
        c_own.wait_send()
        late += list(moves)
    for ok, copy in late:
        pl.when(ok)(copy.wait_send)
    grad_out.wait()
    upd_out.wait()


def settle(upd_ref, grad_ref, upd_out, grad_out, held, sems):
    size = upd_ref.shape[0] // CUTS
    steps = []
    for i in range(CUTS):
        rs = pl.ds(i * size, size)
        for j, (src, dst) in enumerate(((upd_ref, upd_out), (grad_ref, grad_out))):
            steps.append((
                pltpu.make_async_copy(src.at[rs], held.at[j, rs], sems.at[0, j, i]),
                pltpu.make_async_copy(held.at[j, rs], dst.at[rs], sems.at[1, j, i]),
            ))
    for load, _ in steps:
        load.start()
    for load, store in steps:
        load.wait()
        store.start()
    for _, store in steps:
        store.wait()


def body(n_row, n_rep, node_feats, block_cols, block_vals, w_in, w_out, cotangent):
    rows, quarter = cotangent.shape
    row_blocks, slots = block_cols.shape
    feat, hidw = w_in.shape
    half = rows // 2
    kinds = 1 + (2 + WIDE) * PARTS
    width = quarter // WIDE
    vmem = pl.BlockSpec(memory_space=pltpu.VMEM)
    anywhere = pl.BlockSpec(memory_space=pl.ANY)
    dma = pltpu.SemaphoreType.DMA
    made = pl.pallas_call(
        functools.partial(kernel, n_row, n_rep),
        out_shape=(jax.ShapeDtypeStruct((rows, quarter), BF16),) * 2,
        in_specs=[pl.BlockSpec(memory_space=pltpu.SMEM), vmem] + [anywhere] * 5,
        out_specs=(anywhere, anywhere),
        scratch_shapes=[
            pltpu.VMEM((rows, quarter), BF16),
            pltpu.VMEM((rows, quarter), BF16),
            pltpu.VMEM((5 * row_blocks, 128, quarter), BF16),
            pltpu.VMEM((row_blocks * slots, 16, 128), jnp.int32),
            pltpu.VMEM((row_blocks, slots, 128, 128), BF16),
            pltpu.VMEM((row_blocks, slots, 128, 128), BF16),
            pltpu.VMEM((5 * rows, rows), BF16),
            pltpu.VMEM((feat, hidw), BF16),
            pltpu.VMEM((feat, hidw), BF16),
            pltpu.VMEM((feat, hidw), BF16),
            pltpu.VMEM((feat, hidw), BF16),
            pltpu.VMEM((rows, quarter), BF16),
            pltpu.VMEM((n_rep, half, quarter), BF16),
            pltpu.VMEM((rows, quarter), BF16),
            pltpu.VMEM((n_rep, half, quarter), BF16),
            pltpu.VMEM((half, 2 * hidw), BF16),
            pltpu.VMEM((half, 2 * hidw), BF16),
            pltpu.VMEM((n_rep, WIDE, half, width), BF16),
            pltpu.VMEM((n_rep, half, quarter), BF16),
            pltpu.VMEM((n_rep, WIDE, half, width), BF16),
            pltpu.VMEM((n_rep, half, quarter), BF16),
            pltpu.VMEM((WIDE, rows, width), BF16),
            pltpu.VMEM((4 * WIDE, rows, width), BF16),
            pltpu.VMEM((2 * WIDE, rows, width), BF16),
            pltpu.VMEM((2 * WIDE, rows, width), BF16),
            pltpu.VMEM((row_blocks // 2, 128, quarter), BF16),
            pltpu.VMEM((WIDE, rows // 2, width), BF16),
            dma((8,)),
            dma((8,)),
            dma((8,)),
            dma((8,)),
            dma((8,)),
            dma((kinds, n_rep - 1)),
            dma((kinds, n_rep - 1)),
            dma((4 * WIDE,)),
            dma((4 * WIDE,)),
            dma((4 * WIDE,)),
            dma((4 * WIDE,)),
        ],
        compiler_params=pltpu.CompilerParams(
            collective_id=0, has_side_effects=True, vmem_limit_bytes=60 * 1024 * 1024
        ),
    )(block_cols.T, block_cols.T, node_feats.reshape(row_blocks, 128, feat), block_vals, w_in, w_out, cotangent)
    return pl.pallas_call(
        settle,
        out_shape=(jax.ShapeDtypeStruct((rows, quarter), BF16),) * 2,
        in_specs=[anywhere] * 2,
        out_specs=(anywhere,) * 2,
        scratch_shapes=[pltpu.VMEM((2, rows, quarter), BF16), dma((2, 2, CUTS))],
    )(*made)


def solution(mesh):
    in_specs = (
        P("row", None),
        P("row", None),
        P("row", None, None, None),
        P(None, "rep"),
        P(None, "rep"),
        P("row", "rep"),
    )
    out_specs = (P("row", "rep"), P("row", "rep"))
    run = functools.partial(body, mesh.shape["row"], mesh.shape["rep"])
    return jax.shard_map(run, mesh=mesh, in_specs=in_specs, out_specs=out_specs, check_vma=False)
```

```python
import functools

import jax
import jax.numpy as jnp
from jax import lax
from jax.experimental import pallas as pl
from jax.experimental.pallas import tpu as pltpu
from jax.sharding import PartitionSpec as P

F32 = jnp.float32
BF16 = jnp.bfloat16
MESH = pl.DeviceIdType.MESH
PARTS = 2
WIDE = 2
CUTS = 4


def dot(a, b, dims=((1,), (0,))):
    return lax.dot_general(a, b, (dims, ((), ())), preferred_element_type=F32)


def gelu_pair(v):
    c = 0.7978845608
    vv = v * v
    t = jnp.tanh(c * (v + 0.044715 * v * vv))
    half = 0.5 * (1.0 + t)
    value = v * half
    slope = half + 0.5 * v * (1.0 - t * t) * c * (1.0 + 3.0 * 0.044715 * vv)
    return value, slope


def kernel(
    n_row, n_rep, places_ref, feats_ref, vals_ref, w_in_ref, w_out_ref, cot_ref,
    upd_ref, grad_ref,
    cols_ref, spread_ref, ext, marks, vals, vals_t, dense_t, w1_in, w1_out, w2_in, w2_out, cot, cot_full, agg, agg_full, hid, gp,
    adj_p, out_p, adj_in, out_in, adj, c_send, c_sib, c_nbr, f_relay, c_relay,
    loc_sem, f_send, f_recv, w_send, w_recv, a_send, a_recv, c_sends, c_recvs, b_sends, b_recvs,
):
    r, z = lax.axis_index("row"), lax.axis_index("rep")
    k = lax.rem(r, 2)
    sib = r + 1 - 2 * k
    z1, z2 = lax.rem(z, 2), lax.div(z, 2)
    mate = z + 1 - 2 * z1
    peers = [z + 2 - 4 * z2, n_rep - 1 - z, mate]
    bit2, bit4 = lax.rem(lax.div(r, 2), 2), lax.rem(lax.div(r, 4), 2)
    near, far = r + 2 - 4 * bit2, r + 4 - 8 * bit4
    rows, quarter = cot.shape
    half = rows // 2
    part = half // PARTS
    width = quarter // WIDE
    slots, row_blocks = cols_ref.shape
    feat, hidw = w1_in.shape
    has_up, has_dn = r + 2 < n_row, r >= 2
    turning, passing = bit2 != bit4, bit2 == bit4
    turn_up, turn_dn = jnp.logical_and(turning, bit2 == 1), jnp.logical_and(turning, bit2 == 0)
    straight_up = jnp.logical_and(has_up, jnp.logical_not(turn_up))
    straight_dn = jnp.logical_and(has_dn, jnp.logical_not(turn_dn))
    hb = row_blocks // 2
    first = (r - 2) * row_blocks

    def remote(src, dst, send, recv, dev):
        return pltpu.make_async_remote_copy(
            src_ref=src, dst_ref=dst, send_sem=send, recv_sem=recv, device_id=dev, device_id_type=MESH
        )

    def panel(ref, slot):
        return ref.at[pl.ds(slot * row_blocks, row_blocks)]

    def half_part(ref, s, c, count=1):
        start = pl.multiple_of(s * half + c * part, part)
        return ref.at[pl.ds(start, count * part)]

    barrier = pltpu.get_barrier_semaphore()
    for zp in peers:
        pl.semaphore_signal(barrier, inc=1, device_id=(r, zp), device_id_type=MESH)
    pl.semaphore_signal(barrier, inc=1, device_id=(sib, z), device_id_type=MESH)
    pl.semaphore_signal(barrier, inc=1, device_id=(far, z), device_id_type=MESH)

    @pl.when(has_up)
    def _():
        pl.semaphore_signal(barrier, inc=1, device_id=(r + 2, z), device_id_type=MESH)

    @pl.when(has_dn)
    def _():
        pl.semaphore_signal(barrier, inc=1, device_id=(r - 2, z), device_id_type=MESH)

    columns = pl.ds(pl.multiple_of(z * quarter, quarter), quarter)
    own_copy = pltpu.make_async_copy(feats_ref.at[:, :, columns], panel(ext, 2), loc_sem.at[0])
    loads = [
        pltpu.make_async_copy(src, dst, loc_sem.at[1 + i])
        for i, (src, dst) in enumerate(
            (
                (vals_ref, vals),
                (places_ref, cols_ref),
                (places_ref, spread_ref),
                (half_part(cot_ref, z1, 0, PARTS), cot_full.at[z]),
                (w_in_ref, w1_in),
                (w_out_ref, w1_out),
                (cot_ref, cot),
            )
        )
    ]
    own_copy.start()
    for copy in loads:
        copy.start()
    own_copy.wait()
    pl.semaphore_wait(barrier, n_rep + 1 + has_up.astype(jnp.int32) + has_dn.astype(jnp.int32))

    own = panel(ext, 2)

    def some(slot, h):
        return ext.at[pl.ds(slot * row_blocks + h * hb, hb)]

    f_up = remote(some(2, 0), some(0, 0), f_send.at[0], f_recv.at[0], (r + 2, z))
    f_dn = remote(some(2, 0), some(4, 0), f_send.at[1], f_recv.at[1], (r - 2, z))
    f_up2 = remote(some(2, 1), some(0, 1), f_send.at[4], f_recv.at[4], (r + 2, z))
    f_dn2 = remote(some(2, 1), some(4, 1), f_send.at[5], f_recv.at[5], (r - 2, z))
    f_out = remote(some(2, 1), f_relay, f_send.at[6], f_recv.at[6], (far, z))
    f_on = remote(f_relay, some(4 - 4 * bit2, 1), f_send.at[7], f_recv.at[5 - bit2], (near, z))
    f_sib = remote(own, panel(ext, 1 + 2 * k), f_send.at[2], f_recv.at[2], (sib, z))
    f_fwd = remote(
        panel(ext, 4 - 4 * k), panel(ext, 3 - 2 * k), f_send.at[3], f_recv.at[3], (sib, z)
    )
    from_dn = [
        remote(some(0, h), some(0, h), f_send.at[4 * h], f_recv.at[4 * h], (r - 2, z))
        for h in range(2)
    ]
    from_up = [
        remote(some(4, h), some(4, h), f_send.at[4 * h + 1], f_recv.at[4 * h + 1], (r + 2, z))
        for h in range(2)
    ]
    from_sib = remote(own, panel(ext, 3 - 2 * k), f_send.at[2], f_recv.at[2], (sib, z))
    from_fwd = remote(own, panel(ext, 1 + 2 * k), f_send.at[3], f_recv.at[3], (sib, z))
    fwd_out = jnp.where(k == 0, r + 2 < n_row, r >= 2)
    fwd_in = jnp.where(k == 0, r >= 2, r + 2 < n_row)

    starts = (
        (turning, f_out), (has_up, f_up), (has_dn, f_dn), (straight_up, f_up2), (straight_dn, f_dn2)
    )
    for ok, copy in starts:
        pl.when(ok)(copy.start)
    f_sib.start()

    eighth = feat // 8

    def span(ref, start, count):
        return ref.at[pl.ds(pl.multiple_of(start * eighth, eighth), count * eighth)]

    def rounds(raw, full, base, bit_a, dev_a, bit_b, dev_b):
        mine = 4 * k + 2 * bit_b + bit_a
        plan = (
            (raw, mine, mine, 1, (r, mate)),
            (full, mine, mine + 1 - 2 * bit_a, 1, (dev_a, z)),
            (full, 4 * k + 2 * bit_b, 4 * k + 2 - 2 * bit_b, 2, (dev_b, z)),
            (full, 4 * k, 4 - 4 * k, 4, (sib, z)),
        )
        sent, got = [], []
        for i, (src, lo, there, count, dev) in enumerate(plan):
            sems = (w_send.at[base + i], w_recv.at[base + i])
            sent.append(remote(span(src, lo, count), span(full, lo, count), *sems, dev))
            got.append(remote(span(full, there, count), span(full, there, count), *sems, dev))
        return sent, got

    in_sent, in_got = rounds(w_in_ref, w2_in, 0, bit2, near, bit4, far)
    out_sent, out_got = rounds(w_out_ref, w2_out, 4, bit4, far, bit2, near)

    def exchange(src, dst, kind, c, count=1):
        return [
            remote(
                half_part(src, lax.rem(zp, 2), c, count),
                dst.at[z, pl.ds(c * part, count * part)],
                a_send.at[kind, i], a_recv.at[kind, i], (r, zp),
            )
            for i, zp in enumerate(peers)
        ]

    def arrivals(buf, kind, c, count=1):
        views = [buf.at[zf, pl.ds(c * part, count * part)] for zf in peers]
        return [
            remote(v, v, a_send.at[kind, i], a_recv.at[kind, i], (r, zf))
            for i, (v, zf) in enumerate(zip(views, peers))
        ]

    in_sent[0].start()
    out_sent[0].start()
    cot_out = exchange(cot_ref, cot_full, 0, 0, PARTS)
    for copy in cot_out:
        copy.start()

    @pl.when(jnp.logical_not(has_dn))
    def _():
        ext[0:row_blocks] = jnp.zeros((row_blocks, 128, quarter), BF16)

    @pl.when(jnp.logical_not(has_up))
    def _():
        ext[4 * row_blocks : 5 * row_blocks] = jnp.zeros((row_blocks, 128, quarter), BF16)

    @pl.when(r < 1)
    def _():
        ext[row_blocks : 2 * row_blocks] = jnp.zeros((row_blocks, 128, quarter), BF16)

    @pl.when(r + 1 >= n_row)
    def _():
        ext[3 * row_blocks : 4 * row_blocks] = jnp.zeros((row_blocks, 128, quarter), BF16)

    for copy in loads:
        copy.wait()

    def transpose_block(b, carry):
        for s in range(slots):
            vals_t[b, s] = vals[b, s].astype(F32).T.astype(BF16)
        return carry

    lax.fori_loop(0, row_blocks, transpose_block, 0)

    for b in range(row_blocks):
        for s in range(slots):
            col = jnp.broadcast_to(spread_ref[s : s + 1, b : b + 1], (16, 128))
            marks[b * slots + s] = jnp.where(col >= 0, col - first, -1)

    def fill_dense(t, carry):
        at = pl.ds(pl.multiple_of(t * 128, 128), 128)
        for b in range(row_blocks):
            turned = jnp.zeros((8, 16, 128), BF16)
            for s in range(slots):
                keep = jnp.where(marks[b * slots + s] == t, 1.0, 0.0).astype(BF16)[None]
                turned = turned + vals_t[b, s].reshape(8, 16, 128) * keep
            dense_t[at, b * 128 : (b + 1) * 128] = turned.reshape(128, 128)
        return carry

    @pl.when(passing)
    def _():
        f_out.wait_recv()
        f_on.start()

    @pl.when(has_dn)
    def _():
        for copy in from_dn:
            copy.wait_recv()

    @pl.when(has_up)
    def _():
        for copy in from_up:
            copy.wait_recv()

    @pl.when(fwd_out)
    def _():
        f_fwd.start()

    from_sib.wait_recv()

    @pl.when(fwd_in)
    def _():
        from_fwd.wait_recv()

    def gather(b):
        left, right = [], []
        for s in range(slots):
            col = cols_ref[s, b]
            absent = lax.shift_right_logical(col, 31)
            place = col - first + absent * (1 + first + 2 * row_blocks + b)
            keep = jnp.where(marks[b * slots + s] >= 0, 1.0, 0.0).astype(BF16)[None]
            left.append((vals[b, s].reshape(8, 16, 128) * keep).reshape(128, 128))
            right.append(ext[jnp.minimum(jnp.maximum(place, 0), 5 * row_blocks - 1)])
        res = dot(jnp.concatenate(left, axis=1), jnp.concatenate(right, axis=0))
        agg[b * 128 : (b + 1) * 128, :] = res.astype(BF16)

    agg_out = []
    per_part = part // 128
    for c in range(PARTS):
        for s in range(2):
            for i in range(per_part):
                gather((s * PARTS + c) * per_part + i)
        agg_out.append(exchange(agg, agg_full, 1 + c, c))
        for copy in agg_out[c]:
            copy.start()
    for c in range(PARTS):
        agg_full[z, pl.ds(c * part, part)] = agg[
            pl.ds(pl.multiple_of(z1 * half + c * part, part), part), :
        ]

    out_got[0].wait_recv()
    out_sent[1].start()
    in_got[0].wait_recv()
    in_sent[1].start()
    cut = 3 * row_blocks
    lax.fori_loop(0, cut, fill_dense, 0)
    in_got[1].wait_recv()
    in_sent[2].start()
    out_got[1].wait_recv()
    out_sent[2].start()
    lax.fori_loop(cut, 5 * row_blocks, fill_dense, 0)
    tile = 256

    def hidden_part(w_a, w_b, base, c):
        rs = pl.ds(c * part, part)

        def step(i, carry):
            hc = pl.ds(pl.multiple_of(i * tile, tile), tile)
            to = pl.ds(pl.multiple_of(base + i * tile, tile), tile)
            x = jnp.concatenate([agg_full[q, rs] for q in range(n_rep)], axis=1)
            g = jnp.concatenate([cot_full[q, rs] for q in range(n_rep)], axis=1)
            value, slope = gelu_pair(dot(x, w_a[:, hc]))
            hid[rs, to] = value.astype(BF16)
            gp[rs, to] = (dot(g, w_b[:, hc]) * slope).astype(BF16)
            return carry

        lax.fori_loop(0, hidw // tile, step, 0)

    def product(src, w_a, w_b, zq, c):
        at = pl.ds(pl.multiple_of(zq * quarter, quarter), quarter)
        rs = pl.ds(c * part, part)
        res = dot(src[rs, :hidw], w_a[at, :], ((1,), (1,)))
        res = res + dot(src[rs, hidw:], w_b[at, :], ((1,), (1,)))
        return res.astype(BF16)

    def adj_copies(f, c):
        kind = 1 + PARTS + f * PARTS + c
        rs = pl.ds(c * part, part)
        return [
            remote(
                adj_p.at[zp, f, rs], adj_in.at[z, f, rs],
                a_send.at[kind, i], a_recv.at[kind, i], (r, zp),
            )
            for i, zp in enumerate(peers)
        ]

    def adj_arrivals(f, c):
        kind = 1 + PARTS + f * PARTS + c
        views = [adj_in.at[zf, f, pl.ds(c * part, part)] for zf in peers]
        return [
            remote(v, v, a_send.at[kind, i], a_recv.at[kind, i], (r, zf))
            for i, (v, zf) in enumerate(zip(views, peers))
        ]

    for copy in arrivals(cot_full, 0, 0, PARTS):
        copy.wait_recv()
    adj_sent = [[adj_copies(f, c) for c in range(PARTS)] for f in range(WIDE)]
    for c in range(PARTS):
        for copy in arrivals(agg_full, 1 + c, c):
            copy.wait_recv()
        hidden_part(w1_in, w1_out, 0, c)
        if c == 0:
            in_got[2].wait_recv()
            in_sent[3].start()
            out_got[2].wait_recv()
            out_sent[3].start()
            in_got[3].wait_recv()
            out_got[3].wait_recv()
        hidden_part(w2_in, w2_out, hidw, c)
        rs = pl.ds(c * part, part)
        for i, zp in enumerate(peers + [z]):
            res = product(gp, w1_in, w2_in, zp, c)
            made = adj_p if i < n_rep - 1 else adj_in
            for f in range(WIDE):
                made[zp, f, rs] = res[:, f * width : (f + 1) * width]
            if i < n_rep - 1:
                adj_sent[0][c][i].start()

    out_sends = []
    for c in range(PARTS):
        rs = pl.ds(c * part, part)
        kind = 1 + (1 + WIDE) * PARTS + c
        for i, zp in enumerate(peers):
            out_p[zp, rs] = product(hid, w1_out, w2_out, zp, c)
            out_sends.append(
                remote(
                    out_p.at[zp, rs], out_in.at[z, rs],
                    a_send.at[kind, i], a_recv.at[kind, i], (r, zp),
                )
            )
        out_in[z, rs] = product(hid, w1_out, w2_out, z, c)

    tile = 256
    plain_to, helped_to = r - 2 + 4 * k, r + 2 - 4 * k
    plain_ok, helped_ok = fwd_in, fwd_out
    turn_plain = jnp.logical_and(turning, k == bit2)
    turn_helped = jnp.logical_and(turning, k != bit2)
    p5_sent = []

    def turn(f):
        for c in range(PARTS):
            for copy in adj_arrivals(f, c):
                copy.wait_recv()
        for s in range(2):
            total = adj_in[s, f].astype(F32)
            for q in range(s + 2, n_rep, 2):
                total = total + adj_in[q, f].astype(F32)
            adj[f, s * half : (s + 1) * half] = total.astype(BF16)

        def put(p, slot):
            def step(m, carry):
                at = pl.ds(pl.multiple_of(m * tile, tile), tile)
                c_send[4 * f + slot, at, :] = piece(f, p, m).astype(BF16)
                return carry

            lax.fori_loop(0, rows // tile, step, 0)

        def cross(slot, dst, got, dev):
            return remote(
                c_send.at[4 * f + slot], dst, c_sends.at[4 * f + slot], c_recvs.at[4 * f + got], dev
            )

        c_help = cross(0, c_sib.at[2 * f], 0, (sib, z))
        c_own = cross(1, c_sib.at[2 * f + 1], 1, (sib, z))
        top, low = pl.ds(0, rows // 2), pl.ds(rows // 2, rows // 2)

        def sides(slot, nbr, dev):
            return (
                remote(
                    c_send.at[4 * f + slot, top], c_nbr.at[2 * f + nbr, top],
                    c_sends.at[4 * f + slot], c_recvs.at[4 * f + 2 + nbr], dev,
                ),
                remote(
                    c_send.at[4 * f + slot, low], c_nbr.at[2 * f + nbr, low],
                    b_sends.at[4 * f + slot], b_recvs.at[4 * f + 2 + nbr], dev,
                ),
            )

        c_plain = sides(2, 1 - k, (plain_to, z))
        c_helped = sides(3, k, (helped_to, z))
        c_out = remote(
            c_send.at[4 * f + jnp.where(k == bit2, 2, 3), low], c_relay.at[f],
            b_sends.at[4 * f], b_recvs.at[4 * f], (far, z),
        )
        c_on = remote(
            c_relay.at[f], c_nbr.at[2 * f + 1 - bit2, low],
            b_sends.at[4 * f + 1], b_recvs.at[4 * f + 3 - bit2], (near, z),
        )
        moves = (
            (plain_ok, c_plain[0]), (jnp.logical_and(plain_ok, jnp.logical_not(turn_plain)), c_plain[1]),
            (helped_ok, c_helped[0]),
            (jnp.logical_and(helped_ok, jnp.logical_not(turn_helped)), c_helped[1]),
            (turning, c_out), (passing, c_on),
        )
        put(1 + 2 * k, 0)
        c_help.start()
        put(4 * k, 2)

        pl.when(turn_plain)(c_out.start)
        for ok, copy in moves[:2]:
            pl.when(ok)(copy.start)
        c_help.wait_recv()

        def add_help(m, carry):
            at = pl.ds(pl.multiple_of(m * tile, tile), tile)
            total = piece(f, 4 - 4 * k, m) + c_sib[2 * f, at, :].astype(F32)
            c_send[4 * f + 3, at, :] = total.astype(BF16)
            return carry

        lax.fori_loop(0, rows // tile, add_help, 0)

        pl.when(turn_helped)(c_out.start)
        for ok, copy in moves[2:4]:
            pl.when(ok)(copy.start)
        put(3 - 2 * k, 1)
        c_own.start()

        @pl.when(passing)
        def _():
            c_out.wait_recv()
            c_on.start()

        p5_sent.append((c_help, c_own, moves))

    def piece(f, p, m):
        at = pl.ds(pl.multiple_of(p * rows + m * tile, tile), tile)
        return dot(dense_t[at, :], adj[f])

    def finish(f):
        p5_sent[f][1].wait_recv()

        def landed(nbr, dev):
            for h, sems in enumerate((c_recvs, b_recvs)):
                ref = c_nbr.at[2 * f + nbr, pl.ds(h * (rows // 2), rows // 2)]
                remote(ref, ref, c_sends.at[4 * f + 2], sems.at[4 * f + 2 + nbr], (dev, z)).wait_recv()

        @pl.when(has_dn)
        def _():
            landed(0, r - 2)

        @pl.when(jnp.logical_not(has_dn))
        def _():
            c_nbr[2 * f] = jnp.zeros((rows, width), BF16)

        @pl.when(has_up)
        def _():
            landed(1, r + 2)

        @pl.when(jnp.logical_not(has_up))
        def _():
            c_nbr[2 * f + 1] = jnp.zeros((rows, width), BF16)

        cs = slice(f * width, (f + 1) * width)

        def step(m, carry):
            at = pl.ds(pl.multiple_of(m * tile, tile), tile)
            total = piece(f, 2, m) + c_sib[2 * f + 1, at, :].astype(F32)
            total = total + c_nbr[2 * f, at, :].astype(F32) + c_nbr[2 * f + 1, at, :].astype(F32)
            grad_ref[at, cs] = (cot[at, cs].astype(F32) + total).astype(BF16)
            return carry

        lax.fori_loop(0, rows // tile, step, 0)

    for f in range(WIDE):
        for copies in adj_sent[f]:
            for copy in copies:
                copy.wait_send()
        following = sum(adj_sent[f + 1], []) if f + 1 < WIDE else out_sends
        for copy in following:
            copy.start()
        turn(f)
    for f in range(WIDE):
        finish(f)
    for c in range(PARTS):
        for copy in arrivals(out_in, 1 + (1 + WIDE) * PARTS + c, c):
            copy.wait_recv()
        rs = pl.ds(c * part, part)
        for s in range(2):
            total = out_in[s, rs].astype(F32)
            for q in range(s + 2, n_rep, 2):
                total = total + out_in[q, rs].astype(F32)
            start, count = 2 * row_blocks + s * row_blocks // 2 + c * per_part, per_part
            mine = ext[start : start + count].reshape(part, quarter)
            at = pl.ds(s * half + c * part, part)
            upd_ref[at] = (mine.astype(F32) + total).astype(BF16)

    for copy in cot_out + in_sent + out_sent + agg_out[0] + agg_out[1] + out_sends + [f_sib]:
        copy.wait_send()
    late = list(starts) + [(fwd_out, f_fwd), (passing, f_on)]
    for c_help, c_own, moves in p5_sent:
        c_help.wait_send()
        c_own.wait_send()
        late += list(moves)
    for ok, copy in late:
        pl.when(ok)(copy.wait_send)


def settle(upd_ref, grad_ref, upd_out, grad_out, sems):
    size = upd_ref.shape[0] // CUTS
    copies = [
        pltpu.make_async_copy(
            src.at[pl.ds(i * size, size)], dst.at[pl.ds(i * size, size)], sems.at[j, i]
        )
        for j, (src, dst) in enumerate(((upd_ref, upd_out), (grad_ref, grad_out)))
        for i in range(CUTS)
    ]
    for copy in copies:
        copy.start()
    for copy in copies:
        copy.wait()


def body(n_row, n_rep, node_feats, block_cols, block_vals, w_in, w_out, cotangent):
    rows, quarter = cotangent.shape
    row_blocks, slots = block_cols.shape
    feat, hidw = w_in.shape
    half = rows // 2
    kinds = 1 + (2 + WIDE) * PARTS
    width = quarter // WIDE
    vmem = pl.BlockSpec(memory_space=pltpu.VMEM)
    anywhere = pl.BlockSpec(memory_space=pl.ANY)
    dma = pltpu.SemaphoreType.DMA
    made = pl.pallas_call(
        functools.partial(kernel, n_row, n_rep),
        out_shape=(pltpu.VMEM((rows, quarter), BF16),) * 2,
        in_specs=[anywhere] * 6,
        out_specs=(vmem, vmem),
        scratch_shapes=[
            pltpu.SMEM((slots, row_blocks), jnp.int32),
            pltpu.VMEM((slots, row_blocks), jnp.int32),
            pltpu.VMEM((5 * row_blocks, 128, quarter), BF16),
            pltpu.VMEM((row_blocks * slots, 16, 128), jnp.int32),
            pltpu.VMEM((row_blocks, slots, 128, 128), BF16),
            pltpu.VMEM((row_blocks, slots, 128, 128), BF16),
            pltpu.VMEM((5 * rows, rows), BF16),
            pltpu.VMEM((feat, hidw), BF16),
            pltpu.VMEM((feat, hidw), BF16),
            pltpu.VMEM((feat, hidw), BF16),
            pltpu.VMEM((feat, hidw), BF16),
            pltpu.VMEM((rows, quarter), BF16),
            pltpu.VMEM((n_rep, half, quarter), BF16),
            pltpu.VMEM((rows, quarter), BF16),
            pltpu.VMEM((n_rep, half, quarter), BF16),
            pltpu.VMEM((half, 2 * hidw), BF16),
            pltpu.VMEM((half, 2 * hidw), BF16),
            pltpu.VMEM((n_rep, WIDE, half, width), BF16),
            pltpu.VMEM((n_rep, half, quarter), BF16),
            pltpu.VMEM((n_rep, WIDE, half, width), BF16),
            pltpu.VMEM((n_rep, half, quarter), BF16),
            pltpu.VMEM((WIDE, rows, width), BF16),
            pltpu.VMEM((4 * WIDE, rows, width), BF16),
            pltpu.VMEM((2 * WIDE, rows, width), BF16),
            pltpu.VMEM((2 * WIDE, rows, width), BF16),
            pltpu.VMEM((row_blocks // 2, 128, quarter), BF16),
            pltpu.VMEM((WIDE, rows // 2, width), BF16),
            dma((8,)),
            dma((8,)),
            dma((8,)),
            dma((8,)),
            dma((8,)),
            dma((kinds, n_rep - 1)),
            dma((kinds, n_rep - 1)),
            dma((4 * WIDE,)),
            dma((4 * WIDE,)),
            dma((4 * WIDE,)),
            dma((4 * WIDE,)),
        ],
        compiler_params=pltpu.CompilerParams(
            collective_id=0, has_side_effects=True, vmem_limit_bytes=56 * 1024 * 1024
        ),
    )(block_cols.T, node_feats.reshape(row_blocks, 128, feat), block_vals, w_in, w_out, cotangent)
    return pl.pallas_call(
        settle,
        out_shape=(jax.ShapeDtypeStruct((rows, quarter), BF16),) * 2,
        in_specs=[vmem] * 2,
        out_specs=(anywhere,) * 2,
        scratch_shapes=[dma((2, CUTS))],
    )(*(pltpu.with_memory_space_constraint(m, pltpu.VMEM) for m in made))


def solution(mesh):
    in_specs = (
        P("row", None),
        P("row", None),
        P("row", None, None, None),
        P(None, "rep"),
        P(None, "rep"),
        P("row", "rep"),
    )
    out_specs = (P("row", "rep"), P("row", "rep"))
    run = functools.partial(body, mesh.shape["row"], mesh.shape["rep"])
    return jax.shard_map(run, mesh=mesh, in_specs=in_specs, out_specs=out_specs, check_vma=False)
```

```python
import functools

import jax
import jax.numpy as jnp
from jax import lax
from jax.experimental import pallas as pl
from jax.experimental.pallas import tpu as pltpu
from jax.sharding import PartitionSpec as P

F32 = jnp.float32
BF16 = jnp.bfloat16
MESH = pl.DeviceIdType.MESH
PARTS = 2
WIDE = 2
CUTS = 4


def dot(a, b, dims=((1,), (0,))):
    return lax.dot_general(a, b, (dims, ((), ())), preferred_element_type=F32)


def gelu_pair(v):
    c = 0.7978845608
    vv = v * v
    t = jnp.tanh(c * (v + 0.044715 * v * vv))
    half = 0.5 * (1.0 + t)
    value = v * half
    slope = half + 0.5 * v * (1.0 - t * t) * c * (1.0 + 3.0 * 0.044715 * vv)
    return value, slope


def kernel(
    n_row, n_rep, places_ref, feats_ref, vals_ref, w_in_ref, w_out_ref, cot_ref,
    upd_ref, grad_ref,
    cols_ref, spread_ref, ext, marks, vals, vals_t, dense_t, w1_in, w1_out, w2_in, w2_out, cot, cot_full, agg, agg_full, hid, gp, gh,
    adj_p, out_p, adj_in, out_in, adj, c_send, c_sib, c_nbr, f_relay, c_relay,
    loc_sem, f_send, f_recv, w_send, w_recv, a_send, a_recv, c_sends, c_recvs, b_sends, b_recvs,
):
    r, z = lax.axis_index("row"), lax.axis_index("rep")
    k = lax.rem(r, 2)
    sib = r + 1 - 2 * k
    z1, z2 = lax.rem(z, 2), lax.div(z, 2)
    mate = z + 1 - 2 * z1
    peers = [z + 2 - 4 * z2, n_rep - 1 - z, mate]
    bit2, bit4 = lax.rem(lax.div(r, 2), 2), lax.rem(lax.div(r, 4), 2)
    near, far = r + 2 - 4 * bit2, r + 4 - 8 * bit4
    rows, quarter = cot.shape
    half = rows // 2
    part = half // PARTS
    width = quarter // WIDE
    slots, row_blocks = cols_ref.shape
    feat, hidw = w1_in.shape
    has_up, has_dn = r + 2 < n_row, r >= 2
    turning, passing = bit2 != bit4, bit2 == bit4
    turn_up, turn_dn = jnp.logical_and(turning, bit2 == 1), jnp.logical_and(turning, bit2 == 0)
    straight_up = jnp.logical_and(has_up, jnp.logical_not(turn_up))
    straight_dn = jnp.logical_and(has_dn, jnp.logical_not(turn_dn))
    hb = row_blocks // 2
    first = (r - 2) * row_blocks

    def remote(src, dst, send, recv, dev):
        return pltpu.make_async_remote_copy(
            src_ref=src, dst_ref=dst, send_sem=send, recv_sem=recv, device_id=dev, device_id_type=MESH
        )

    def panel(ref, slot):
        return ref.at[pl.ds(slot * row_blocks, row_blocks)]

    def half_part(ref, s, c, count=1):
        start = pl.multiple_of(s * half + c * part, part)
        return ref.at[pl.ds(start, count * part)]

    barrier = pltpu.get_barrier_semaphore()
    for zp in peers:
        pl.semaphore_signal(barrier, inc=1, device_id=(r, zp), device_id_type=MESH)
    pl.semaphore_signal(barrier, inc=1, device_id=(sib, z), device_id_type=MESH)
    pl.semaphore_signal(barrier, inc=1, device_id=(far, z), device_id_type=MESH)

    @pl.when(has_up)
    def _():
        pl.semaphore_signal(barrier, inc=1, device_id=(r + 2, z), device_id_type=MESH)

    @pl.when(has_dn)
    def _():
        pl.semaphore_signal(barrier, inc=1, device_id=(r - 2, z), device_id_type=MESH)

    columns = pl.ds(pl.multiple_of(z * quarter, quarter), quarter)
    own_copy = pltpu.make_async_copy(feats_ref.at[:, :, columns], panel(ext, 2), loc_sem.at[0])
    loads = [
        pltpu.make_async_copy(src, dst, loc_sem.at[1 + i])
        for i, (src, dst) in enumerate(
            (
                (vals_ref, vals),
                (places_ref, cols_ref),
                (places_ref, spread_ref),
                (half_part(cot_ref, z1, 0, PARTS), cot_full.at[z]),
                (w_in_ref, w1_in),
                (w_out_ref, w1_out),
                (cot_ref, cot),
            )
        )
    ]
    own_copy.start()
    for copy in loads:
        copy.start()
    own_copy.wait()
    pl.semaphore_wait(barrier, n_rep + 1 + has_up.astype(jnp.int32) + has_dn.astype(jnp.int32))

    own = panel(ext, 2)

    def some(slot, h):
        return ext.at[pl.ds(slot * row_blocks + h * hb, hb)]

    f_up = remote(some(2, 0), some(0, 0), f_send.at[0], f_recv.at[0], (r + 2, z))
    f_dn = remote(some(2, 0), some(4, 0), f_send.at[1], f_recv.at[1], (r - 2, z))
    f_up2 = remote(some(2, 1), some(0, 1), f_send.at[4], f_recv.at[4], (r + 2, z))
    f_dn2 = remote(some(2, 1), some(4, 1), f_send.at[5], f_recv.at[5], (r - 2, z))
    f_out = remote(some(2, 1), f_relay, f_send.at[6], f_recv.at[6], (far, z))
    f_on = remote(f_relay, some(4 - 4 * bit2, 1), f_send.at[7], f_recv.at[5 - bit2], (near, z))
    f_sib = remote(own, panel(ext, 1 + 2 * k), f_send.at[2], f_recv.at[2], (sib, z))
    f_fwd = remote(
        panel(ext, 4 - 4 * k), panel(ext, 3 - 2 * k), f_send.at[3], f_recv.at[3], (sib, z)
    )
    from_dn = [
        remote(some(0, h), some(0, h), f_send.at[4 * h], f_recv.at[4 * h], (r - 2, z))
        for h in range(2)
    ]
    from_up = [
        remote(some(4, h), some(4, h), f_send.at[4 * h + 1], f_recv.at[4 * h + 1], (r + 2, z))
        for h in range(2)
    ]
    from_sib = remote(own, panel(ext, 3 - 2 * k), f_send.at[2], f_recv.at[2], (sib, z))
    from_fwd = remote(own, panel(ext, 1 + 2 * k), f_send.at[3], f_recv.at[3], (sib, z))
    fwd_out = jnp.where(k == 0, r + 2 < n_row, r >= 2)
    fwd_in = jnp.where(k == 0, r >= 2, r + 2 < n_row)

    starts = (
        (turning, f_out), (has_up, f_up), (has_dn, f_dn), (straight_up, f_up2), (straight_dn, f_dn2)
    )
    for ok, copy in starts:
        pl.when(ok)(copy.start)
    f_sib.start()

    eighth = feat // 8

    def span(ref, start, count):
        return ref.at[pl.ds(pl.multiple_of(start * eighth, eighth), count * eighth)]

    def rounds(raw, full, base, bit_a, dev_a, bit_b, dev_b):
        mine = 4 * k + 2 * bit_b + bit_a
        plan = (
            (raw, mine, mine, 1, (r, mate)),
            (full, mine, mine + 1 - 2 * bit_a, 1, (dev_a, z)),
            (full, 4 * k + 2 * bit_b, 4 * k + 2 - 2 * bit_b, 2, (dev_b, z)),
            (full, 4 * k, 4 - 4 * k, 4, (sib, z)),
        )
        sent, got = [], []
        for i, (src, lo, there, count, dev) in enumerate(plan):
            sems = (w_send.at[base + i], w_recv.at[base + i])
            sent.append(remote(span(src, lo, count), span(full, lo, count), *sems, dev))
            got.append(remote(span(full, there, count), span(full, there, count), *sems, dev))
        return sent, got

    in_sent, in_got = rounds(w_in_ref, w2_in, 0, bit2, near, bit4, far)
    out_sent, out_got = rounds(w_out_ref, w2_out, 4, bit4, far, bit2, near)

    def exchange(src, dst, kind, c, count=1):
        return [
            remote(
                half_part(src, lax.rem(zp, 2), c, count),
                dst.at[z, pl.ds(c * part, count * part)],
                a_send.at[kind, i], a_recv.at[kind, i], (r, zp),
            )
            for i, zp in enumerate(peers)
        ]

    def arrivals(buf, kind, c, count=1):
        views = [buf.at[zf, pl.ds(c * part, count * part)] for zf in peers]
        return [
            remote(v, v, a_send.at[kind, i], a_recv.at[kind, i], (r, zf))
            for i, (v, zf) in enumerate(zip(views, peers))
        ]

    in_sent[0].start()
    out_sent[0].start()
    cot_out = exchange(cot_ref, cot_full, 0, 0, PARTS)
    outer = z1 == z2
    for copy in cot_out[:2]:
        pl.when(jnp.logical_not(outer))(copy.start)

    @pl.when(jnp.logical_not(has_dn))
    def _():
        ext[0:row_blocks] = jnp.zeros((row_blocks, 128, quarter), BF16)

    @pl.when(jnp.logical_not(has_up))
    def _():
        ext[4 * row_blocks : 5 * row_blocks] = jnp.zeros((row_blocks, 128, quarter), BF16)

    @pl.when(r < 1)
    def _():
        ext[row_blocks : 2 * row_blocks] = jnp.zeros((row_blocks, 128, quarter), BF16)

    @pl.when(r + 1 >= n_row)
    def _():
        ext[3 * row_blocks : 4 * row_blocks] = jnp.zeros((row_blocks, 128, quarter), BF16)

    for copy in loads:
        copy.wait()

    def transpose_block(b, carry):
        for s in range(slots):
            vals_t[b, s] = vals[b, s].astype(F32).T.astype(BF16)
        return carry

    lax.fori_loop(0, row_blocks, transpose_block, 0)

    for b in range(row_blocks):
        for s in range(slots):
            col = jnp.broadcast_to(spread_ref[s : s + 1, b : b + 1], (16, 128))
            marks[b * slots + s] = jnp.where(col >= 0, col - first, -1)

    def fill_dense(t, carry):
        at = pl.ds(pl.multiple_of(t * 128, 128), 128)
        for b in range(row_blocks):
            turned = jnp.zeros((8, 16, 128), BF16)
            for s in range(slots):
                keep = jnp.where(marks[b * slots + s] == t, 1.0, 0.0).astype(BF16)[None]
                turned = turned + vals_t[b, s].reshape(8, 16, 128) * keep
            dense_t[at, b * 128 : (b + 1) * 128] = turned.reshape(128, 128)
        return carry

    @pl.when(passing)
    def _():
        f_out.wait_recv()
        f_on.start()

    in_sent[0].wait_send()
    out_sent[0].wait_send()
    for copy in cot_out[:2]:
        pl.when(outer)(copy.start)
    cot_out[2].start()
    out_got[0].wait_recv()
    out_sent[1].start()
    in_got[0].wait_recv()

    @pl.when(has_dn)
    def _():
        for copy in from_dn:
            copy.wait_recv()

    @pl.when(has_up)
    def _():
        for copy in from_up:
            copy.wait_recv()

    @pl.when(fwd_out)
    def _():
        f_fwd.start()

    from_sib.wait_recv()

    @pl.when(fwd_in)
    def _():
        from_fwd.wait_recv()

    def gather(b):
        left, right = [], []
        for s in range(slots):
            col = cols_ref[s, b]
            absent = lax.shift_right_logical(col, 31)
            place = col - first + absent * (1 + first + 2 * row_blocks + b)
            keep = jnp.where(marks[b * slots + s] >= 0, 1.0, 0.0).astype(BF16)[None]
            left.append((vals[b, s].reshape(8, 16, 128) * keep).reshape(128, 128))
            right.append(ext[jnp.minimum(jnp.maximum(place, 0), 5 * row_blocks - 1)])
        res = dot(jnp.concatenate(left, axis=1), jnp.concatenate(right, axis=0))
        agg[b * 128 : (b + 1) * 128, :] = res.astype(BF16)

    agg_out = []
    per_part = part // 128
    for c in range(PARTS):
        for s in range(2):
            for i in range(per_part):
                gather((s * PARTS + c) * per_part + i)
        agg_out.append(exchange(agg, agg_full, 1 + c, c))
        for copy in agg_out[c]:
            copy.start()
    for c in range(PARTS):
        agg_full[z, pl.ds(c * part, part)] = agg[
            pl.ds(pl.multiple_of(z1 * half + c * part, part), part), :
        ]

    in_sent[1].start()
    out_got[1].wait_recv()
    out_sent[2].start()
    cut = 2 * row_blocks
    lax.fori_loop(0, cut, fill_dense, 0)
    in_got[1].wait_recv()
    in_sent[2].start()
    lax.fori_loop(cut, 5 * row_blocks, fill_dense, 0)
    tile = 256

    def grad_part(w_b, base):
        def step(i, carry):
            hc = pl.ds(pl.multiple_of(i * tile, tile), tile)
            to = pl.ds(pl.multiple_of(base + i * tile, tile), tile)
            for c in range(PARTS):
                rs = pl.ds(c * part, part)
                g = jnp.concatenate([cot_full[q, rs] for q in range(n_rep)], axis=1)
                gh[rs, to] = dot(g, w_b[:, hc])
            return carry

        lax.fori_loop(0, hidw // tile, step, 0)

    def hidden_part(w_a, base, c):
        rs = pl.ds(c * part, part)

        def step(i, carry):
            hc = pl.ds(pl.multiple_of(i * tile, tile), tile)
            to = pl.ds(pl.multiple_of(base + i * tile, tile), tile)
            x = jnp.concatenate([agg_full[q, rs] for q in range(n_rep)], axis=1)
            value, slope = gelu_pair(dot(x, w_a[:, hc]))
            hid[rs, to] = value.astype(BF16)
            gp[rs, to] = (gh[rs, to] * slope).astype(BF16)
            return carry

        lax.fori_loop(0, hidw // tile, step, 0)

    def product(src, w_a, w_b, zq, c):
        at = pl.ds(pl.multiple_of(zq * quarter, quarter), quarter)
        rs = pl.ds(c * part, part)
        res = dot(src[rs, :hidw], w_a[at, :], ((1,), (1,)))
        res = res + dot(src[rs, hidw:], w_b[at, :], ((1,), (1,)))
        return res.astype(BF16)

    def adj_copies(f, c):
        kind = 1 + PARTS + f * PARTS + c
        rs = pl.ds(c * part, part)
        return [
            remote(
                adj_p.at[zp, f, rs], adj_in.at[z, f, rs],
                a_send.at[kind, i], a_recv.at[kind, i], (r, zp),
            )
            for i, zp in enumerate(peers)
        ]

    def adj_arrivals(f, c):
        kind = 1 + PARTS + f * PARTS + c
        views = [adj_in.at[zf, f, pl.ds(c * part, part)] for zf in peers]
        return [
            remote(v, v, a_send.at[kind, i], a_recv.at[kind, i], (r, zf))
            for i, (v, zf) in enumerate(zip(views, peers))
        ]

    for copy in arrivals(cot_full, 0, 0, PARTS):
        copy.wait_recv()
    grad_part(w1_out, 0)
    out_got[2].wait_recv()
    out_sent[3].start()
    in_got[2].wait_recv()
    in_sent[3].start()
    out_got[3].wait_recv()
    grad_part(w2_out, hidw)
    in_got[3].wait_recv()
    adj_sent = [[adj_copies(f, c) for c in range(PARTS)] for f in range(WIDE)]
    for c in range(PARTS):
        for copy in arrivals(agg_full, 1 + c, c):
            copy.wait_recv()
        hidden_part(w1_in, 0, c)
        hidden_part(w2_in, hidw, c)
        rs = pl.ds(c * part, part)
        for i, zp in enumerate(peers + [z]):
            res = product(gp, w1_in, w2_in, zp, c)
            made = adj_p if i < n_rep - 1 else adj_in
            for f in range(WIDE):
                made[zp, f, rs] = res[:, f * width : (f + 1) * width]
            if i < n_rep - 1:
                adj_sent[0][c][i].start()

    out_sends = []
    for c in range(PARTS):
        rs = pl.ds(c * part, part)
        kind = 1 + (1 + WIDE) * PARTS + c
        for i, zp in enumerate(peers):
            out_p[zp, rs] = product(hid, w1_out, w2_out, zp, c)
            out_sends.append(
                remote(
                    out_p.at[zp, rs], out_in.at[z, rs],
                    a_send.at[kind, i], a_recv.at[kind, i], (r, zp),
                )
            )
        out_in[z, rs] = product(hid, w1_out, w2_out, z, c)

    tile = 256
    plain_to, helped_to = r - 2 + 4 * k, r + 2 - 4 * k
    plain_ok, helped_ok = fwd_in, fwd_out
    turn_plain = jnp.logical_and(turning, k == bit2)
    turn_helped = jnp.logical_and(turning, k != bit2)
    p5_sent = []

    def turn(f):
        for c in range(PARTS):
            for copy in adj_arrivals(f, c):
                copy.wait_recv()
        for s in range(2):
            total = adj_in[s, f].astype(F32)
            for q in range(s + 2, n_rep, 2):
                total = total + adj_in[q, f].astype(F32)
            adj[f, s * half : (s + 1) * half] = total.astype(BF16)

        def put(p, slot):
            def step(m, carry):
                at = pl.ds(pl.multiple_of(m * tile, tile), tile)
                c_send[4 * f + slot, at, :] = piece(f, p, m).astype(BF16)
                return carry

            lax.fori_loop(0, rows // tile, step, 0)

        def cross(slot, dst, got, dev):
            return remote(
                c_send.at[4 * f + slot], dst, c_sends.at[4 * f + slot], c_recvs.at[4 * f + got], dev
            )

        c_help = cross(0, c_sib.at[2 * f], 0, (sib, z))
        c_own = cross(1, c_sib.at[2 * f + 1], 1, (sib, z))
        top, low = pl.ds(0, rows // 2), pl.ds(rows // 2, rows // 2)

        def sides(slot, nbr, dev):
            return (
                remote(
                    c_send.at[4 * f + slot, top], c_nbr.at[2 * f + nbr, top],
                    c_sends.at[4 * f + slot], c_recvs.at[4 * f + 2 + nbr], dev,
                ),
                remote(
                    c_send.at[4 * f + slot, low], c_nbr.at[2 * f + nbr, low],
                    b_sends.at[4 * f + slot], b_recvs.at[4 * f + 2 + nbr], dev,
                ),
            )

        c_plain = sides(2, 1 - k, (plain_to, z))
        c_helped = sides(3, k, (helped_to, z))
        c_out = remote(
            c_send.at[4 * f + jnp.where(k == bit2, 2, 3), low], c_relay.at[f],
            b_sends.at[4 * f], b_recvs.at[4 * f], (far, z),
        )
        c_on = remote(
            c_relay.at[f], c_nbr.at[2 * f + 1 - bit2, low],
            b_sends.at[4 * f + 1], b_recvs.at[4 * f + 3 - bit2], (near, z),
        )
        moves = (
            (plain_ok, c_plain[0]), (jnp.logical_and(plain_ok, jnp.logical_not(turn_plain)), c_plain[1]),
            (helped_ok, c_helped[0]),
            (jnp.logical_and(helped_ok, jnp.logical_not(turn_helped)), c_helped[1]),
            (turning, c_out), (passing, c_on),
        )
        put(4 * k, 2)
        pl.when(turn_plain)(c_out.start)
        for ok, copy in moves[:2]:
            pl.when(ok)(copy.start)
        put(1 + 2 * k, 0)
        c_help.start()
        c_help.wait_recv()

        def add_help(m, carry):
            at = pl.ds(pl.multiple_of(m * tile, tile), tile)
            total = piece(f, 4 - 4 * k, m) + c_sib[2 * f, at, :].astype(F32)
            c_send[4 * f + 3, at, :] = total.astype(BF16)
            return carry

        lax.fori_loop(0, rows // tile, add_help, 0)

        pl.when(turn_helped)(c_out.start)
        for ok, copy in moves[2:4]:
            pl.when(ok)(copy.start)
        @pl.when(passing)
        def _():
            c_out.wait_recv()
            c_on.start()

        put(3 - 2 * k, 1)
        c_own.start()

        p5_sent.append((c_help, c_own, moves))

    def piece(f, p, m):
        at = pl.ds(pl.multiple_of(p * rows + m * tile, tile), tile)
        return dot(dense_t[at, :], adj[f])

    def finish(f):
        p5_sent[f][1].wait_recv()

        def landed(nbr, dev):
            for h, sems in enumerate((c_recvs, b_recvs)):
                ref = c_nbr.at[2 * f + nbr, pl.ds(h * (rows // 2), rows // 2)]
                remote(ref, ref, c_sends.at[4 * f + 2], sems.at[4 * f + 2 + nbr], (dev, z)).wait_recv()

        @pl.when(has_dn)
        def _():
            landed(0, r - 2)

        @pl.when(jnp.logical_not(has_dn))
        def _():
            c_nbr[2 * f] = jnp.zeros((rows, width), BF16)

        @pl.when(has_up)
        def _():
            landed(1, r + 2)

        @pl.when(jnp.logical_not(has_up))
        def _():
            c_nbr[2 * f + 1] = jnp.zeros((rows, width), BF16)

        cs = slice(f * width, (f + 1) * width)

        def step(m, carry):
            at = pl.ds(pl.multiple_of(m * tile, tile), tile)
            total = piece(f, 2, m) + c_sib[2 * f + 1, at, :].astype(F32)
            total = total + c_nbr[2 * f, at, :].astype(F32) + c_nbr[2 * f + 1, at, :].astype(F32)
            grad_ref[at, cs] = (cot[at, cs].astype(F32) + total).astype(BF16)
            return carry

        lax.fori_loop(0, rows // tile, step, 0)

    for f in range(WIDE):
        for copies in adj_sent[f]:
            for copy in copies:
                copy.wait_send()
        following = sum(adj_sent[f + 1], []) if f + 1 < WIDE else out_sends
        for copy in following:
            copy.start()
        turn(f)
    for f in range(WIDE):
        finish(f)
    for c in range(PARTS):
        for copy in arrivals(out_in, 1 + (1 + WIDE) * PARTS + c, c):
            copy.wait_recv()
        rs = pl.ds(c * part, part)
        for s in range(2):
            total = out_in[s, rs].astype(F32)
            for q in range(s + 2, n_rep, 2):
                total = total + out_in[q, rs].astype(F32)
            start, count = 2 * row_blocks + s * row_blocks // 2 + c * per_part, per_part
            mine = ext[start : start + count].reshape(part, quarter)
            at = pl.ds(s * half + c * part, part)
            upd_ref[at] = (mine.astype(F32) + total).astype(BF16)

    for copy in cot_out + in_sent[1:] + out_sent[1:] + agg_out[0] + agg_out[1] + out_sends + [f_sib]:
        copy.wait_send()
    late = list(starts) + [(fwd_out, f_fwd), (passing, f_on)]
    for c_help, c_own, moves in p5_sent:
        c_help.wait_send()
        c_own.wait_send()
        late += list(moves)
    for ok, copy in late:
        pl.when(ok)(copy.wait_send)


def settle(upd_ref, grad_ref, upd_out, grad_out, sems):
    size = upd_ref.shape[0] // CUTS
    copies = [
        pltpu.make_async_copy(
            src.at[pl.ds(i * size, size)], dst.at[pl.ds(i * size, size)], sems.at[j, i]
        )
        for j, (src, dst) in enumerate(((upd_ref, upd_out), (grad_ref, grad_out)))
        for i in range(CUTS)
    ]
    for copy in copies:
        copy.start()
    for copy in copies:
        copy.wait()


def body(n_row, n_rep, node_feats, block_cols, block_vals, w_in, w_out, cotangent):
    rows, quarter = cotangent.shape
    row_blocks, slots = block_cols.shape
    feat, hidw = w_in.shape
    half = rows // 2
    kinds = 1 + (2 + WIDE) * PARTS
    width = quarter // WIDE
    vmem = pl.BlockSpec(memory_space=pltpu.VMEM)
    anywhere = pl.BlockSpec(memory_space=pl.ANY)
    dma = pltpu.SemaphoreType.DMA
    made = pl.pallas_call(
        functools.partial(kernel, n_row, n_rep),
        out_shape=(pltpu.VMEM((rows, quarter), BF16),) * 2,
        in_specs=[anywhere] * 6,
        out_specs=(vmem, vmem),
        scratch_shapes=[
            pltpu.SMEM((slots, row_blocks), jnp.int32),
            pltpu.VMEM((slots, row_blocks), jnp.int32),
            pltpu.VMEM((5 * row_blocks, 128, quarter), BF16),
            pltpu.VMEM((row_blocks * slots, 16, 128), jnp.int32),
            pltpu.VMEM((row_blocks, slots, 128, 128), BF16),
            pltpu.VMEM((row_blocks, slots, 128, 128), BF16),
            pltpu.VMEM((5 * rows, rows), BF16),
            pltpu.VMEM((feat, hidw), BF16),
            pltpu.VMEM((feat, hidw), BF16),
            pltpu.VMEM((feat, hidw), BF16),
            pltpu.VMEM((feat, hidw), BF16),
            pltpu.VMEM((rows, quarter), BF16),
            pltpu.VMEM((n_rep, half, quarter), BF16),
            pltpu.VMEM((rows, quarter), BF16),
            pltpu.VMEM((n_rep, half, quarter), BF16),
            pltpu.VMEM((half, 2 * hidw), BF16),
            pltpu.VMEM((half, 2 * hidw), BF16),
            pltpu.VMEM((half, 2 * hidw), F32),
            pltpu.VMEM((n_rep, WIDE, half, width), BF16),
            pltpu.VMEM((n_rep, half, quarter), BF16),
            pltpu.VMEM((n_rep, WIDE, half, width), BF16),
            pltpu.VMEM((n_rep, half, quarter), BF16),
            pltpu.VMEM((WIDE, rows, width), BF16),
            pltpu.VMEM((4 * WIDE, rows, width), BF16),
            pltpu.VMEM((2 * WIDE, rows, width), BF16),
            pltpu.VMEM((2 * WIDE, rows, width), BF16),
            pltpu.VMEM((row_blocks // 2, 128, quarter), BF16),
            pltpu.VMEM((WIDE, rows // 2, width), BF16),
            dma((8,)),
            dma((8,)),
            dma((8,)),
            dma((8,)),
            dma((8,)),
            dma((kinds, n_rep - 1)),
            dma((kinds, n_rep - 1)),
            dma((4 * WIDE,)),
            dma((4 * WIDE,)),
            dma((4 * WIDE,)),
            dma((4 * WIDE,)),
        ],
        compiler_params=pltpu.CompilerParams(
            collective_id=0, has_side_effects=True, vmem_limit_bytes=56 * 1024 * 1024
        ),
    )(block_cols.T, node_feats.reshape(row_blocks, 128, feat), block_vals, w_in, w_out, cotangent)
    return pl.pallas_call(
        settle,
        out_shape=(jax.ShapeDtypeStruct((rows, quarter), BF16),) * 2,
        in_specs=[vmem] * 2,
        out_specs=(anywhere,) * 2,
        scratch_shapes=[dma((2, CUTS))],
    )(*(pltpu.with_memory_space_constraint(m, pltpu.VMEM) for m in made))


def solution(mesh):
    in_specs = (
        P("row", None),
        P("row", None),
        P("row", None, None, None),
        P(None, "rep"),
        P(None, "rep"),
        P("row", "rep"),
    )
    out_specs = (P("row", "rep"), P("row", "rep"))
    run = functools.partial(body, mesh.shape["row"], mesh.shape["rep"])
    return jax.shard_map(run, mesh=mesh, in_specs=in_specs, out_specs=out_specs, check_vma=False)
```

```python
import functools

import jax
import jax.numpy as jnp
from jax import lax
from jax.experimental import pallas as pl
from jax.experimental.pallas import tpu as pltpu
from jax.sharding import PartitionSpec as P

F32 = jnp.float32
BF16 = jnp.bfloat16
MESH = pl.DeviceIdType.MESH
PARTS = 2
WIDE = 2
CUTS = 4


def dot(a, b, dims=((1,), (0,))):
    return lax.dot_general(a, b, (dims, ((), ())), preferred_element_type=F32)


def gelu_pair(v):
    c = 0.7978845608
    vv = v * v
    t = jnp.tanh(c * (v + 0.044715 * v * vv))
    half = 0.5 * (1.0 + t)
    value = v * half
    slope = half + 0.5 * v * (1.0 - t * t) * c * (1.0 + 3.0 * 0.044715 * vv)
    return value, slope


def kernel(
    n_row, n_rep, places_ref, feats_ref, vals_ref, w_in_ref, w_out_ref, cot_ref,
    upd_ref, grad_ref,
    cols_ref, spread_ref, ext, marks, vals, vals_t, dense_t, w1_in, w1_out, w2_in, w2_out, cot, cot_full, agg, agg_full, hid, gp, gh,
    adj_p, out_p, adj_in, out_in, adj, c_send, c_sib, c_nbr, f_relay, c_relay,
    loc_sem, f_send, f_recv, w_send, w_recv, a_send, a_recv, c_sends, c_recvs, b_sends, b_recvs,
):
    r, z = lax.axis_index("row"), lax.axis_index("rep")
    k = lax.rem(r, 2)
    sib = r + 1 - 2 * k
    z1, z2 = lax.rem(z, 2), lax.div(z, 2)
    mate = z + 1 - 2 * z1
    peers = [z + 2 - 4 * z2, n_rep - 1 - z, mate]
    bit2, bit4 = lax.rem(lax.div(r, 2), 2), lax.rem(lax.div(r, 4), 2)
    near, far = r + 2 - 4 * bit2, r + 4 - 8 * bit4
    rows, quarter = cot.shape
    half = rows // 2
    part = half // PARTS
    width = quarter // WIDE
    slots, row_blocks = cols_ref.shape
    feat, hidw = w1_in.shape
    has_up, has_dn = r + 2 < n_row, r >= 2
    turning, passing = bit2 != bit4, bit2 == bit4
    turn_up, turn_dn = jnp.logical_and(turning, bit2 == 1), jnp.logical_and(turning, bit2 == 0)
    straight_up = jnp.logical_and(has_up, jnp.logical_not(turn_up))
    straight_dn = jnp.logical_and(has_dn, jnp.logical_not(turn_dn))
    hb = row_blocks // 2
    first = (r - 2) * row_blocks

    def remote(src, dst, send, recv, dev):
        return pltpu.make_async_remote_copy(
            src_ref=src, dst_ref=dst, send_sem=send, recv_sem=recv, device_id=dev, device_id_type=MESH
        )

    def panel(ref, slot):
        return ref.at[pl.ds(slot * row_blocks, row_blocks)]

    def half_part(ref, s, c, count=1):
        start = pl.multiple_of(s * half + c * part, part)
        return ref.at[pl.ds(start, count * part)]

    barrier = pltpu.get_barrier_semaphore()
    for zp in peers:
        pl.semaphore_signal(barrier, inc=1, device_id=(r, zp), device_id_type=MESH)
    pl.semaphore_signal(barrier, inc=1, device_id=(sib, z), device_id_type=MESH)
    pl.semaphore_signal(barrier, inc=1, device_id=(far, z), device_id_type=MESH)

    @pl.when(has_up)
    def _():
        pl.semaphore_signal(barrier, inc=1, device_id=(r + 2, z), device_id_type=MESH)

    @pl.when(has_dn)
    def _():
        pl.semaphore_signal(barrier, inc=1, device_id=(r - 2, z), device_id_type=MESH)

    columns = pl.ds(pl.multiple_of(z * quarter, quarter), quarter)
    own_copy = pltpu.make_async_copy(feats_ref.at[:, :, columns], panel(ext, 2), loc_sem.at[0])
    loads = [
        pltpu.make_async_copy(src, dst, loc_sem.at[1 + i])
        for i, (src, dst) in enumerate(
            (
                (vals_ref, vals),
                (places_ref, cols_ref),
                (places_ref, spread_ref),
                (half_part(cot_ref, z1, 0, PARTS), cot_full.at[z]),
                (w_in_ref, w1_in),
                (w_out_ref, w1_out),
                (cot_ref, cot),
            )
        )
    ]
    own_copy.start()
    for copy in loads:
        copy.start()
    own_copy.wait()
    pl.semaphore_wait(barrier, n_rep + 1 + has_up.astype(jnp.int32) + has_dn.astype(jnp.int32))

    own = panel(ext, 2)

    def some(slot, h):
        return ext.at[pl.ds(slot * row_blocks + h * hb, hb)]

    f_up = remote(some(2, 0), some(0, 0), f_send.at[0], f_recv.at[0], (r + 2, z))
    f_dn = remote(some(2, 0), some(4, 0), f_send.at[1], f_recv.at[1], (r - 2, z))
    f_up2 = remote(some(2, 1), some(0, 1), f_send.at[4], f_recv.at[4], (r + 2, z))
    f_dn2 = remote(some(2, 1), some(4, 1), f_send.at[5], f_recv.at[5], (r - 2, z))
    f_out = remote(some(2, 1), f_relay, f_send.at[6], f_recv.at[6], (far, z))
    f_on = remote(f_relay, some(4 - 4 * bit2, 1), f_send.at[7], f_recv.at[5 - bit2], (near, z))
    f_sib = remote(own, panel(ext, 1 + 2 * k), f_send.at[2], f_recv.at[2], (sib, z))
    f_fwd = remote(
        panel(ext, 4 - 4 * k), panel(ext, 3 - 2 * k), f_send.at[3], f_recv.at[3], (sib, z)
    )
    from_dn = [
        remote(some(0, h), some(0, h), f_send.at[4 * h], f_recv.at[4 * h], (r - 2, z))
        for h in range(2)
    ]
    from_up = [
        remote(some(4, h), some(4, h), f_send.at[4 * h + 1], f_recv.at[4 * h + 1], (r + 2, z))
        for h in range(2)
    ]
    from_sib = remote(own, panel(ext, 3 - 2 * k), f_send.at[2], f_recv.at[2], (sib, z))
    from_fwd = remote(own, panel(ext, 1 + 2 * k), f_send.at[3], f_recv.at[3], (sib, z))
    fwd_out = jnp.where(k == 0, r + 2 < n_row, r >= 2)
    fwd_in = jnp.where(k == 0, r >= 2, r + 2 < n_row)

    starts = (
        (turning, f_out), (has_up, f_up), (has_dn, f_dn), (straight_up, f_up2), (straight_dn, f_dn2)
    )
    for ok, copy in starts:
        pl.when(ok)(copy.start)
    f_sib.start()

    eighth = feat // 8

    def span(ref, start, count):
        return ref.at[pl.ds(pl.multiple_of(start * eighth, eighth), count * eighth)]

    def rounds(raw, full, base, bit_a, dev_a, bit_b, dev_b):
        mine = 4 * k + 2 * bit_b + bit_a
        plan = (
            (raw, mine, mine, 1, (r, mate)),
            (full, mine, mine + 1 - 2 * bit_a, 1, (dev_a, z)),
            (full, 4 * k + 2 * bit_b, 4 * k + 2 - 2 * bit_b, 2, (dev_b, z)),
            (full, 4 * k, 4 - 4 * k, 4, (sib, z)),
        )
        sent, got = [], []
        for i, (src, lo, there, count, dev) in enumerate(plan):
            sems = (w_send.at[base + i], w_recv.at[base + i])
            sent.append(remote(span(src, lo, count), span(full, lo, count), *sems, dev))
            got.append(remote(span(full, there, count), span(full, there, count), *sems, dev))
        return sent, got

    in_sent, in_got = rounds(w_in_ref, w2_in, 0, bit2, near, bit4, far)
    out_sent, out_got = rounds(w_out_ref, w2_out, 4, bit4, far, bit2, near)

    def exchange(src, dst, kind, c, count=1):
        return [
            remote(
                half_part(src, lax.rem(zp, 2), c, count),
                dst.at[z, pl.ds(c * part, count * part)],
                a_send.at[kind, i], a_recv.at[kind, i], (r, zp),
            )
            for i, zp in enumerate(peers)
        ]

    def arrivals(buf, kind, c, count=1):
        views = [buf.at[zf, pl.ds(c * part, count * part)] for zf in peers]
        return [
            remote(v, v, a_send.at[kind, i], a_recv.at[kind, i], (r, zf))
            for i, (v, zf) in enumerate(zip(views, peers))
        ]

    in_sent[0].start()
    out_sent[0].start()
    cot_out = exchange(cot_ref, cot_full, 0, 0, PARTS)
    outer = z1 == z2
    for copy in cot_out[:2]:
        pl.when(jnp.logical_not(outer))(copy.start)

    @pl.when(jnp.logical_not(has_dn))
    def _():
        ext[0:row_blocks] = jnp.zeros((row_blocks, 128, quarter), BF16)

    @pl.when(jnp.logical_not(has_up))
    def _():
        ext[4 * row_blocks : 5 * row_blocks] = jnp.zeros((row_blocks, 128, quarter), BF16)

    @pl.when(r < 1)
    def _():
        ext[row_blocks : 2 * row_blocks] = jnp.zeros((row_blocks, 128, quarter), BF16)

    @pl.when(r + 1 >= n_row)
    def _():
        ext[3 * row_blocks : 4 * row_blocks] = jnp.zeros((row_blocks, 128, quarter), BF16)

    for copy in loads:
        copy.wait()

    def transpose_block(b, carry):
        for s in range(slots):
            vals_t[b, s] = vals[b, s].astype(F32).T.astype(BF16)
        return carry

    lax.fori_loop(0, row_blocks, transpose_block, 0)

    for b in range(row_blocks):
        for s in range(slots):
            col = jnp.broadcast_to(spread_ref[s : s + 1, b : b + 1], (16, 128))
            marks[b * slots + s] = jnp.where(col >= 0, col - first, -1)

    def fill_dense(t, carry):
        at = pl.ds(pl.multiple_of(t * 128, 128), 128)
        for b in range(row_blocks):
            turned = jnp.zeros((8, 16, 128), BF16)
            for s in range(slots):
                keep = jnp.where(marks[b * slots + s] == t, 1.0, 0.0).astype(BF16)[None]
                turned = turned + vals_t[b, s].reshape(8, 16, 128) * keep
            dense_t[at, b * 128 : (b + 1) * 128] = turned.reshape(128, 128)
        return carry

    @pl.when(passing)
    def _():
        f_out.wait_recv()
        f_on.start()

    in_sent[0].wait_send()
    out_sent[0].wait_send()
    for copy in cot_out[:2]:
        pl.when(outer)(copy.start)
    cot_out[2].start()
    out_got[0].wait_recv()
    out_sent[1].start()
    in_got[0].wait_recv()

    @pl.when(has_dn)
    def _():
        for copy in from_dn:
            copy.wait_recv()

    @pl.when(has_up)
    def _():
        for copy in from_up:
            copy.wait_recv()

    @pl.when(fwd_out)
    def _():
        f_fwd.start()

    from_sib.wait_recv()

    @pl.when(fwd_in)
    def _():
        from_fwd.wait_recv()

    def gather(b):
        left, right = [], []
        for s in range(slots):
            col = cols_ref[s, b]
            absent = lax.shift_right_logical(col, 31)
            place = col - first + absent * (1 + first + 2 * row_blocks + b)
            keep = jnp.where(marks[b * slots + s] >= 0, 1.0, 0.0).astype(BF16)[None]
            left.append((vals[b, s].reshape(8, 16, 128) * keep).reshape(128, 128))
            right.append(ext[jnp.minimum(jnp.maximum(place, 0), 5 * row_blocks - 1)])
        res = dot(jnp.concatenate(left, axis=1), jnp.concatenate(right, axis=0))
        agg[b * 128 : (b + 1) * 128, :] = res.astype(BF16)

    agg_out = []
    per_part = part // 128
    for c in range(PARTS):
        for s in range(2):
            for i in range(per_part):
                gather((s * PARTS + c) * per_part + i)
        agg_out.append(exchange(agg, agg_full, 1 + c, c))
        for copy in agg_out[c]:
            copy.start()
    for c in range(PARTS):
        agg_full[z, pl.ds(c * part, part)] = agg[
            pl.ds(pl.multiple_of(z1 * half + c * part, part), part), :
        ]

    in_sent[1].start()
    out_got[1].wait_recv()
    out_sent[2].start()
    cut = 2 * row_blocks
    lax.fori_loop(0, cut, fill_dense, 0)
    in_got[1].wait_recv()
    in_sent[2].start()
    lax.fori_loop(cut, 5 * row_blocks, fill_dense, 0)
    tile = 512

    def grad_part(w_b, base):
        def step(i, carry):
            hc = pl.ds(pl.multiple_of(i * tile, tile), tile)
            to = pl.ds(pl.multiple_of(base + i * tile, tile), tile)
            for c in range(PARTS):
                rs = pl.ds(c * part, part)
                g = jnp.concatenate([cot_full[q, rs] for q in range(n_rep)], axis=1)
                gh[rs, to] = dot(g, w_b[:, hc])
            return carry

        lax.fori_loop(0, hidw // tile, step, 0)

    def hidden_part(w_a, base, c):
        rs = pl.ds(c * part, part)

        def step(i, carry):
            hc = pl.ds(pl.multiple_of(i * tile, tile), tile)
            to = pl.ds(pl.multiple_of(base + i * tile, tile), tile)
            x = jnp.concatenate([agg_full[q, rs] for q in range(n_rep)], axis=1)
            value, slope = gelu_pair(dot(x, w_a[:, hc]))
            hid[rs, to] = value.astype(BF16)
            gp[rs, to] = (gh[rs, to] * slope).astype(BF16)
            return carry

        lax.fori_loop(0, hidw // tile, step, 0)

    def product(src, w_a, w_b, zq, c):
        at = pl.ds(pl.multiple_of(zq * quarter, quarter), quarter)
        rs = pl.ds(c * part, part)
        res = dot(src[rs, :hidw], w_a[at, :], ((1,), (1,)))
        res = res + dot(src[rs, hidw:], w_b[at, :], ((1,), (1,)))
        return res.astype(BF16)

    def adj_copies(f, c):
        kind = 1 + PARTS + f * PARTS + c
        rs = pl.ds(c * part, part)
        return [
            remote(
                adj_p.at[zp, f, rs], adj_in.at[z, f, rs],
                a_send.at[kind, i], a_recv.at[kind, i], (r, zp),
            )
            for i, zp in enumerate(peers)
        ]

    def adj_arrivals(f, c):
        kind = 1 + PARTS + f * PARTS + c
        views = [adj_in.at[zf, f, pl.ds(c * part, part)] for zf in peers]
        return [
            remote(v, v, a_send.at[kind, i], a_recv.at[kind, i], (r, zf))
            for i, (v, zf) in enumerate(zip(views, peers))
        ]

    for copy in arrivals(cot_full, 0, 0, PARTS):
        copy.wait_recv()
    grad_part(w1_out, 0)
    out_got[2].wait_recv()
    out_sent[3].start()
    in_got[2].wait_recv()
    in_sent[3].start()
    out_got[3].wait_recv()
    grad_part(w2_out, hidw)
    in_got[3].wait_recv()
    adj_sent = [[adj_copies(f, c) for c in range(PARTS)] for f in range(WIDE)]
    for c in range(PARTS):
        for copy in arrivals(agg_full, 1 + c, c):
            copy.wait_recv()
        hidden_part(w1_in, 0, c)
        hidden_part(w2_in, hidw, c)
        rs = pl.ds(c * part, part)
        for i, zp in enumerate(peers + [z]):
            res = product(gp, w1_in, w2_in, zp, c)
            made = adj_p if i < n_rep - 1 else adj_in
            for f in range(WIDE):
                made[zp, f, rs] = res[:, f * width : (f + 1) * width]
            if i < n_rep - 1:
                adj_sent[0][c][i].start()

    out_sends = []
    for c in range(PARTS):
        rs = pl.ds(c * part, part)
        kind = 1 + (1 + WIDE) * PARTS + c
        for i, zp in enumerate(peers):
            out_p[zp, rs] = product(hid, w1_out, w2_out, zp, c)
            out_sends.append(
                remote(
                    out_p.at[zp, rs], out_in.at[z, rs],
                    a_send.at[kind, i], a_recv.at[kind, i], (r, zp),
                )
            )
        out_in[z, rs] = product(hid, w1_out, w2_out, z, c)

    tile = 256
    plain_to, helped_to = r - 2 + 4 * k, r + 2 - 4 * k
    plain_ok, helped_ok = fwd_in, fwd_out
    turn_plain = jnp.logical_and(turning, k == bit2)
    turn_helped = jnp.logical_and(turning, k != bit2)
    p5_sent = []

    def turn(f):
        for c in range(PARTS):
            for copy in adj_arrivals(f, c):
                copy.wait_recv()
        for s in range(2):
            total = adj_in[s, f].astype(F32)
            for q in range(s + 2, n_rep, 2):
                total = total + adj_in[q, f].astype(F32)
            adj[f, s * half : (s + 1) * half] = total.astype(BF16)

        def put(p, slot):
            def step(m, carry):
                at = pl.ds(pl.multiple_of(m * tile, tile), tile)
                c_send[4 * f + slot, at, :] = piece(f, p, m).astype(BF16)
                return carry

            lax.fori_loop(0, rows // tile, step, 0)

        def cross(slot, dst, got, dev):
            return remote(
                c_send.at[4 * f + slot], dst, c_sends.at[4 * f + slot], c_recvs.at[4 * f + got], dev
            )

        c_help = cross(0, c_sib.at[2 * f], 0, (sib, z))
        c_own = cross(1, c_sib.at[2 * f + 1], 1, (sib, z))
        top, low = pl.ds(0, rows // 2), pl.ds(rows // 2, rows // 2)

        def sides(slot, nbr, dev):
            return (
                remote(
                    c_send.at[4 * f + slot, top], c_nbr.at[2 * f + nbr, top],
                    c_sends.at[4 * f + slot], c_recvs.at[4 * f + 2 + nbr], dev,
                ),
                remote(
                    c_send.at[4 * f + slot, low], c_nbr.at[2 * f + nbr, low],
                    b_sends.at[4 * f + slot], b_recvs.at[4 * f + 2 + nbr], dev,
                ),
            )

        c_plain = sides(2, 1 - k, (plain_to, z))
        c_helped = sides(3, k, (helped_to, z))
        c_out = remote(
            c_send.at[4 * f + jnp.where(k == bit2, 2, 3), low], c_relay.at[f],
            b_sends.at[4 * f], b_recvs.at[4 * f], (far, z),
        )
        c_on = remote(
            c_relay.at[f], c_nbr.at[2 * f + 1 - bit2, low],
            b_sends.at[4 * f + 1], b_recvs.at[4 * f + 3 - bit2], (near, z),
        )
        moves = (
            (plain_ok, c_plain[0]), (jnp.logical_and(plain_ok, jnp.logical_not(turn_plain)), c_plain[1]),
            (helped_ok, c_helped[0]),
            (jnp.logical_and(helped_ok, jnp.logical_not(turn_helped)), c_helped[1]),
            (turning, c_out), (passing, c_on),
        )
        put(4 * k, 2)
        pl.when(turn_plain)(c_out.start)
        for ok, copy in moves[:2]:
            pl.when(ok)(copy.start)
        put(1 + 2 * k, 0)
        c_help.start()
        c_help.wait_recv()

        def add_help(m, carry):
            at = pl.ds(pl.multiple_of(m * tile, tile), tile)
            total = piece(f, 4 - 4 * k, m) + c_sib[2 * f, at, :].astype(F32)
            c_send[4 * f + 3, at, :] = total.astype(BF16)
            return carry

        lax.fori_loop(0, rows // tile, add_help, 0)

        pl.when(turn_helped)(c_out.start)
        for ok, copy in moves[2:4]:
            pl.when(ok)(copy.start)
        @pl.when(passing)
        def _():
            c_out.wait_recv()
            c_on.start()

        put(3 - 2 * k, 1)
        c_own.start()

        p5_sent.append((c_help, c_own, moves))

    def piece(f, p, m):
        at = pl.ds(pl.multiple_of(p * rows + m * tile, tile), tile)
        return dot(dense_t[at, :], adj[f])

    def finish(f):
        p5_sent[f][1].wait_recv()

        def landed(nbr, dev):
            for h, sems in enumerate((c_recvs, b_recvs)):
                ref = c_nbr.at[2 * f + nbr, pl.ds(h * (rows // 2), rows // 2)]
                remote(ref, ref, c_sends.at[4 * f + 2], sems.at[4 * f + 2 + nbr], (dev, z)).wait_recv()

        @pl.when(has_dn)
        def _():
            landed(0, r - 2)

        @pl.when(jnp.logical_not(has_dn))
        def _():
            c_nbr[2 * f] = jnp.zeros((rows, width), BF16)

        @pl.when(has_up)
        def _():
            landed(1, r + 2)

        @pl.when(jnp.logical_not(has_up))
        def _():
            c_nbr[2 * f + 1] = jnp.zeros((rows, width), BF16)

        cs = slice(f * width, (f + 1) * width)

        def step(m, carry):
            at = pl.ds(pl.multiple_of(m * tile, tile), tile)
            total = piece(f, 2, m) + c_sib[2 * f + 1, at, :].astype(F32)
            total = total + c_nbr[2 * f, at, :].astype(F32) + c_nbr[2 * f + 1, at, :].astype(F32)
            grad_ref[at, cs] = (cot[at, cs].astype(F32) + total).astype(BF16)
            return carry

        lax.fori_loop(0, rows // tile, step, 0)

    for f in range(WIDE):
        for copies in adj_sent[f]:
            for copy in copies:
                copy.wait_send()
        following = sum(adj_sent[f + 1], []) if f + 1 < WIDE else out_sends
        for copy in following:
            copy.start()
        turn(f)
    for f in range(WIDE):
        finish(f)
    for c in range(PARTS):
        for copy in arrivals(out_in, 1 + (1 + WIDE) * PARTS + c, c):
            copy.wait_recv()
        rs = pl.ds(c * part, part)
        for s in range(2):
            total = out_in[s, rs].astype(F32)
            for q in range(s + 2, n_rep, 2):
                total = total + out_in[q, rs].astype(F32)
            start, count = 2 * row_blocks + s * row_blocks // 2 + c * per_part, per_part
            mine = ext[start : start + count].reshape(part, quarter)
            at = pl.ds(s * half + c * part, part)
            upd_ref[at] = (mine.astype(F32) + total).astype(BF16)

    for copy in cot_out + in_sent[1:] + out_sent[1:] + agg_out[0] + agg_out[1] + out_sends + [f_sib]:
        copy.wait_send()
    late = list(starts) + [(fwd_out, f_fwd), (passing, f_on)]
    for c_help, c_own, moves in p5_sent:
        c_help.wait_send()
        c_own.wait_send()
        late += list(moves)
    for ok, copy in late:
        pl.when(ok)(copy.wait_send)


def settle(upd_ref, grad_ref, upd_out, grad_out, sems):
    size = upd_ref.shape[0] // CUTS
    copies = [
        pltpu.make_async_copy(
            src.at[pl.ds(i * size, size)], dst.at[pl.ds(i * size, size)], sems.at[j, i]
        )
        for j, (src, dst) in enumerate(((upd_ref, upd_out), (grad_ref, grad_out)))
        for i in range(CUTS)
    ]
    for copy in copies:
        copy.start()
    for copy in copies:
        copy.wait()


def body(n_row, n_rep, node_feats, block_cols, block_vals, w_in, w_out, cotangent):
    rows, quarter = cotangent.shape
    row_blocks, slots = block_cols.shape
    feat, hidw = w_in.shape
    half = rows // 2
    kinds = 1 + (2 + WIDE) * PARTS
    width = quarter // WIDE
    vmem = pl.BlockSpec(memory_space=pltpu.VMEM)
    anywhere = pl.BlockSpec(memory_space=pl.ANY)
    dma = pltpu.SemaphoreType.DMA
    made = pl.pallas_call(
        functools.partial(kernel, n_row, n_rep),
        out_shape=(pltpu.VMEM((rows, quarter), BF16),) * 2,
        in_specs=[anywhere] * 6,
        out_specs=(vmem, vmem),
        scratch_shapes=[
            pltpu.SMEM((slots, row_blocks), jnp.int32),
            pltpu.VMEM((slots, row_blocks), jnp.int32),
            pltpu.VMEM((5 * row_blocks, 128, quarter), BF16),
            pltpu.VMEM((row_blocks * slots, 16, 128), jnp.int32),
            pltpu.VMEM((row_blocks, slots, 128, 128), BF16),
            pltpu.VMEM((row_blocks, slots, 128, 128), BF16),
            pltpu.VMEM((5 * rows, rows), BF16),
            pltpu.VMEM((feat, hidw), BF16),
            pltpu.VMEM((feat, hidw), BF16),
            pltpu.VMEM((feat, hidw), BF16),
            pltpu.VMEM((feat, hidw), BF16),
            pltpu.VMEM((rows, quarter), BF16),
            pltpu.VMEM((n_rep, half, quarter), BF16),
            pltpu.VMEM((rows, quarter), BF16),
            pltpu.VMEM((n_rep, half, quarter), BF16),
            pltpu.VMEM((half, 2 * hidw), BF16),
            pltpu.VMEM((half, 2 * hidw), BF16),
            pltpu.VMEM((half, 2 * hidw), F32),
            pltpu.VMEM((n_rep, WIDE, half, width), BF16),
            pltpu.VMEM((n_rep, half, quarter), BF16),
            pltpu.VMEM((n_rep, WIDE, half, width), BF16),
            pltpu.VMEM((n_rep, half, quarter), BF16),
            pltpu.VMEM((WIDE, rows, width), BF16),
            pltpu.VMEM((4 * WIDE, rows, width), BF16),
            pltpu.VMEM((2 * WIDE, rows, width), BF16),
            pltpu.VMEM((2 * WIDE, rows, width), BF16),
            pltpu.VMEM((row_blocks // 2, 128, quarter), BF16),
            pltpu.VMEM((WIDE, rows // 2, width), BF16),
            dma((8,)),
            dma((8,)),
            dma((8,)),
            dma((8,)),
            dma((8,)),
            dma((kinds, n_rep - 1)),
            dma((kinds, n_rep - 1)),
            dma((4 * WIDE,)),
            dma((4 * WIDE,)),
            dma((4 * WIDE,)),
            dma((4 * WIDE,)),
        ],
        compiler_params=pltpu.CompilerParams(
            collective_id=0, has_side_effects=True, vmem_limit_bytes=56 * 1024 * 1024
        ),
    )(block_cols.T, node_feats.reshape(row_blocks, 128, feat), block_vals, w_in, w_out, cotangent)
    return pl.pallas_call(
        settle,
        out_shape=(jax.ShapeDtypeStruct((rows, quarter), BF16),) * 2,
        in_specs=[vmem] * 2,
        out_specs=(anywhere,) * 2,
        scratch_shapes=[dma((2, CUTS))],
    )(*(pltpu.with_memory_space_constraint(m, pltpu.VMEM) for m in made))


def solution(mesh):
    in_specs = (
        P("row", None),
        P("row", None),
        P("row", None, None, None),
        P(None, "rep"),
        P(None, "rep"),
        P("row", "rep"),
    )
    out_specs = (P("row", "rep"), P("row", "rep"))
    run = functools.partial(body, mesh.shape["row"], mesh.shape["rep"])
    return jax.shard_map(run, mesh=mesh, in_specs=in_specs, out_specs=out_specs, check_vma=False)
```

```python
import functools

import jax
import jax.numpy as jnp
from jax import lax
from jax.experimental import pallas as pl
from jax.experimental.pallas import tpu as pltpu
from jax.sharding import PartitionSpec as P

F32 = jnp.float32
BF16 = jnp.bfloat16
MESH = pl.DeviceIdType.MESH
PARTS = 2
WIDE = 2
CUTS = 4


def dot(a, b, dims=((1,), (0,))):
    return lax.dot_general(a, b, (dims, ((), ())), preferred_element_type=F32)


def gelu_pair(v):
    c = 0.7978845608
    vv = v * v
    t = jnp.tanh(c * (v + 0.044715 * v * vv))
    half = 0.5 * (1.0 + t)
    value = v * half
    slope = half + 0.5 * v * (1.0 - t * t) * c * (1.0 + 3.0 * 0.044715 * vv)
    return value, slope


def kernel(
    n_row, n_rep, places_ref, feats_ref, vals_ref, w_in_ref, w_out_ref, cot_ref,
    upd_ref, grad_ref,
    cols_ref, spread_ref, ext, marks, vals, vals_t, dense_t, w1_in, w1_out, w2_in, w2_out, cot, cot_full, agg, agg_full, hid, gp, gh,
    adj_p, out_p, adj_in, out_in, adj, c_send, c_sib, c_nbr, f_relay, c_relay,
    loc_sem, f_send, f_recv, w_send, w_recv, a_send, a_recv, c_sends, c_recvs, b_sends, b_recvs,
):
    r, z = lax.axis_index("row"), lax.axis_index("rep")
    k = lax.rem(r, 2)
    sib = r + 1 - 2 * k
    z1, z2 = lax.rem(z, 2), lax.div(z, 2)
    mate = z + 1 - 2 * z1
    peers = [z + 2 - 4 * z2, n_rep - 1 - z, mate]
    bit2, bit4 = lax.rem(lax.div(r, 2), 2), lax.rem(lax.div(r, 4), 2)
    near, far = r + 2 - 4 * bit2, r + 4 - 8 * bit4
    rows, quarter = cot.shape
    half = rows // 2
    part = half // PARTS
    width = quarter // WIDE
    slots, row_blocks = cols_ref.shape
    feat, hidw = w1_in.shape
    has_up, has_dn = r + 2 < n_row, r >= 2
    turning, passing = bit2 != bit4, bit2 == bit4
    turn_up, turn_dn = jnp.logical_and(turning, bit2 == 1), jnp.logical_and(turning, bit2 == 0)
    straight_up = jnp.logical_and(has_up, jnp.logical_not(turn_up))
    straight_dn = jnp.logical_and(has_dn, jnp.logical_not(turn_dn))
    hb = row_blocks // 2
    first = (r - 2) * row_blocks

    def remote(src, dst, send, recv, dev):
        return pltpu.make_async_remote_copy(
            src_ref=src, dst_ref=dst, send_sem=send, recv_sem=recv, device_id=dev, device_id_type=MESH
        )

    def panel(ref, slot):
        return ref.at[pl.ds(slot * row_blocks, row_blocks)]

    def half_part(ref, s, c, count=1):
        start = pl.multiple_of(s * half + c * part, part)
        return ref.at[pl.ds(start, count * part)]

    barrier = pltpu.get_barrier_semaphore()
    for zp in peers:
        pl.semaphore_signal(barrier, inc=1, device_id=(r, zp), device_id_type=MESH)
    pl.semaphore_signal(barrier, inc=1, device_id=(sib, z), device_id_type=MESH)
    pl.semaphore_signal(barrier, inc=1, device_id=(far, z), device_id_type=MESH)

    @pl.when(has_up)
    def _():
        pl.semaphore_signal(barrier, inc=1, device_id=(r + 2, z), device_id_type=MESH)

    @pl.when(has_dn)
    def _():
        pl.semaphore_signal(barrier, inc=1, device_id=(r - 2, z), device_id_type=MESH)

    columns = pl.ds(pl.multiple_of(z * quarter, quarter), quarter)
    own_copy = pltpu.make_async_copy(feats_ref.at[:, :, columns], panel(ext, 2), loc_sem.at[0])
    loads = [
        pltpu.make_async_copy(src, dst, loc_sem.at[1 + i])
        for i, (src, dst) in enumerate(
            (
                (vals_ref, vals),
                (places_ref, cols_ref),
                (places_ref, spread_ref),
                (half_part(cot_ref, z1, 0, PARTS), cot_full.at[z]),
                (w_in_ref, w1_in),
                (w_out_ref, w1_out),
                (cot_ref, cot),
            )
        )
    ]
    own_copy.start()
    for copy in loads:
        copy.start()
    own_copy.wait()
    pl.semaphore_wait(barrier, n_rep + 1 + has_up.astype(jnp.int32) + has_dn.astype(jnp.int32))

    own = panel(ext, 2)

    def some(slot, h):
        return ext.at[pl.ds(slot * row_blocks + h * hb, hb)]

    f_up = remote(some(2, 0), some(0, 0), f_send.at[0], f_recv.at[0], (r + 2, z))
    f_dn = remote(some(2, 0), some(4, 0), f_send.at[1], f_recv.at[1], (r - 2, z))
    f_up2 = remote(some(2, 1), some(0, 1), f_send.at[4], f_recv.at[4], (r + 2, z))
    f_dn2 = remote(some(2, 1), some(4, 1), f_send.at[5], f_recv.at[5], (r - 2, z))
    f_out = remote(some(2, 1), f_relay, f_send.at[6], f_recv.at[6], (far, z))
    f_on = remote(f_relay, some(4 - 4 * bit2, 1), f_send.at[7], f_recv.at[5 - bit2], (near, z))
    f_sib = remote(own, panel(ext, 1 + 2 * k), f_send.at[2], f_recv.at[2], (sib, z))
    f_fwd = remote(
        panel(ext, 4 - 4 * k), panel(ext, 3 - 2 * k), f_send.at[3], f_recv.at[3], (sib, z)
    )
    from_dn = [
        remote(some(0, h), some(0, h), f_send.at[4 * h], f_recv.at[4 * h], (r - 2, z))
        for h in range(2)
    ]
    from_up = [
        remote(some(4, h), some(4, h), f_send.at[4 * h + 1], f_recv.at[4 * h + 1], (r + 2, z))
        for h in range(2)
    ]
    from_sib = remote(own, panel(ext, 3 - 2 * k), f_send.at[2], f_recv.at[2], (sib, z))
    from_fwd = remote(own, panel(ext, 1 + 2 * k), f_send.at[3], f_recv.at[3], (sib, z))
    fwd_out = jnp.where(k == 0, r + 2 < n_row, r >= 2)
    fwd_in = jnp.where(k == 0, r >= 2, r + 2 < n_row)

    starts = (
        (turning, f_out), (has_up, f_up), (has_dn, f_dn), (straight_up, f_up2), (straight_dn, f_dn2)
    )
    for ok, copy in starts:
        pl.when(ok)(copy.start)
    f_sib.start()

    eighth = feat // 8

    def span(ref, start, count):
        return ref.at[pl.ds(pl.multiple_of(start * eighth, eighth), count * eighth)]

    def rounds(raw, full, base, bit_a, dev_a, bit_b, dev_b):
        mine = 4 * k + 2 * bit_b + bit_a
        plan = (
            (raw, mine, mine, 1, (r, mate)),
            (full, mine, mine + 1 - 2 * bit_a, 1, (dev_a, z)),
            (full, 4 * k + 2 * bit_b, 4 * k + 2 - 2 * bit_b, 2, (dev_b, z)),
            (full, 4 * k, 4 - 4 * k, 4, (sib, z)),
        )
        sent, got = [], []
        for i, (src, lo, there, count, dev) in enumerate(plan):
            sems = (w_send.at[base + i], w_recv.at[base + i])
            sent.append(remote(span(src, lo, count), span(full, lo, count), *sems, dev))
            got.append(remote(span(full, there, count), span(full, there, count), *sems, dev))
        return sent, got

    in_sent, in_got = rounds(w_in_ref, w2_in, 0, bit2, near, bit4, far)
    out_sent, out_got = rounds(w_out_ref, w2_out, 4, bit4, far, bit2, near)

    def exchange(src, dst, kind, c, count=1):
        return [
            remote(
                half_part(src, lax.rem(zp, 2), c, count),
                dst.at[z, pl.ds(c * part, count * part)],
                a_send.at[kind, i], a_recv.at[kind, i], (r, zp),
            )
            for i, zp in enumerate(peers)
        ]

    def arrivals(buf, kind, c, count=1):
        views = [buf.at[zf, pl.ds(c * part, count * part)] for zf in peers]
        return [
            remote(v, v, a_send.at[kind, i], a_recv.at[kind, i], (r, zf))
            for i, (v, zf) in enumerate(zip(views, peers))
        ]

    in_sent[0].start()
    out_sent[0].start()
    cot_out = exchange(cot_ref, cot_full, 0, 0, PARTS)
    outer = z1 == z2
    for copy in cot_out[:2]:
        pl.when(jnp.logical_not(outer))(copy.start)

    @pl.when(jnp.logical_not(has_dn))
    def _():
        ext[0:row_blocks] = jnp.zeros((row_blocks, 128, quarter), BF16)

    @pl.when(jnp.logical_not(has_up))
    def _():
        ext[4 * row_blocks : 5 * row_blocks] = jnp.zeros((row_blocks, 128, quarter), BF16)

    @pl.when(r < 1)
    def _():
        ext[row_blocks : 2 * row_blocks] = jnp.zeros((row_blocks, 128, quarter), BF16)

    @pl.when(r + 1 >= n_row)
    def _():
        ext[3 * row_blocks : 4 * row_blocks] = jnp.zeros((row_blocks, 128, quarter), BF16)

    for copy in loads:
        copy.wait()

    def transpose_block(b, carry):
        for s in range(slots):
            vals_t[b, s] = vals[b, s].astype(F32).T.astype(BF16)
        return carry

    lax.fori_loop(0, row_blocks, transpose_block, 0)

    for b in range(row_blocks):
        for s in range(slots):
            col = jnp.broadcast_to(spread_ref[s : s + 1, b : b + 1], (16, 128))
            marks[b * slots + s] = jnp.where(col >= 0, col - first, -1)

    def fill_dense(t, carry):
        at = pl.ds(pl.multiple_of(t * 128, 128), 128)
        for b in range(row_blocks):
            turned = jnp.zeros((8, 16, 128), BF16)
            for s in range(slots):
                keep = jnp.where(marks[b * slots + s] == t, 1.0, 0.0).astype(BF16)[None]
                turned = turned + vals_t[b, s].reshape(8, 16, 128) * keep
            dense_t[at, b * 128 : (b + 1) * 128] = turned.reshape(128, 128)
        return carry

    @pl.when(passing)
    def _():
        f_out.wait_recv()
        f_on.start()

    in_sent[0].wait_send()
    out_sent[0].wait_send()
    for copy in cot_out[:2]:
        pl.when(outer)(copy.start)
    cot_out[2].start()
    out_got[0].wait_recv()
    out_sent[1].start()
    in_got[0].wait_recv()

    @pl.when(has_dn)
    def _():
        for copy in from_dn:
            copy.wait_recv()

    @pl.when(has_up)
    def _():
        for copy in from_up:
            copy.wait_recv()

    @pl.when(fwd_out)
    def _():
        f_fwd.start()

    from_sib.wait_recv()

    @pl.when(fwd_in)
    def _():
        from_fwd.wait_recv()

    def gather(b):
        left, right = [], []
        for s in range(slots):
            col = cols_ref[s, b]
            absent = lax.shift_right_logical(col, 31)
            place = col - first + absent * (1 + first + 2 * row_blocks + b)
            keep = jnp.where(marks[b * slots + s] >= 0, 1.0, 0.0).astype(BF16)[None]
            left.append((vals[b, s].reshape(8, 16, 128) * keep).reshape(128, 128))
            right.append(ext[jnp.minimum(jnp.maximum(place, 0), 5 * row_blocks - 1)])
        res = dot(jnp.concatenate(left, axis=1), jnp.concatenate(right, axis=0))
        agg[b * 128 : (b + 1) * 128, :] = res.astype(BF16)

    agg_out = []
    per_part = part // 128
    for c in range(PARTS):
        for s in range(2):
            for i in range(per_part):
                gather((s * PARTS + c) * per_part + i)
        agg_out.append(exchange(agg, agg_full, 1 + c, c))
        for copy in agg_out[c]:
            copy.start()
    for c in range(PARTS):
        agg_full[z, pl.ds(c * part, part)] = agg[
            pl.ds(pl.multiple_of(z1 * half + c * part, part), part), :
        ]

    in_sent[1].start()
    out_got[1].wait_recv()
    out_sent[2].start()
    cut = 2 * row_blocks
    lax.fori_loop(0, cut, fill_dense, 0)
    in_got[1].wait_recv()
    in_sent[2].start()
    lax.fori_loop(cut, 5 * row_blocks, fill_dense, 0)
    tile = 1024

    def grad_part(w_b, base):
        def step(i, carry):
            hc = pl.ds(pl.multiple_of(i * tile, tile), tile)
            to = pl.ds(pl.multiple_of(base + i * tile, tile), tile)
            for c in range(PARTS):
                rs = pl.ds(c * part, part)
                g = jnp.concatenate([cot_full[q, rs] for q in range(n_rep)], axis=1)
                gh[rs, to] = dot(g, w_b[:, hc])
            return carry

        lax.fori_loop(0, hidw // tile, step, 0)

    def hidden_part(w_a, base, c):
        rs = pl.ds(c * part, part)

        def step(i, carry):
            hc = pl.ds(pl.multiple_of(i * tile, tile), tile)
            to = pl.ds(pl.multiple_of(base + i * tile, tile), tile)
            x = jnp.concatenate([agg_full[q, rs] for q in range(n_rep)], axis=1)
            value, slope = gelu_pair(dot(x, w_a[:, hc]))
            hid[rs, to] = value.astype(BF16)
            gp[rs, to] = (gh[rs, to] * slope).astype(BF16)
            return carry

        lax.fori_loop(0, hidw // tile, step, 0)

    def product(src, w_a, w_b, zq, c):
        at = pl.ds(pl.multiple_of(zq * quarter, quarter), quarter)
        rs = pl.ds(c * part, part)
        res = dot(src[rs, :hidw], w_a[at, :], ((1,), (1,)))
        res = res + dot(src[rs, hidw:], w_b[at, :], ((1,), (1,)))
        return res.astype(BF16)

    def adj_copies(f, c):
        kind = 1 + PARTS + f * PARTS + c
        rs = pl.ds(c * part, part)
        return [
            remote(
                adj_p.at[zp, f, rs], adj_in.at[z, f, rs],
                a_send.at[kind, i], a_recv.at[kind, i], (r, zp),
            )
            for i, zp in enumerate(peers)
        ]

    def adj_arrivals(f, c):
        kind = 1 + PARTS + f * PARTS + c
        views = [adj_in.at[zf, f, pl.ds(c * part, part)] for zf in peers]
        return [
            remote(v, v, a_send.at[kind, i], a_recv.at[kind, i], (r, zf))
            for i, (v, zf) in enumerate(zip(views, peers))
        ]

    for copy in arrivals(cot_full, 0, 0, PARTS):
        copy.wait_recv()
    grad_part(w1_out, 0)
    out_got[2].wait_recv()
    out_sent[3].start()
    in_got[2].wait_recv()
    in_sent[3].start()
    out_got[3].wait_recv()
    grad_part(w2_out, hidw)
    in_got[3].wait_recv()
    adj_sent = [[adj_copies(f, c) for c in range(PARTS)] for f in range(WIDE)]
    for c in range(PARTS):
        for copy in arrivals(agg_full, 1 + c, c):
            copy.wait_recv()
        hidden_part(w1_in, 0, c)
        hidden_part(w2_in, hidw, c)
        rs = pl.ds(c * part, part)
        for i, zp in enumerate(peers + [z]):
            res = product(gp, w1_in, w2_in, zp, c)
            made = adj_p if i < n_rep - 1 else adj_in
            for f in range(WIDE):
                made[zp, f, rs] = res[:, f * width : (f + 1) * width]
            if i < n_rep - 1:
                adj_sent[0][c][i].start()

    out_sends = []
    for c in range(PARTS):
        rs = pl.ds(c * part, part)
        kind = 1 + (1 + WIDE) * PARTS + c
        for i, zp in enumerate(peers):
            out_p[zp, rs] = product(hid, w1_out, w2_out, zp, c)
            out_sends.append(
                remote(
                    out_p.at[zp, rs], out_in.at[z, rs],
                    a_send.at[kind, i], a_recv.at[kind, i], (r, zp),
                )
            )
        out_in[z, rs] = product(hid, w1_out, w2_out, z, c)

    tile = 256
    plain_to, helped_to = r - 2 + 4 * k, r + 2 - 4 * k
    plain_ok, helped_ok = fwd_in, fwd_out
    turn_plain = jnp.logical_and(turning, k == bit2)
    turn_helped = jnp.logical_and(turning, k != bit2)
    p5_sent = []

    def turn(f):
        for c in range(PARTS):
            for copy in adj_arrivals(f, c):
                copy.wait_recv()
        for s in range(2):
            total = adj_in[s, f].astype(F32)
            for q in range(s + 2, n_rep, 2):
                total = total + adj_in[q, f].astype(F32)
            adj[f, s * half : (s + 1) * half] = total.astype(BF16)

        def put(p, slot):
            def step(m, carry):
                at = pl.ds(pl.multiple_of(m * tile, tile), tile)
                c_send[4 * f + slot, at, :] = piece(f, p, m).astype(BF16)
                return carry

            lax.fori_loop(0, rows // tile, step, 0)

        def cross(slot, dst, got, dev):
            return remote(
                c_send.at[4 * f + slot], dst, c_sends.at[4 * f + slot], c_recvs.at[4 * f + got], dev
            )

        c_help = cross(0, c_sib.at[2 * f], 0, (sib, z))
        c_own = cross(1, c_sib.at[2 * f + 1], 1, (sib, z))
        top, low = pl.ds(0, rows // 2), pl.ds(rows // 2, rows // 2)

        def sides(slot, nbr, dev):
            return (
                remote(
                    c_send.at[4 * f + slot, top], c_nbr.at[2 * f + nbr, top],
                    c_sends.at[4 * f + slot], c_recvs.at[4 * f + 2 + nbr], dev,
                ),
                remote(
                    c_send.at[4 * f + slot, low], c_nbr.at[2 * f + nbr, low],
                    b_sends.at[4 * f + slot], b_recvs.at[4 * f + 2 + nbr], dev,
                ),
            )

        c_plain = sides(2, 1 - k, (plain_to, z))
        c_helped = sides(3, k, (helped_to, z))
        c_out = remote(
            c_send.at[4 * f + jnp.where(k == bit2, 2, 3), low], c_relay.at[f],
            b_sends.at[4 * f], b_recvs.at[4 * f], (far, z),
        )
        c_on = remote(
            c_relay.at[f], c_nbr.at[2 * f + 1 - bit2, low],
            b_sends.at[4 * f + 1], b_recvs.at[4 * f + 3 - bit2], (near, z),
        )
        moves = (
            (plain_ok, c_plain[0]), (jnp.logical_and(plain_ok, jnp.logical_not(turn_plain)), c_plain[1]),
            (helped_ok, c_helped[0]),
            (jnp.logical_and(helped_ok, jnp.logical_not(turn_helped)), c_helped[1]),
            (turning, c_out), (passing, c_on),
        )
        put(4 * k, 2)
        pl.when(turn_plain)(c_out.start)
        for ok, copy in moves[:2]:
            pl.when(ok)(copy.start)
        put(1 + 2 * k, 0)
        c_help.start()
        c_help.wait_recv()

        def add_help(m, carry):
            at = pl.ds(pl.multiple_of(m * tile, tile), tile)
            total = piece(f, 4 - 4 * k, m) + c_sib[2 * f, at, :].astype(F32)
            c_send[4 * f + 3, at, :] = total.astype(BF16)
            return carry

        lax.fori_loop(0, rows // tile, add_help, 0)

        pl.when(turn_helped)(c_out.start)
        for ok, copy in moves[2:4]:
            pl.when(ok)(copy.start)
        @pl.when(passing)
        def _():
            c_out.wait_recv()
            c_on.start()

        put(3 - 2 * k, 1)
        c_own.start()

        p5_sent.append((c_help, c_own, moves))

    def piece(f, p, m):
        at = pl.ds(pl.multiple_of(p * rows + m * tile, tile), tile)
        return dot(dense_t[at, :], adj[f])

    def finish(f):
        p5_sent[f][1].wait_recv()

        def landed(nbr, dev):
            for h, sems in enumerate((c_recvs, b_recvs)):
                ref = c_nbr.at[2 * f + nbr, pl.ds(h * (rows // 2), rows // 2)]
                remote(ref, ref, c_sends.at[4 * f + 2], sems.at[4 * f + 2 + nbr], (dev, z)).wait_recv()

        @pl.when(has_dn)
        def _():
            landed(0, r - 2)

        @pl.when(jnp.logical_not(has_dn))
        def _():
            c_nbr[2 * f] = jnp.zeros((rows, width), BF16)

        @pl.when(has_up)
        def _():
            landed(1, r + 2)

        @pl.when(jnp.logical_not(has_up))
        def _():
            c_nbr[2 * f + 1] = jnp.zeros((rows, width), BF16)

        cs = slice(f * width, (f + 1) * width)

        def step(m, carry):
            at = pl.ds(pl.multiple_of(m * tile, tile), tile)
            total = piece(f, 2, m) + c_sib[2 * f + 1, at, :].astype(F32)
            total = total + c_nbr[2 * f, at, :].astype(F32) + c_nbr[2 * f + 1, at, :].astype(F32)
            grad_ref[at, cs] = (cot[at, cs].astype(F32) + total).astype(BF16)
            return carry

        lax.fori_loop(0, rows // tile, step, 0)

    for f in range(WIDE):
        for copies in adj_sent[f]:
            for copy in copies:
                copy.wait_send()
        following = sum(adj_sent[f + 1], []) if f + 1 < WIDE else out_sends
        for copy in following:
            copy.start()
        turn(f)
    for f in range(WIDE):
        finish(f)
    for c in range(PARTS):
        for copy in arrivals(out_in, 1 + (1 + WIDE) * PARTS + c, c):
            copy.wait_recv()
        rs = pl.ds(c * part, part)
        for s in range(2):
            total = out_in[s, rs].astype(F32)
            for q in range(s + 2, n_rep, 2):
                total = total + out_in[q, rs].astype(F32)
            start, count = 2 * row_blocks + s * row_blocks // 2 + c * per_part, per_part
            mine = ext[start : start + count].reshape(part, quarter)
            at = pl.ds(s * half + c * part, part)
            upd_ref[at] = (mine.astype(F32) + total).astype(BF16)

    for copy in cot_out + in_sent[1:] + out_sent[1:] + agg_out[0] + agg_out[1] + out_sends + [f_sib]:
        copy.wait_send()
    late = list(starts) + [(fwd_out, f_fwd), (passing, f_on)]
    for c_help, c_own, moves in p5_sent:
        c_help.wait_send()
        c_own.wait_send()
        late += list(moves)
    for ok, copy in late:
        pl.when(ok)(copy.wait_send)


def settle(upd_ref, grad_ref, upd_out, grad_out, sems):
    size = upd_ref.shape[0] // CUTS
    copies = [
        pltpu.make_async_copy(
            src.at[pl.ds(i * size, size)], dst.at[pl.ds(i * size, size)], sems.at[j, i]
        )
        for j, (src, dst) in enumerate(((upd_ref, upd_out), (grad_ref, grad_out)))
        for i in range(CUTS)
    ]
    for copy in copies:
        copy.start()
    for copy in copies:
        copy.wait()


def body(n_row, n_rep, node_feats, block_cols, block_vals, w_in, w_out, cotangent):
    rows, quarter = cotangent.shape
    row_blocks, slots = block_cols.shape
    feat, hidw = w_in.shape
    half = rows // 2
    kinds = 1 + (2 + WIDE) * PARTS
    width = quarter // WIDE
    vmem = pl.BlockSpec(memory_space=pltpu.VMEM)
    anywhere = pl.BlockSpec(memory_space=pl.ANY)
    dma = pltpu.SemaphoreType.DMA
    made = pl.pallas_call(
        functools.partial(kernel, n_row, n_rep),
        out_shape=(pltpu.VMEM((rows, quarter), BF16),) * 2,
        in_specs=[anywhere] * 6,
        out_specs=(vmem, vmem),
        scratch_shapes=[
            pltpu.SMEM((slots, row_blocks), jnp.int32),
            pltpu.VMEM((slots, row_blocks), jnp.int32),
            pltpu.VMEM((5 * row_blocks, 128, quarter), BF16),
            pltpu.VMEM((row_blocks * slots, 16, 128), jnp.int32),
            pltpu.VMEM((row_blocks, slots, 128, 128), BF16),
            pltpu.VMEM((row_blocks, slots, 128, 128), BF16),
            pltpu.VMEM((5 * rows, rows), BF16),
            pltpu.VMEM((feat, hidw), BF16),
            pltpu.VMEM((feat, hidw), BF16),
            pltpu.VMEM((feat, hidw), BF16),
            pltpu.VMEM((feat, hidw), BF16),
            pltpu.VMEM((rows, quarter), BF16),
            pltpu.VMEM((n_rep, half, quarter), BF16),
            pltpu.VMEM((rows, quarter), BF16),
            pltpu.VMEM((n_rep, half, quarter), BF16),
            pltpu.VMEM((half, 2 * hidw), BF16),
            pltpu.VMEM((half, 2 * hidw), BF16),
            pltpu.VMEM((half, 2 * hidw), F32),
            pltpu.VMEM((n_rep, WIDE, half, width), BF16),
            pltpu.VMEM((n_rep, half, quarter), BF16),
            pltpu.VMEM((n_rep, WIDE, half, width), BF16),
            pltpu.VMEM((n_rep, half, quarter), BF16),
            pltpu.VMEM((WIDE, rows, width), BF16),
            pltpu.VMEM((4 * WIDE, rows, width), BF16),
            pltpu.VMEM((2 * WIDE, rows, width), BF16),
            pltpu.VMEM((2 * WIDE, rows, width), BF16),
            pltpu.VMEM((row_blocks // 2, 128, quarter), BF16),
            pltpu.VMEM((WIDE, rows // 2, width), BF16),
            dma((8,)),
            dma((8,)),
            dma((8,)),
            dma((8,)),
            dma((8,)),
            dma((kinds, n_rep - 1)),
            dma((kinds, n_rep - 1)),
            dma((4 * WIDE,)),
            dma((4 * WIDE,)),
            dma((4 * WIDE,)),
            dma((4 * WIDE,)),
        ],
        compiler_params=pltpu.CompilerParams(
            collective_id=0, has_side_effects=True, vmem_limit_bytes=56 * 1024 * 1024
        ),
    )(block_cols.T, node_feats.reshape(row_blocks, 128, feat), block_vals, w_in, w_out, cotangent)
    return pl.pallas_call(
        settle,
        out_shape=(jax.ShapeDtypeStruct((rows, quarter), BF16),) * 2,
        in_specs=[vmem] * 2,
        out_specs=(anywhere,) * 2,
        scratch_shapes=[dma((2, CUTS))],
    )(*(pltpu.with_memory_space_constraint(m, pltpu.VMEM) for m in made))


def solution(mesh):
    in_specs = (
        P("row", None),
        P("row", None),
        P("row", None, None, None),
        P(None, "rep"),
        P(None, "rep"),
        P("row", "rep"),
    )
    out_specs = (P("row", "rep"), P("row", "rep"))
    run = functools.partial(body, mesh.shape["row"], mesh.shape["rep"])
    return jax.shard_map(run, mesh=mesh, in_specs=in_specs, out_specs=out_specs, check_vma=False)
```
